32 devices in a mesh: dp: 2 (over y), pb: 4 (over z), ka: 4 (over x, core).
Axes of the slice: x: 2, y: 2, z: 4, core: 2. Of those that a mesh axis runs over, the one named last changes fastest.
Arguments:
- inputs: bfloat16 [4, 2048, 2048], P('dp', ('pb', 'ka')), may hold values from -6 to 6
- out_cotangent: bfloat16 [4, 2048, 2048], P('dp', ('pb', 'ka')), may hold values from -6 to 6
- doc_lengths: int32 [4, 4], P('dp'), may hold values from 0 to 2048, as said below
- ln1_gain: float32 [2048], P(('dp', 'pb', 'ka')), may hold values from 0.5 to 1.5
- w_query: float32 [2048, 2048], P(('dp', 'pb', 'ka'))
- w_key: float32 [2048, 2048], P(('dp', 'pb', 'ka'))
- w_value: float32 [2048, 4096], P(('dp', 'pb', 'ka')), may hold values from -0.125 to 0.125
- w_gate: float32 [2048, 4096], P(('dp', 'pb', 'ka')), may hold values from -0.125 to 0.125
- w_out: float32 [4096, 2048], P(('dp', 'pb', 'ka')), may hold values from -0.09375 to 0.09375
- ln2_gain: float32 [2048], P(('dp', 'pb', 'ka')), may hold values from 0.5 to 1.5
- w_up: float32 [2048, 4096], P(('dp', 'pb', 'ka')), may hold values from -0.125 to 0.125
- up_bias: float32 [4096], P(('dp', 'pb', 'ka')), may hold values from -3 to 3
- w_down: float32 [4096, 2048], P(('dp', 'pb', 'ka')), may hold values from -0.09375 to 0.09375
Outputs:
- output: bfloat16 [4, 2048, 2048], P('dp', ('pb', 'ka'))
- grad_inputs: float32 [4, 2048, 2048], P('dp', ('pb', 'ka'))
- grad_ln1_gain: float32 [2048], P(('dp', 'pb', 'ka'))
- grad_w_query: float32 [2048, 2048], P(('dp', 'pb', 'ka'))
- grad_w_key: float32 [2048, 2048], P(('dp', 'pb', 'ka'))
- grad_w_value: float32 [2048, 4096], P(('dp', 'pb', 'ka'))
- grad_w_gate: float32 [2048, 4096], P(('dp', 'pb', 'ka'))
- grad_w_out: float32 [4096, 2048], P(('dp', 'pb', 'ka'))
- grad_ln2_gain: float32 [2048], P(('dp', 'pb', 'ka'))
- grad_w_up: float32 [2048, 4096], P(('dp', 'pb', 'ka'))
- grad_up_bias: float32 [4096], P(('dp', 'pb', 'ka'))
- grad_w_down: float32 [4096, 2048], P(('dp', 'pb', 'ka'))
The draws below stay inside these ranges and needn't reach their ends.
Inputs may be any that keep to these rules, and one draw needn't show every extreme that they name: `doc_lengths`: each row packs its 2048 positions with documents of 512, 1024 or 2048 positions that sum to 2048, followed by zeros; in each aligned block of 2 rows exactly one row holds one document of 2048 positions, and every other row holds two or more documents.
All inputs are finite; a program needn't handle non-finite values.
Results may differ from the reference program's by a relative error of at most 0.017.
Values may be sent and summed in bfloat16 or wider, within the bound.
A program may use at most 448 MiB of HBM per device.

```python
import jax
import jax.numpy as jnp
from jax import lax

D = 2048
H = 8
DK = 256
DV = 512
FF = 4096
LEN = 2048
XPOS_BASE = 512
BATCH_DP = 2
VD = 4096
BATCH = 4


def shared_projection(key):
    return jax.random.normal(key, (D, H * DK), dtype=jnp.float32) * D ** (-0.5)


def draw_w_query(key, part):
    return shared_projection(key)


def draw_w_key(key, part):
    common = shared_projection(key)
    key = jax.random.fold_in(key, 5)
    own_part = jax.random.normal(key, (D, H * DK), dtype=jnp.float32) * D ** (-0.5)
    return 0.8 * common + 0.6 * own_part


def draw_doc_lengths(key, part):
    key = jax.random.fold_in(key, 11)
    patterns = jnp.array([[4, 0, 0, 0], [2, 2, 0, 0], [2, 1, 1, 0], [1, 2, 1, 0], [1, 1, 2, 0], [1, 1, 1, 1]], dtype=jnp.int32)
    picked = jax.random.randint(jax.random.fold_in(key, 1), (BATCH,), 1, 6)
    whole_rows = jax.random.randint(jax.random.fold_in(key, 2), (BATCH // BATCH_DP,), 0, BATCH_DP)
    row_index = jnp.arange(BATCH, dtype=jnp.int32)
    block_index = row_index // BATCH_DP
    block_pick = (block_index[:, None] == jnp.arange(BATCH // BATCH_DP, dtype=jnp.int32)[None, :]).astype(jnp.int32)
    chosen = jnp.sum(block_pick * whole_rows[None, :], axis=1)
    picked = jnp.where(row_index % BATCH_DP == chosen, 0, picked)
    one_hot = (picked[:, None] == jnp.arange(6, dtype=jnp.int32)[None, :]).astype(jnp.int32)
    quarters = jnp.sum(one_hot[:, :, None] * patterns[None, :, :], axis=1)
    return quarters * (LEN // 4)


def shard_levels(stream_key, extent, cuts, low, largest):
    factor_of, own = 1.0, jax.random.fold_in(stream_key, 6)
    for axis_at, parts in cuts:
        draws = jnp.exp(jax.random.uniform(jax.random.fold_in(own, axis_at), (parts,), jnp.float32, low / len(cuts), largest / len(cuts)))
        factor_of = factor_of * jnp.repeat(draws, extent[axis_at] // parts).reshape([-1 if axis == axis_at else 1 for axis in range(len(extent))])
    return factor_of


def normal_values(stream_key, dims, scale, most, split=(), kind=jnp.bfloat16):
    values = jax.random.normal(stream_key, dims, jnp.float32) * scale
    if len(split) > 0:
        values = shard_levels(stream_key, dims, split, -0.22, 0.18) * values
    return jnp.clip(values, min=-most, max=most).astype(kind)


def setup_inputs(seed: int = 0) -> dict:
    arg_keys = jax.random.split(jax.random.key(seed), 14)
    return {
        "inputs": normal_values(arg_keys[0], (BATCH, LEN, D), 1.0, 6.0, ((0, 2), (1, 16))),
        "out_cotangent": normal_values(arg_keys[1], (BATCH, LEN, D), 1.0, 6.0, ((0, 2), (1, 16))),
        "doc_lengths": draw_doc_lengths(jax.random.fold_in(arg_keys[13], 71), 0),
        "ln1_gain": jnp.clip(1.0 + 0.1 * jax.random.normal(arg_keys[3], (D,), jnp.float32), 0.5, 1.5),
        "w_query": draw_w_query(jax.random.fold_in(arg_keys[13], 71), 0),
        "w_key": draw_w_key(jax.random.fold_in(arg_keys[13], 71), 0),
        "w_value": normal_values(arg_keys[6], (D, VD), D ** -0.5, 0.125, ((0, 32),), jnp.float32),
        "w_gate": normal_values(arg_keys[7], (D, VD), D ** -0.5, 0.125, ((0, 32),), jnp.float32),
        "w_out": normal_values(arg_keys[8], (VD, D), VD ** -0.5, 0.09375, ((0, 32),), jnp.float32),
        "ln2_gain": jnp.clip(1.0 + 0.1 * jax.random.normal(arg_keys[9], (D,), jnp.float32), 0.5, 1.5),
        "w_up": normal_values(arg_keys[10], (D, FF), D ** -0.5, 0.125, ((0, 32),), jnp.float32),
        "up_bias": normal_values(arg_keys[11], (FF,), 0.5, 3.0, ((0, 32),), jnp.float32),
        "w_down": normal_values(arg_keys[12], (FF, D), FF ** -0.5, 0.09375, ((0, 32),), jnp.float32),
    }


@jax.custom_vjp
def low(v):
    return lax.optimization_barrier(v.astype(jnp.bfloat16)).astype(jnp.float32)

@jax.custom_vjp
def low_back(v):
    return v

def low_keep(v):
    return (low(v), None)

def low_pass(kept, grad):
    return (grad,)

def back_keep(v):
    return (v, None)

def back_low(kept, grad):
    return (low(grad),)
low.defvjp(low_keep, low_pass)
low_back.defvjp(back_keep, back_low)
epsilon = 1e-05

def product(left, right):
    return jnp.dot(left, right, precision=lax.Precision.HIGHEST, preferred_element_type=jnp.float32)

def layer_norm(values, gain_vec):
    row_mean = lax.optimization_barrier(jnp.mean(values, axis=-1, keepdims=True))
    centered = values - row_mean
    inv_scale = lax.rsqrt(lax.optimization_barrier(jnp.mean(centered * centered, axis=-1, keepdims=True)) + epsilon)
    return centered * inv_scale * gain_vec

def group_norm(values, head_count):
    shaped = values.reshape(values.shape[:-1] + (head_count, values.shape[-1] // head_count))
    row_mean = lax.optimization_barrier(jnp.mean(shaped, axis=-1, keepdims=True))
    centered = shaped - row_mean
    inv_scale = lax.rsqrt(lax.optimization_barrier(jnp.mean(centered * centered, axis=-1, keepdims=True)) + epsilon)
    return (centered * inv_scale).reshape(values.shape)

def xpos_turn(values, positions, head_count, scale_base, direction):
    head_size = values.shape[-1] // head_count
    half_size = head_size // 2
    pair_index = jnp.arange(half_size, dtype=jnp.float32)
    frequency = jnp.exp(-jnp.log(10000.0) * pair_index / half_size)
    xpos_zeta = (pair_index / half_size + 0.4) / 1.4
    angles = positions[:, None] * frequency[None, :]
    factor = jnp.exp(direction * positions[:, None] / scale_base * jnp.log(xpos_zeta)[None, :])
    cosine = (jnp.cos(angles) * factor)[:, None, :]
    sine_part = (jnp.sin(angles) * factor)[:, None, :]
    shaped = values.reshape(values.shape[:-1] + (head_count, head_size))
    first_half = shaped[..., :half_size]
    second = shaped[..., half_size:]
    turned = jnp.concatenate([first_half * cosine - second * sine_part, second * cosine + first_half * sine_part], axis=-1)
    return turned.reshape(values.shape)

def doc_starts(lengths, positions):
    doc_ends = jnp.cumsum(lengths, axis=-1).astype(jnp.int32)
    before = (doc_ends[:, None, :] <= positions[None, :, None]).astype(jnp.int32)
    return lax.optimization_barrier(jnp.sum(before * lengths[:, None, :], axis=-1)).astype(jnp.int32)

def decay_mask(query_pos, key_pos, starts, head_count):
    distance = query_pos[:, None] - key_pos[None, :]
    allowed = (distance >= 0)[None, :, :] & (key_pos[None, None, :] >= starts[:, :, None])
    head_index = jnp.arange(head_count, dtype=jnp.float32)
    log_gamma = jnp.log(1.0 - jnp.exp2(-5.0 - head_index))
    decay_rate = jnp.exp(jnp.maximum(distance, 0).astype(jnp.float32)[None, :, :] * log_gamma[:, None, None])
    return jnp.where(allowed[:, None, :, :], decay_rate[None, :, :, :], jnp.float32(0.0))

def forward_row(row_input, lengths, parameters):
    gain_one, weight_query, weight_key, weight_value, weight_gate, weight_out, gain_two, weight_up, bias_up, weight_down = [low(member) for member in parameters]
    positions = jnp.arange(LEN, dtype=jnp.int32)
    places = positions.astype(jnp.float32)
    normed_one = low(layer_norm(row_input, gain_one))
    query_pre = low_back(product(normed_one, weight_query))
    key_pre = low_back(product(normed_one, weight_key))
    value_pre = low_back(product(normed_one, weight_value))
    gate_pre = low_back(product(normed_one, weight_gate))
    query_rot = low(xpos_turn(query_pre, places, H, XPOS_BASE, 1.0) * DK ** (-0.5))
    key_rot = low(xpos_turn(key_pre, places, H, XPOS_BASE, -1.0))
    value_low = low(value_pre)
    starts = doc_starts(lengths[None, :], positions)
    decay = decay_mask(positions, positions, starts, H)[0]
    query_heads = query_rot.reshape(LEN, H, DK)
    key_heads = key_rot.reshape(LEN, H, DK)
    value_heads = value_low.reshape(LEN, H, DV)
    raw_scores = low_back(jnp.einsum('qhd,khd->hqk', query_heads, key_heads, precision=lax.Precision.HIGHEST))
    scores = low(raw_scores * decay)
    retained = low_back(jnp.einsum('hqk,khe->qhe', scores, value_heads, precision=lax.Precision.HIGHEST).reshape(LEN, H * DV))
    gated = low(jax.nn.silu(gate_pre) * group_norm(retained, H))
    attended = low_back(product(gated, weight_out))
    middle = row_input + attended
    normed_two = low(layer_norm(middle, gain_two))
    up_pre = low_back(product(normed_two, weight_up) + bias_up)
    active = low(jax.nn.gelu(up_pre, approximate=False))
    return middle + product(active, weight_down)

def reference(inputs, out_cotangent, doc_lengths, ln1_gain, w_query, w_key, w_value, w_gate, w_out, ln2_gain, w_up, up_bias, w_down):
    parameters = (ln1_gain, w_query, w_key, w_value, w_gate, w_out, ln2_gain, w_up, up_bias, w_down)
    input_rows = inputs.astype(jnp.float32)
    cotangent = out_cotangent.astype(jnp.float32)

    def forward(rows_all, weights_all):
        row_step = jax.checkpoint(lambda row_pair: forward_row(row_pair[0], row_pair[1], weights_all))
        return lax.map(row_step, (rows_all, doc_lengths))
    output, backward = jax.vjp(forward, input_rows, parameters)
    grad_rows, grad_params = backward(cotangent)
    return (output.astype(jnp.bfloat16), grad_rows, grad_params[0], grad_params[1], grad_params[2], grad_params[3], grad_params[4], grad_params[5], grad_params[6], grad_params[7], grad_params[8], grad_params[9])
```

```python
import functools
import math

import jax
import jax.numpy as jnp
import numpy as np
from jax import lax
from jax.experimental import pallas as pl
from jax.experimental.pallas import tpu as pltpu
from jax.sharding import Mesh
from jax.sharding import PartitionSpec as P

H = 8
XPOS_BASE = 512.0
EPSILON = 1e-05
MESH = pl.DeviceIdType.MESH
F32 = jnp.float32
BF16 = jnp.bfloat16

PLANE = ("dpl", "ka")
LINE = ("dph", "pb")


def plane_ids():
    row = lax.axis_index("dpl")
    col = lax.axis_index("ka")
    other_row = 1 - row
    across = lax.rem(col + 2, 4)
    sibling = col + 1 - 2 * lax.rem(col, 2)
    return row, col, other_row, across, sibling


def greet(targets):
    barrier = pltpu.get_barrier_semaphore()
    for target in targets:
        pl.semaphore_signal(barrier, inc=1, device_id=target, device_id_type=MESH)
    pl.semaphore_wait(barrier, len(targets))


def gather_kernel(shard, full, local_sem, send_sem, recv_sem):
    batch, length, _ = shard.shape
    half = length // 2
    row, col, other_row, across, sibling = plane_ids()
    to_x = {"ka": across}
    to_y = {"dpl": other_row}
    to_s = {"ka": sibling}

    def slot(r, c, start=0, size=length):
        return full.at[pl.ds(r * batch, batch), pl.ds(c * length + start, size), :]

    sent = []

    def send(src, dst, index, target):
        copy = pltpu.make_async_remote_copy(
            src_ref=src,
            dst_ref=dst,
            send_sem=send_sem.at[index],
            recv_sem=recv_sem.at[index],
            device_id=target,
            device_id_type=MESH,
        )
        copy.start()
        sent.append(copy)
        return copy

    greet((to_x, to_y, to_s))
    mine = pltpu.make_async_copy(shard, slot(row, col), local_sem)
    from_x = send(shard, slot(row, col), 0, to_x)
    from_y = send(shard, slot(row, col), 1, to_y)
    own_s = send(shard, slot(row, col), 2, to_s)
    mine.start()

    def onward(r, c, start, size, index, target):
        return send(slot(r, c, start, size), slot(r, c, start, size), index, target)

    from_x.wait_recv()
    diag_y = onward(row, across, 0, half, 3, to_y)
    relay_x = onward(row, across, 0, length, 4, to_s)
    from_y.wait_recv()
    diag_x = onward(other_row, col, half, half, 5, to_x)
    relay_y = onward(other_row, col, 0, length, 6, to_s)
    diag_y.wait_recv()
    relay_a = onward(other_row, across, 0, half, 7, to_s)
    diag_x.wait_recv()
    relay_b = onward(other_row, across, half, half, 8, to_s)
    for copy in (own_s, relay_x, relay_y, relay_a, relay_b):
        copy.wait_recv()
    for copy in sent:
        copy.wait_send()
    mine.wait()


def plane_gather(shard, collective_id):
    batch, length, width = shard.shape
    return pl.pallas_call(
        gather_kernel,
        out_shape=jax.ShapeDtypeStruct((2 * batch, 4 * length, width), shard.dtype),
        in_specs=[pl.BlockSpec(memory_space=pl.ANY)],
        out_specs=pl.BlockSpec(memory_space=pl.ANY),
        scratch_shapes=[
            pltpu.SemaphoreType.DMA,
            pltpu.SemaphoreType.DMA((9,)),
            pltpu.SemaphoreType.DMA((9,)),
        ],
        compiler_params=pltpu.CompilerParams(
            collective_id=collective_id, has_side_effects=True
        ),
        name="plane_gather",
    )(shard)


def scatter_kernel(
    part, total, own, sib, from_x, from_y, diag_a, diag_b, load_sem, send_sem, recv_sem
):
    batch, length, width = total.shape
    half = length // 2
    row, col, other_row, across, sibling = plane_ids()
    across_s = lax.rem(sibling + 2, 4)
    to_x = {"ka": across}
    to_y = {"dpl": other_row}
    to_s = {"ka": sibling}
    mine = ((other_row, across), (row, across), (other_row, col), (row, col))
    theirs = ((other_row, across_s), (row, across_s), (other_row, sibling), (row, sibling))

    def piece(r, c):
        return part.at[pl.ds(r * batch, batch), pl.ds(c * length, length), :]

    def send(src, dst, index, target):
        copy = pltpu.make_async_remote_copy(
            src_ref=src,
            dst_ref=dst,
            send_sem=send_sem.at[index],
            recv_sem=recv_sem.at[index],
            device_id=target,
            device_id_type=MESH,
        )
        copy.start()
        return copy

    loads = []
    for j in range(4):
        copy = pltpu.make_async_copy(piece(*mine[j]), own.at[j], load_sem.at[j])
        copy.start()
        loads.append(copy)
    greet((to_x, to_y, to_s))
    swaps = [send(piece(*theirs[j]), sib.at[j], j, to_s) for j in range(4)]

    step = 16

    def add(out_ref, refs, start, size):
        def body(i, carry):
            rows = pl.ds(start + i * step, step)
            value = refs[0][:, rows, :].astype(F32)
            for other in refs[1:]:
                value = value + other[:, rows, :].astype(F32)
            out_ref[:, rows, :] = value.astype(out_ref.dtype)
            return carry

        lax.fori_loop(0, size // step, body, 0)

    def add_at(out_ref, out_start, first, first_start, size):
        def body(i, carry):
            rows = pl.ds(out_start + i * step, step)
            value = out_ref[:, rows, :].astype(F32) + first[
                :, pl.ds(first_start + i * step, step), :
            ].astype(F32)
            out_ref[:, rows, :] = value.astype(out_ref.dtype)
            return carry

        lax.fori_loop(0, size // step, body, 0)

    lower, upper = pl.ds(0, half), pl.ds(half, half)

    def merge(j):
        loads[j].wait()
        swaps[j].wait_recv()
        add(own.at[j], (own.at[j], sib.at[j]), 0, length)

    merge(0)
    first_a = send(own.at[0, :, lower, :], diag_a, 4, to_x)
    first_b = send(own.at[0, :, upper, :], diag_b, 5, to_y)
    merge(1)
    x_lower = send(own.at[1, :, lower, :], from_x.at[:, lower, :], 6, to_x)
    merge(2)
    y_upper = send(own.at[2, :, upper, :], from_y.at[:, upper, :], 7, to_y)
    first_b.wait_recv()
    add_at(own.at[1], half, diag_b, 0, half)
    x_upper = send(own.at[1, :, upper, :], from_x.at[:, upper, :], 8, to_x)
    first_a.wait_recv()
    add_at(own.at[2], 0, diag_a, 0, half)
    y_lower = send(own.at[2, :, lower, :], from_y.at[:, lower, :], 9, to_y)
    merge(3)
    x_lower.wait_recv()
    y_lower.wait_recv()
    add(total, (own.at[3], from_x, from_y), 0, half)
    y_upper.wait_recv()
    x_upper.wait_recv()
    add(total, (own.at[3], from_x, from_y), half, half)
    for copy in swaps:
        copy.wait_send()
    for copy in (first_a, first_b, x_lower, x_upper, y_lower, y_upper):
        copy.wait_send()


def plane_scatter(part, collective_id):
    batch, length, width = part.shape[0] // 2, part.shape[1] // 4, part.shape[2]
    shape = (batch, length, width)
    return pl.pallas_call(
        scatter_kernel,
        out_shape=jax.ShapeDtypeStruct(shape, F32),
        in_specs=[pl.BlockSpec(memory_space=pl.ANY)],
        out_specs=pl.BlockSpec(memory_space=pltpu.VMEM),
        scratch_shapes=[
            pltpu.VMEM((4,) + shape, BF16),
            pltpu.VMEM((4,) + shape, BF16),
            pltpu.VMEM(shape, BF16),
            pltpu.VMEM(shape, BF16),
            pltpu.VMEM((batch, length // 2, width), BF16),
            pltpu.VMEM((batch, length // 2, width), BF16),
            pltpu.SemaphoreType.DMA((4,)),
            pltpu.SemaphoreType.DMA((10,)),
            pltpu.SemaphoreType.DMA((10,)),
        ],
        compiler_params=pltpu.CompilerParams(
            collective_id=collective_id,
            has_side_effects=True,
            vmem_limit_bytes=40 * 1024 * 1024,
        ),
        name="plane_scatter",
    )(part)


def scan_kernel(count, forward, state, coef, total, message, landed, send_sem, recv_sem):
    place = lax.axis_index("pb")
    if not forward:
        place = count - 1 - place
    rows = state.shape[0]
    has_prev = place > 0
    has_next = place < count - 1
    step = 1 if forward else -1
    here = lax.axis_index("pb")
    barrier = pltpu.get_barrier_semaphore()

    @pl.when(has_prev)
    def _():
        pl.semaphore_signal(barrier, inc=1, device_id={"pb": here - step}, device_id_type=MESH)

    @pl.when(has_next)
    def _():
        pl.semaphore_signal(barrier, inc=1, device_id={"pb": here + step}, device_id_type=MESH)

    pl.semaphore_wait(barrier, has_prev.astype(jnp.int32) + has_next.astype(jnp.int32))

    def hop(s):
        return pltpu.make_async_remote_copy(
            src_ref=message.at[s],
            dst_ref=landed.at[s],
            send_sem=send_sem.at[s],
            recv_sem=recv_sem.at[s],
            device_id={"pb": here + step},
            device_id_type=MESH,
        )

    for s in range(rows):

        @pl.when(has_prev)
        def _():
            hop(s).wait_recv()
            total[s] = (coef[0, s] * landed[s].astype(F32)).astype(BF16)

        @pl.when(jnp.logical_not(has_prev))
        def _():
            total[s] = jnp.zeros(total.shape[1:], BF16)

        @pl.when(has_next)
        def _():
            message[s] = (state[s] + coef[1, s] * total[s].astype(F32)).astype(BF16)
            hop(s).start()

    @pl.when(has_next)
    def _():
        for s in range(rows):
            hop(s).wait_send()


def line_scan(state, coef, count, forward, collective_id):
    return pl.pallas_call(
        functools.partial(scan_kernel, count, forward),
        out_shape=jax.ShapeDtypeStruct(state.shape, BF16),
        in_specs=[
            pl.BlockSpec(memory_space=pltpu.VMEM),
            pl.BlockSpec(memory_space=pltpu.SMEM),
        ],
        out_specs=pl.BlockSpec(memory_space=pltpu.VMEM),
        scratch_shapes=[
            pltpu.VMEM(state.shape, BF16),
            pltpu.VMEM(state.shape, BF16),
            pltpu.SemaphoreType.DMA((state.shape[0],)),
            pltpu.SemaphoreType.DMA((state.shape[0],)),
        ],
        compiler_params=pltpu.CompilerParams(
            collective_id=collective_id,
            has_side_effects=True,
            vmem_limit_bytes=24 * 1024 * 1024,
        ),
        name="line_scan",
    )(state, coef)


def normalize(values):
    mean = jnp.mean(values, axis=-1, keepdims=True)
    centered = values - mean
    inv = lax.rsqrt(jnp.mean(centered * centered, axis=-1, keepdims=True) + EPSILON)
    return centered * inv, inv


def normalize_back(normed, inv, grad):
    mean = jnp.mean(grad, axis=-1, keepdims=True)
    along = jnp.mean(grad * normed, axis=-1, keepdims=True)
    return inv * (grad - mean - normed * along)


def turn_tables(positions, half, direction):
    pair = jnp.arange(half, dtype=F32)
    frequency = jnp.exp(-jnp.log(10000.0) * pair / half)
    zeta = (pair / half + 0.4) / 1.4
    angles = positions[:, None] * frequency[None, :]
    factor = jnp.exp(direction * positions[:, None] / XPOS_BASE * jnp.log(zeta)[None, :])
    return jnp.cos(angles) * factor, jnp.sin(angles) * factor


def turn(values, tables):
    cosine, sine = tables
    half = values.shape[-1] // 2
    first, second = values[..., :half], values[..., half:]
    return jnp.concatenate(
        [first * cosine - second * sine, second * cosine + first * sine], axis=-1
    )


def turn_back(values, tables):
    cosine, sine = tables
    return turn(values, (cosine, -sine))


def mm(left, right):
    return jnp.einsum("sti,io->sto", left, right, preferred_element_type=F32)


def mm_back(left, right):
    return jnp.einsum("sto,io->sti", left, right, preferred_element_type=F32)


def mm_grad(left, right):
    return jnp.einsum("sti,sto->io", left, right, preferred_element_type=F32)


def on_device(
    inputs,
    out_cotangent,
    doc_lengths,
    ln1_gain,
    w_query,
    w_key,
    w_value,
    w_gate,
    w_out,
    ln2_gain,
    w_up,
    up_bias,
    w_down,
):
    n_dph, n_dpl, n_pb, n_ka = (lax.axis_size(a) for a in ("dph", "dpl", "pb", "ka"))
    at_dpl, at_pb, at_ka = (lax.axis_index(a) for a in ("dpl", "pb", "ka"))
    batch, length, width = inputs.shape
    span = n_ka * length
    rows = w_query.shape[0]
    wide_rows = w_down.shape[0]
    key_width = w_query.shape[1] // H
    value_width = w_value.shape[1] // H
    units = n_dph * n_pb * wide_rows
    group = n_dpl * n_ka
    heads_pb = H // (n_dpl * n_dph)

    def to_inner(values):
        lead = values.shape[:-1]
        cut = values.reshape(lead + (n_dph, n_dpl, n_pb, n_ka * rows))
        return jnp.swapaxes(cut, -3, -2).reshape(values.shape)

    def to_outer(values):
        lead = values.shape[:-1]
        cut = values.reshape(lead + (n_dph, n_pb, n_dpl, n_ka * rows))
        return jnp.swapaxes(cut, -3, -2).reshape(values.shape)

    def by_head(weight):
        cut = weight.reshape(rows, H // (n_dpl * heads_pb), n_dpl, heads_pb, -1)
        return jnp.swapaxes(cut, 1, 2).reshape(rows, group, -1)

    def from_head(values):
        cut = values.reshape(rows, n_dpl, H // (n_dpl * heads_pb), heads_pb, -1)
        return jnp.swapaxes(cut, 1, 2).reshape(rows, -1)

    def by_unit(weight):
        cut = weight.reshape(rows, n_dph, n_dpl, n_pb, n_ka, wide_rows)
        return jnp.transpose(cut, (0, 2, 4, 1, 3, 5)).reshape(rows, group, units)

    def from_unit(values):
        cut = values.reshape(rows, n_dpl, n_ka, n_dph, n_pb, wide_rows)
        return jnp.transpose(cut, (0, 3, 1, 4, 2, 5)).reshape(rows, -1)

    def swap_plane(values):
        return lax.all_to_all(values, PLANE, split_axis=1, concat_axis=0, tiled=True).reshape(
            group * rows, -1
        )

    def swap_plane_back(values):
        cut = values.reshape(group * rows, 1, -1)
        return lax.all_to_all(cut, PLANE, split_axis=0, concat_axis=1, tiled=True)

    def gather_line(values):
        return lax.all_gather(values, LINE, axis=0, tiled=True)

    def scatter_line(values):
        return lax.psum_scatter(values, LINE, scatter_dimension=0, tiled=True)

    gain_one = ln1_gain.astype(BF16).astype(F32)[:, None]
    gain_two = ln2_gain.astype(BF16).astype(F32)[:, None]
    firsts = [w.astype(BF16) for w in (w_query, w_key, w_value, w_gate)]
    up_low = w_up.astype(BF16)

    def scaled(weight, gain):
        return (weight.astype(F32) * gain).astype(BF16)

    first_pack = jnp.concatenate([by_head(scaled(w, gain_one)) for w in firsts], axis=-1)
    weight_first = gather_line(swap_plane(first_pack))
    weight_out_rows = gather_line(to_inner(w_out.astype(BF16)))
    weight_out = lax.all_to_all(weight_out_rows, "ka", split_axis=0, concat_axis=0, tiled=True)
    weight_out = (
        weight_out.reshape(n_ka, n_pb // heads_pb, wide_rows, width)
        .swapaxes(0, 1)
        .reshape(value_width, width)
    )
    weight_up = gather_line(swap_plane(by_unit(scaled(up_low, gain_two))))
    down_pack = jnp.concatenate(
        [
            to_inner(w_down.astype(BF16)),
            jnp.broadcast_to(up_bias.astype(BF16)[:, None], (wide_rows, 128)),
        ],
        axis=-1,
    )
    down_pack = gather_line(down_pack)
    weight_down = down_pack[:, :width]
    bias_up = down_pack[:, width].astype(F32)

    head = (
        (at_ka // heads_pb) * (n_dpl * heads_pb) + at_dpl * heads_pb + at_ka % heads_pb
    ).astype(F32)
    log_gamma = jnp.log(1.0 - jnp.exp2(-5.0 - head))
    offsets = jnp.arange(span, dtype=jnp.int32)
    places = (at_pb * span + offsets).astype(F32)
    tables_q = turn_tables(places, key_width // 2, 1.0)
    tables_k = turn_tables(places, key_width // 2, -1.0)
    distance = offsets[:, None] - offsets[None, :]
    decay = jnp.where(
        distance >= 0, jnp.exp(jnp.maximum(distance, 0).astype(F32) * log_gamma), 0.0
    )
    decay_in = jnp.exp(offsets.astype(F32) * log_gamma)[:, None]
    decay_out = jnp.exp((span - offsets).astype(F32) * log_gamma)[:, None]
    decay_span = jnp.exp(span * log_gamma)
    lengths = lax.all_gather(doc_lengths, "dpl", axis=0, tiled=True)
    ends = jnp.cumsum(lengths, axis=-1)
    edge = at_pb * span

    def goes_on(start):
        return jnp.all(ends != start, axis=-1).astype(F32)

    coef_forward = jnp.stack([goes_on(edge), jnp.full((n_dpl * batch,), decay_span)])
    coef_backward = jnp.stack([goes_on(edge + span), jnp.full((n_dpl * batch,), decay_span)])

    rows_in = to_inner(inputs).astype(F32)
    rows_cot = to_inner(out_cotangent)
    normed_one, inv_one = normalize(rows_in)
    normed_one_all = plane_gather(normed_one.astype(BF16), 0)
    cot_all = plane_gather(rows_cot, 1)
    first = mm(normed_one_all, weight_first)
    query_pre = first[..., :key_width]
    key_pre = first[..., key_width : 2 * key_width]
    value = first[..., 2 * key_width : 2 * key_width + value_width].astype(BF16)
    gate = first[..., 2 * key_width + value_width :]
    scale = key_width ** (-0.5)
    query = (turn(query_pre, tables_q) * scale).astype(BF16)
    key = turn(key_pre, tables_k).astype(BF16)
    key_out = (key.astype(F32) * decay_out).astype(BF16)
    state = jnp.einsum("smd,sme->sde", key_out, value, preferred_element_type=F32)
    carried = line_scan(state, coef_forward, n_pb, True, 2)
    raw = jnp.einsum("snd,smd->snm", query, key, preferred_element_type=F32)
    scores = (raw * decay).astype(BF16)
    retained = jnp.einsum("snm,sme->sne", scores, value, preferred_element_type=F32)
    retained = retained + decay_in * jnp.einsum(
        "snd,sde->sne", query, carried, preferred_element_type=F32
    )
    normed_ret, inv_ret = normalize(retained)
    opened = jax.nn.sigmoid(gate)
    silu = gate * opened
    gated = (silu * normed_ret).astype(BF16)
    attended = plane_scatter(mm(gated, weight_out).astype(BF16), 3)
    middle = rows_in + attended
    normed_two, inv_two = normalize(middle)
    normed_two_all = plane_gather(normed_two.astype(BF16), 4)
    up_pre = mm(normed_two_all, weight_up) + bias_up
    bell = 0.5 * (1.0 + lax.erf(up_pre * np.float32(math.sqrt(0.5))))
    active = (up_pre * bell).astype(BF16)

    slope = bell + up_pre * (
        jnp.exp(-0.5 * up_pre * up_pre) * np.float32(1.0 / math.sqrt(2.0 * math.pi))
    )
    grad_up_pre = (mm_back(cot_all, weight_down) * slope).astype(BF16)
    normed_two_back = plane_scatter(mm_back(grad_up_pre, weight_up).astype(BF16), 5)
    grad_middle = rows_cot.astype(F32) + normalize_back(normed_two, inv_two, normed_two_back)
    grad_down = mm_grad(active, cot_all).astype(BF16)
    grad_bias = jnp.sum(grad_up_pre.astype(F32), axis=(0, 1)).astype(BF16)
    grad_down = scatter_line(
        jnp.concatenate(
            [grad_down, jnp.broadcast_to(grad_bias[:, None], (units, 128))], axis=-1
        )
    )
    grad_up = scatter_line(mm_grad(normed_two_all, grad_up_pre).astype(BF16))
    grad_mid_all = plane_gather(grad_middle.astype(BF16), 6)
    grad_gated = mm_back(grad_mid_all, weight_out)
    grad_gate = (grad_gated * normed_ret * (opened + silu * (1.0 - opened))).astype(BF16)
    grad_ret = normalize_back(normed_ret, inv_ret, grad_gated * silu).astype(BF16)
    query_in = (query.astype(F32) * decay_in).astype(BF16)
    grad_state = jnp.einsum("snd,sne->sde", query_in, grad_ret, preferred_element_type=F32)
    grad_carried = line_scan(grad_state, coef_backward, n_pb, False, 7)
    grad_out = mm_grad(gated, grad_mid_all).astype(BF16)
    grad_gate_w = scatter_line(mm_grad(normed_one_all, grad_gate).astype(BF16))
    grad_scores = (
        jnp.einsum("sne,sme->snm", grad_ret, value, preferred_element_type=F32) * decay
    ).astype(BF16)
    grad_query = jnp.einsum("snm,smd->snd", grad_scores, key, preferred_element_type=F32)
    grad_query = grad_query + decay_in * jnp.einsum(
        "sne,sde->snd", grad_ret, carried, preferred_element_type=F32
    )
    grad_key = jnp.einsum("snm,snd->smd", grad_scores, query, preferred_element_type=F32)
    grad_key = grad_key + decay_out * jnp.einsum(
        "sme,sde->smd", value, grad_carried, preferred_element_type=F32
    )
    grad_value = jnp.einsum("snm,sne->sme", scores, grad_ret, preferred_element_type=F32)
    grad_value = grad_value + decay_out * jnp.einsum(
        "smd,sde->sme", key, grad_carried, preferred_element_type=F32
    )
    grad_qkv = jnp.concatenate(
        [
            (turn_back(grad_query, tables_q) * scale).astype(BF16),
            turn_back(grad_key, tables_k).astype(BF16),
            grad_value.astype(BF16),
        ],
        axis=-1,
    )
    grad_qkv_w = scatter_line(mm_grad(normed_one_all, grad_qkv).astype(BF16))
    qkv_width = grad_qkv.shape[-1]
    normed_one_back = mm_back(grad_qkv, weight_first[:, :qkv_width]) + mm_back(
        grad_gate, weight_first[:, qkv_width:]
    )
    normed_one_back = plane_scatter(normed_one_back.astype(BF16), 8)
    grad_inputs = to_outer(
        grad_middle + normalize_back(normed_one, inv_one, normed_one_back)
    )
    ff_out = plane_scatter(mm(active, weight_down).astype(BF16), 9)
    output = to_outer((middle + ff_out).astype(BF16))

    grad_out = (
        grad_out.reshape(n_pb // heads_pb, n_ka, wide_rows, width)
        .swapaxes(0, 1)
        .reshape(value_width, width)
    )
    grad_out = lax.all_to_all(grad_out, "ka", split_axis=0, concat_axis=0, tiled=True)
    shard_out = to_outer(scatter_line(grad_out).astype(F32))
    shard_down = to_outer(grad_down[:, :width].astype(F32))
    shard_bias = grad_down[:, width].astype(F32)
    shard_up = from_unit(swap_plane_back(grad_up)).astype(F32)
    shard_gate = from_head(swap_plane_back(grad_gate_w)).astype(F32)
    back = swap_plane_back(grad_qkv_w)
    shard_query = from_head(back[..., :key_width]).astype(F32)
    shard_key = from_head(back[..., key_width : 2 * key_width]).astype(F32)
    shard_value = from_head(back[..., 2 * key_width :]).astype(F32)
    shards = (shard_query, shard_key, shard_value, shard_gate)
    shard_gain_one = sum(
        jnp.sum(low.astype(F32) * grad, axis=-1) for low, grad in zip(firsts, shards)
    )
    shard_gain_two = jnp.sum(up_low.astype(F32) * shard_up, axis=-1)
    shard_query, shard_key, shard_value, shard_gate = (gain_one * g for g in shards)
    return (
        output,
        grad_inputs,
        shard_gain_one,
        shard_query,
        shard_key,
        shard_value,
        shard_gate,
        shard_out,
        shard_gain_two,
        gain_two * shard_up,
        shard_bias,
        shard_down,
    )


def solution(mesh):
    dp, pb, ka = (mesh.shape[a] for a in ("dp", "pb", "ka"))
    fine = Mesh(mesh.devices.reshape(dp // 2, 2, pb, ka), ("dph", "dpl", "pb", "ka"))
    dp_axes = ("dph", "dpl")
    every = ("dph", "dpl", "pb", "ka")
    tokens = P(dp_axes, ("pb", "ka"), None)
    matrix = P(every, None)
    vector = P(every)
    return jax.shard_map(
        on_device,
        mesh=fine,
        in_specs=(
            tokens,
            tokens,
            P(dp_axes, None),
            vector,
            matrix,
            matrix,
            matrix,
            matrix,
            matrix,
            vector,
            matrix,
            vector,
            matrix,
        ),
        out_specs=(
            tokens,
            tokens,
            vector,
            matrix,
            matrix,
            matrix,
            matrix,
            matrix,
            vector,
            matrix,
            vector,
            matrix,
        ),
        check_vma=False,
    )
```

```python
import functools
import math

import jax
import jax.numpy as jnp
import numpy as np
from jax import lax
from jax.experimental import pallas as pl
from jax.experimental.pallas import tpu as pltpu
from jax.sharding import Mesh
from jax.sharding import PartitionSpec as P

H = 8
XPOS_BASE = 512.0
EPSILON = 1e-05
MESH = pl.DeviceIdType.MESH
F32 = jnp.float32
BF16 = jnp.bfloat16

PLANE = ("dpl", "ka")
LINE = ("dph", "pb")


def plane_ids():
    row = lax.axis_index("dpl")
    col = lax.axis_index("ka")
    other_row = 1 - row
    across = lax.rem(col + 2, 4)
    sibling = col + 1 - 2 * lax.rem(col, 2)
    return row, col, other_row, across, sibling


def greet(targets):
    barrier = pltpu.get_barrier_semaphore()
    for target in targets:
        pl.semaphore_signal(barrier, inc=1, device_id=target, device_id_type=MESH)
    pl.semaphore_wait(barrier, len(targets))


def gather_stages(shard, full, local_sem, send_sem, recv_sem):
    batch, length, _ = shard.shape
    half = length // 2
    row, col, other_row, across, sibling = plane_ids()
    to_x = {"ka": across}
    to_y = {"dpl": other_row}
    to_s = {"ka": sibling}

    def slot(r, c, start=0, size=length):
        return full.at[pl.ds(r * batch, batch), pl.ds(c * length + start, size), :]

    def hop(index, target, dst, src=None):
        return pltpu.make_async_remote_copy(
            src_ref=dst if src is None else src,
            dst_ref=dst,
            send_sem=send_sem.at[index],
            recv_sem=recv_sem.at[index],
            device_id=target,
            device_id_type=MESH,
        )

    mine = pltpu.make_async_copy(shard, slot(row, col), local_sem)
    from_x = hop(0, to_x, slot(row, col), shard)
    from_y = hop(1, to_y, slot(row, col), shard)
    own_s = hop(2, to_s, slot(row, col), shard)
    diag_y = hop(3, to_y, slot(row, across, 0, half))
    relay_x = hop(4, to_s, slot(row, across))
    diag_x = hop(5, to_x, slot(other_row, col, half, half))
    relay_y = hop(6, to_s, slot(other_row, col))
    relay_a = hop(7, to_s, slot(other_row, across, 0, half))
    relay_b = hop(8, to_s, slot(other_row, across, half, half))

    def begin():
        from_x.start()
        from_y.start()
        own_s.start()
        mine.start()

    def relay():
        from_x.wait_recv()
        diag_y.start()
        relay_x.start()
        from_y.wait_recv()
        diag_x.start()
        relay_y.start()

    def diagonal():
        diag_y.wait_recv()
        relay_a.start()
        diag_x.wait_recv()
        relay_b.start()

    def end():
        for copy in (own_s, relay_x, relay_y, relay_a, relay_b):
            copy.wait_recv()
        for copy in (from_x, from_y, own_s, diag_y, relay_x, diag_x, relay_y, relay_a, relay_b):
            copy.wait_send()
        mine.wait()

    return (to_x, to_y, to_s), (begin, relay, diagonal, end)


GATHER_SCRATCH = (
    pltpu.SemaphoreType.DMA,
    pltpu.SemaphoreType.DMA((9,)),
    pltpu.SemaphoreType.DMA((9,)),
)


def gathered_shape(shard):
    batch, length, width = shard.shape
    return jax.ShapeDtypeStruct((2 * batch, 4 * length, width), shard.dtype)


def gather_kernel(shard, *refs):
    targets, stages = gather_stages(shard, *refs[-4:])
    greet(targets)
    for stage in stages:
        stage()


def read_rows(ref, b, at, order):
    if not order:
        return ref[b, at, :]
    size = ref.shape[-1] // len(order)
    return jnp.concatenate([ref[b, at, i * size : (i + 1) * size] for i in order], axis=-1)


def write_rows(ref, b, at, order, values):
    if not order:
        ref[b, at, :] = values
        return
    size = ref.shape[-1] // len(order)
    for j, i in enumerate(order):
        ref[b, at, i * size : (i + 1) * size] = values[:, j * size : (j + 1) * size]


def normalize_rows(source, target, order):
    batch, length, _ = source.shape
    step = 16

    def body(i, carry):
        at = pl.ds(i * step, step)
        for b in range(batch):
            normed, _ = normalize(read_rows(source, b, at, order).astype(F32))
            target[b, at, :] = normed.astype(BF16)
        return carry

    lax.fori_loop(0, length // step, body, 0)


def owners_stages(sources, targets, keep_sem, send_sem, recv_sem):
    row, col, other_row, _, _ = plane_ids()
    me = row * 4 + col
    peers = [(row, lax.rem(col + away, 4)) for away in (1, 2, 3)]
    peers += [(other_row, lax.rem(col + away, 4)) for away in (0, 1, 2, 3)]
    copies = []
    for a in range(len(sources)):
        copies.append(
            pltpu.make_async_copy(sources[a].at[me], targets[a].at[me], keep_sem.at[a])
        )
        for i in (6, 5, 4, 3, 2, 1, 0):
            r, c = peers[i]
            copies.append(
                pltpu.make_async_remote_copy(
                    src_ref=sources[a].at[r * 4 + c],
                    dst_ref=targets[a].at[me],
                    send_sem=send_sem.at[a, i],
                    recv_sem=recv_sem.at[a, i],
                    device_id={"dpl": r, "ka": c},
                    device_id_type=MESH,
                )
            )

    def begin():
        for copy in copies:
            copy.start()

    def end():
        for copy in copies:
            copy.wait()

    return [{"dpl": r, "ka": c} for r, c in peers], (begin, end)


def owners_scratch(count):
    return [
        pltpu.SemaphoreType.DMA((count,)),
        pltpu.SemaphoreType.DMA((count, 7)),
        pltpu.SemaphoreType.DMA((count, 7)),
    ]


def trade_stages(line, source, target, sems):
    place, col = lax.axis_index(line), lax.axis_index("ka")
    moves = place != col
    partner = {line: col, "ka": place}

    def trade():
        return pltpu.make_async_remote_copy(
            src_ref=source,
            dst_ref=target,
            send_sem=sems.at[0],
            recv_sem=sems.at[1],
            device_id=partner,
            device_id_type=MESH,
        )

    def keep():
        return pltpu.make_async_copy(source, target, sems.at[2])

    def greet_partner(barrier):
        @pl.when(moves)
        def _():
            pl.semaphore_signal(barrier, inc=1, device_id=partner, device_id_type=MESH)

        return moves.astype(jnp.int32)

    def begin():
        @pl.when(moves)
        def _():
            trade().start()

        @pl.when(jnp.logical_not(moves))
        def _():
            keep().start()

    def end():
        @pl.when(moves)
        def _():
            trade().wait()

        @pl.when(jnp.logical_not(moves))
        def _():
            keep().wait()

    return greet_partner, (begin, end)


TRADE_SCRATCH = (pltpu.SemaphoreType.DMA((3,)),)


def open_kernel(line, order, x, up, out, *refs):
    normed_all, up_mine, out_mine, normed = refs[:4]
    sems = refs[4:]
    targets, owners = owners_stages((up,), (up_mine,), *sems[3:6])
    _, gather = gather_stages(normed, normed_all, *sems[:3])
    greet_partner, trade = trade_stages(line, out, out_mine, sems[6])
    barrier = pltpu.get_barrier_semaphore()
    for target in targets:
        pl.semaphore_signal(barrier, inc=1, device_id=target, device_id_type=MESH)
    extra = greet_partner(barrier)
    normalize_rows(x, normed, order)
    pl.semaphore_wait(barrier, len(targets) + extra)
    gather[0]()
    trade[0]()
    owners[0]()
    for stage in gather[1:]:
        stage()
    owners[1]()
    trade[1]()


def open_plane(x, up, out, line, order, collective_id, *before):
    anywhere = pl.BlockSpec(memory_space=pl.ANY)
    return pl.pallas_call(
        lambda a, b, c, *refs: open_kernel(line, order, a, b, c, *refs[len(before) :]),
        out_shape=[
            gathered_shape(x),
            jax.ShapeDtypeStruct(up.shape, up.dtype),
            jax.ShapeDtypeStruct(out.shape, out.dtype),
        ],
        in_specs=[pl.BlockSpec(memory_space=pltpu.VMEM)] + [anywhere] * (2 + len(before)),
        out_specs=[anywhere] * 3,
        scratch_shapes=[
            pltpu.VMEM(x.shape, BF16),
            *GATHER_SCRATCH,
            *owners_scratch(1),
            *TRADE_SCRATCH,
        ],
        compiler_params=pltpu.CompilerParams(
            collective_id=collective_id,
            has_side_effects=True,
            vmem_limit_bytes=16 * 1024 * 1024,
        ),
        name="open_plane",
    )(x, up, out, *before)


def scatter_stages(
    terms, finish, sent, own, sib, from_x, from_y, diag_a, diag_b, sems, recvs, earlier=()
):
    _, batch, length, width = own.shape
    half = length // 2
    row, col, other_row, across, sibling = plane_ids()
    across_s = lax.rem(sibling + 2, 4)
    to_x = {"ka": across}
    to_y = {"dpl": other_row}
    to_s = {"ka": sibling}
    mine = ((other_row, across), (row, across), (other_row, col), (row, col))
    theirs = ((other_row, across_s), (row, across_s), (other_row, sibling), (row, sibling))
    lower, upper = pl.ds(0, half), pl.ds(half, half)
    step = 16
    tile = 512

    def hop(src, dst, index, target):
        return pltpu.make_async_remote_copy(
            src_ref=src,
            dst_ref=dst,
            send_sem=sems.at[index],
            recv_sem=recvs.at[index],
            device_id=target,
            device_id_type=MESH,
        )

    swaps = [hop(sent.at[j], sib.at[j], j, to_s) for j in range(4)]
    first_a = hop(own.at[0, :, lower, :], diag_a, 4, to_x)
    first_b = hop(own.at[0, :, upper, :], diag_b, 5, to_y)
    x_lower = hop(own.at[1, :, lower, :], from_x.at[:, lower, :], 6, to_x)
    y_upper = hop(own.at[2, :, upper, :], from_y.at[:, upper, :], 7, to_y)
    x_upper = hop(own.at[1, :, upper, :], from_x.at[:, upper, :], 8, to_x)
    y_lower = hop(own.at[2, :, lower, :], from_y.at[:, lower, :], 9, to_y)

    def make(r, c, out):
        def body(n, carry):
            columns = pl.ds(pl.multiple_of(n * tile, tile), tile)
            value = 0.0
            for left, right, flipped in terms:
                block = left[pl.ds(r * batch, batch), pl.ds(c * length, length), :]
                block = block.reshape(batch * length, left.shape[2])
                if flipped:
                    value = value + lax.dot_general(
                        block,
                        right[columns, :],
                        (((1,), (1,)), ((), ())),
                        preferred_element_type=F32,
                    )
                else:
                    value = value + jnp.dot(
                        block, right[:, columns], preferred_element_type=F32
                    )
            out[:, :, columns] = value.reshape(batch, length, tile).astype(BF16)
            return carry

        lax.fori_loop(0, width // tile, body, 0)

    def give(j):
        if earlier:
            earlier[j].wait_send()
        make(*theirs[j], sent.at[j])
        swaps[j].start()

    def add(out_ref, out_start, parts, size):
        def body(i, carry):
            value = 0.0
            for ref, start in parts:
                value = value + ref[:, pl.ds(start + i * step, step), :].astype(F32)
            out_ref[:, pl.ds(out_start + i * step, step), :] = value.astype(out_ref.dtype)
            return carry

        lax.fori_loop(0, size // step, body, 0)

    def merge(j):
        swaps[j].wait_recv()
        add(own.at[j], 0, ((own.at[j], 0), (sib.at[j], 0)), length)

    def stage_begin():
        give(0)
        make(*mine[0], own.at[0])

    def stage_diag():
        merge(0)
        first_a.start()
        first_b.start()
        give(1)
        make(*mine[1], own.at[1])

    def stage_x():
        merge(1)
        x_lower.start()
        give(2)
        make(*mine[2], own.at[2])

    def stage_y():
        merge(2)
        y_upper.start()
        give(3)
        make(*mine[3], own.at[3])

    def stage_rest():
        first_b.wait_recv()
        add(own.at[1], half, ((own.at[1], half), (diag_b, 0)), half)
        x_upper.start()
        first_a.wait_recv()
        add(own.at[2], 0, ((own.at[2], 0), (diag_a, 0)), half)
        y_lower.start()
        merge(3)

    def close(start):
        def body(i, carry):
            at = pl.ds(start + i * step, step)
            for b in range(batch):
                value = own[3, b, at, :].astype(F32)
                value = value + from_x[b, at, :].astype(F32) + from_y[b, at, :].astype(F32)
                finish(b, at, value)
            return carry

        lax.fori_loop(0, half // step, body, 0)

    def stage_end():
        x_lower.wait_recv()
        y_lower.wait_recv()
        close(0)
        y_upper.wait_recv()
        x_upper.wait_recv()
        close(half)
        for copy in (first_a, first_b, x_lower, x_upper, y_lower, y_upper):
            copy.wait_send()

    def stage_free():
        for copy in swaps:
            copy.wait_send()

    stages = (stage_begin, stage_diag, stage_x, stage_y, stage_rest, stage_end, stage_free)
    return (to_x, to_y, to_s), stages, swaps


def scatter_scratch(shape):
    batch, length, width = shape
    return [
        pltpu.VMEM((4,) + shape, BF16),
        pltpu.VMEM((4,) + shape, BF16),
        pltpu.VMEM((4,) + shape, BF16),
        pltpu.VMEM(shape, BF16),
        pltpu.VMEM(shape, BF16),
        pltpu.VMEM((batch, length // 2, width), BF16),
        pltpu.VMEM((batch, length // 2, width), BF16),
        pltpu.SemaphoreType.DMA((10,)),
        pltpu.SemaphoreType.DMA((10,)),
    ]


VMEM = pl.BlockSpec(memory_space=pltpu.VMEM)
ANY = pl.BlockSpec(memory_space=pl.ANY)


def mix_kernel(order, gated, weight, x, *refs):
    middle, normed_all, normed = refs[-15:-12]

    def finish(b, at, value):
        value = value + read_rows(x, b, at, order).astype(F32)
        middle[b, at, :] = value
        normed[b, at, :] = normalize(value)[0].astype(BF16)

    targets, stages, _ = scatter_stages(((gated, weight, False),), finish, *refs[-12:-3])
    _, gather = gather_stages(normed, normed_all, *refs[-3:])
    greet(targets)
    for stage in stages + gather:
        stage()


def plane_mix(gated, weight, x, order, collective_id, *before):
    shape = x.shape
    return pl.pallas_call(
        functools.partial(mix_kernel, order),
        out_shape=[jax.ShapeDtypeStruct(shape, F32), gathered_shape(x)],
        in_specs=[VMEM] * 3 + [ANY] * len(before),
        out_specs=[VMEM, ANY],
        scratch_shapes=[
            pltpu.VMEM(shape, BF16),
            *scatter_scratch(shape),
            *GATHER_SCRATCH,
        ],
        compiler_params=pltpu.CompilerParams(
            collective_id=collective_id,
            has_side_effects=True,
            vmem_limit_bytes=48 * 1024 * 1024,
        ),
        name="plane_mix",
    )(gated, weight, x, *before)


def turn_kernel(order, grad, weight, middle, cot, *refs):
    grad_middle, grad_all, low = refs[-15:-12]

    def finish(b, at, value):
        normed, inv = normalize(middle[b, at, :])
        value = normalize_back(normed, inv, value)
        value = value + read_rows(cot, b, at, order).astype(F32)
        grad_middle[b, at, :] = value
        low[b, at, :] = value.astype(BF16)

    targets, stages, _ = scatter_stages(((grad, weight, True),), finish, *refs[-12:-3])
    _, gather = gather_stages(low, grad_all, *refs[-3:])
    greet(targets)
    for stage in stages + gather:
        stage()


def plane_turn(grad, weight, middle, cot, order, collective_id, *before):
    shape = middle.shape
    return pl.pallas_call(
        functools.partial(turn_kernel, order),
        out_shape=[jax.ShapeDtypeStruct(shape, F32), gathered_shape(cot)],
        in_specs=[VMEM] * 4 + [ANY] * len(before),
        out_specs=[VMEM, ANY],
        scratch_shapes=[
            pltpu.VMEM(shape, BF16),
            *scatter_scratch(shape),
            *GATHER_SCRATCH,
        ],
        compiler_params=pltpu.CompilerParams(
            collective_id=collective_id,
            has_side_effects=True,
            vmem_limit_bytes=48 * 1024 * 1024,
        ),
        name="plane_turn",
    )(grad, weight, middle, cot, *before)


def last_kernel(order, owned, *refs):
    grad_a, weight_a, grad_b, weight_b, x, grad_middle, active, weight_down, middle = refs[:9]
    outs, scratch = refs[-22 - owned : -20], refs[-20:]

    def finish_grad(b, at, value):
        normed, inv = normalize(read_rows(x, b, at, order).astype(F32))
        value = grad_middle[b, at, :] + normalize_back(normed, inv, value)
        write_rows(outs[0], b, at, order, value)

    def finish_out(b, at, value):
        write_rows(outs[1], b, at, order, (middle[b, at, :] + value).astype(BF16))

    terms = ((grad_a, weight_a, True), (grad_b, weight_b, True))
    _, grads, swaps = scatter_stages(terms, finish_grad, *scratch[:9])
    _, out, _ = scatter_stages(
        ((active, weight_down, False),), finish_out, scratch[0], *scratch[9:17], earlier=swaps
    )
    targets, owners = owners_stages(refs[9 : 9 + owned], outs[2:], *scratch[17:])
    greet(targets)
    for stage in grads[:4] + out[:2]:
        stage()
    grads[4]()
    out[2]()
    out[3]()
    owners[0]()
    grads[5]()
    for stage in out[4:]:
        stage()
    owners[1]()


def plane_last(terms, x, grad_middle, summed, owned, order, collective_id, *before):
    shape = x.shape
    return pl.pallas_call(
        functools.partial(last_kernel, order, len(owned)),
        out_shape=[jax.ShapeDtypeStruct(shape, F32), jax.ShapeDtypeStruct(shape, BF16)]
        + [jax.ShapeDtypeStruct(a.shape, a.dtype) for a in owned],
        in_specs=[VMEM] * 9 + [ANY] * (len(owned) + len(before)),
        out_specs=[VMEM] * 2 + [ANY] * len(owned),
        scratch_shapes=scatter_scratch(shape)
        + scatter_scratch(shape)[1:]
        + owners_scratch(len(owned)),
        compiler_params=pltpu.CompilerParams(
            collective_id=collective_id,
            has_side_effects=True,
            vmem_limit_bytes=60 * 1024 * 1024,
        ),
        name="plane_last",
    )(*terms, x, grad_middle, *summed, *owned, *before)


def scan_kernel(count, forward, cuts, gathers, order, state, coef, *refs):
    targets, stages = (), ()
    if gathers:
        moved = refs[0]
        total, result, message, landed, send_sem, recv_sem = refs[-11:-5]
        shard, shard_sem = refs[-5:-3]
        targets, stages = gather_stages(shard, result, *refs[-3:])
    else:
        total, message, landed, send_sem, recv_sem = refs[-5:]
    here = lax.axis_index("pb")
    place = here if forward else count - 1 - here
    step = 1 if forward else -1
    has_prev = place > 0
    has_next = place < count - 1
    barrier = pltpu.get_barrier_semaphore()

    @pl.when(has_prev)
    def _():
        pl.semaphore_signal(barrier, inc=1, device_id={"pb": here - step}, device_id_type=MESH)

    @pl.when(has_next)
    def _():
        pl.semaphore_signal(barrier, inc=1, device_id={"pb": here + step}, device_id_type=MESH)

    greeted = has_prev.astype(jnp.int32) + has_next.astype(jnp.int32)
    for target in targets:
        pl.semaphore_signal(barrier, inc=1, device_id=target, device_id_type=MESH)
    pl.semaphore_wait(barrier, greeted + len(targets))

    height = state.shape[1] // cuts
    pieces = [(s, c) for s in range(state.shape[0]) for c in range(cuts)]

    def hop(i):
        s, c = pieces[i]
        rows = pl.ds(c * height, height)
        return pltpu.make_async_remote_copy(
            src_ref=message.at[s, rows],
            dst_ref=landed.at[s, rows],
            send_sem=send_sem.at[i],
            recv_sem=recv_sem.at[i],
            device_id={"pb": here + step},
            device_id_type=MESH,
        )

    def emit(i):
        s, c = pieces[i]
        rows = pl.ds(c * height, height)

        @pl.when(jnp.logical_not(has_prev))
        def _():
            message[s, rows] = state[s, rows].astype(BF16)
            hop(i).start()
            total[s, rows] = jnp.zeros((height, state.shape[2]), BF16)

        @pl.when(has_prev)
        def _():
            hop(i).wait_recv()
            total[s, rows] = (coef[0, s] * landed[s, rows].astype(F32)).astype(BF16)

            @pl.when(has_next)
            def _():
                message[s, rows] = (
                    state[s, rows] + coef[1, s] * total[s, rows].astype(F32)
                ).astype(BF16)
                hop(i).start()

    emit(0)
    if gathers:
        size = shard.shape[-1] // max(len(order), 1)
        for move in (0, 1):
            for j, i in enumerate(order or (0,)):
                copy = pltpu.make_async_copy(
                    moved.at[:, :, pl.ds(i * size, size)],
                    shard.at[:, :, pl.ds(j * size, size)],
                    shard_sem.at[j],
                )
                if move:
                    copy.wait()
                else:
                    copy.start()
        stages[0]()
    for i in range(1, len(pieces)):
        emit(i)
        if gathers and i == len(pieces) // 2:
            stages[1]()
        if gathers and i == 3 * len(pieces) // 4:
            stages[2]()
    if gathers:
        stages[3]()

    @pl.when(has_next)
    def _():
        for i in range(len(pieces)):
            hop(i).wait_send()


def line_scan(state, coef, count, forward, order, collective_id, *before, gathered=None):
    cuts = 4
    pieces = state.shape[0] * cuts
    shapes, specs, operands = [jax.ShapeDtypeStruct(state.shape, BF16)], [VMEM], [state, coef]
    scratch = [
        pltpu.VMEM(state.shape, BF16),
        pltpu.VMEM(state.shape, BF16),
        pltpu.SemaphoreType.DMA((pieces,)),
        pltpu.SemaphoreType.DMA((pieces,)),
    ]
    if gathered is not None:
        operands.append(gathered)
        shapes.append(gathered_shape(gathered))
        specs.append(ANY)
        scratch += [
            pltpu.VMEM(gathered.shape, gathered.dtype),
            pltpu.SemaphoreType.DMA((max(len(order), 1),)),
            *GATHER_SCRATCH,
        ]
    results = pl.pallas_call(
        functools.partial(scan_kernel, count, forward, cuts, gathered is not None, order),
        out_shape=shapes,
        in_specs=[VMEM, pl.BlockSpec(memory_space=pltpu.SMEM)]
        + [ANY] * (len(operands) - 2 + len(before)),
        out_specs=specs,
        scratch_shapes=scratch,
        compiler_params=pltpu.CompilerParams(
            collective_id=collective_id,
            has_side_effects=True,
            vmem_limit_bytes=16 * 1024 * 1024,
        ),
        name="line_scan",
    )(*operands, *before)
    return results if gathered is not None else results[0]


def owners_kernel(arrays, line, *refs):
    trades = 1 if line else 0
    scratch = refs[-3 - trades :]
    outs = refs[-3 - trades - arrays - trades : -3 - trades]
    targets, stages = owners_stages(refs[:arrays], outs[:arrays], *scratch[:3])
    barrier = pltpu.get_barrier_semaphore()
    for target in targets:
        pl.semaphore_signal(barrier, inc=1, device_id=target, device_id_type=MESH)
    greeted = len(targets)
    if line:
        greet_partner, trade = trade_stages(line, refs[arrays], outs[arrays], scratch[3])
        greeted = greeted + greet_partner(barrier)
    pl.semaphore_wait(barrier, greeted)
    stages[0]()
    if line:
        trade[0]()
        trade[1]()
    stages[1]()


def to_owners(arrays, collective_id, *before, line="", traded=()):
    count = len(arrays)
    operands = [*arrays, *traded]
    anywhere = pl.BlockSpec(memory_space=pl.ANY)
    return pl.pallas_call(
        functools.partial(owners_kernel, count, line),
        out_shape=[jax.ShapeDtypeStruct(a.shape, a.dtype) for a in operands],
        in_specs=[anywhere] * (len(operands) + len(before)),
        out_specs=[anywhere] * len(operands),
        scratch_shapes=owners_scratch(count) + (list(TRADE_SCRATCH) if line else []),
        compiler_params=pltpu.CompilerParams(
            collective_id=collective_id, has_side_effects=True
        ),
        name="to_owners",
    )(*operands, *before)


def normalize(values):
    mean = jnp.mean(values, axis=-1, keepdims=True)
    centered = values - mean
    inv = lax.rsqrt(jnp.mean(centered * centered, axis=-1, keepdims=True) + EPSILON)
    return centered * inv, inv


def normalize_back(normed, inv, grad):
    mean = jnp.mean(grad, axis=-1, keepdims=True)
    along = jnp.mean(grad * normed, axis=-1, keepdims=True)
    return inv * (grad - mean - normed * along)


def turn_tables(positions, half, direction):
    pair = jnp.arange(half, dtype=F32)
    frequency = jnp.exp(-jnp.log(10000.0) * pair / half)
    zeta = (pair / half + 0.4) / 1.4
    angles = positions[:, None] * frequency[None, :]
    factor = jnp.exp(direction * positions[:, None] / XPOS_BASE * jnp.log(zeta)[None, :])
    return jnp.cos(angles) * factor, jnp.sin(angles) * factor


def turn(values, tables):
    cosine, sine = tables
    half = values.shape[-1] // 2
    first, second = values[..., :half], values[..., half:]
    return jnp.concatenate(
        [first * cosine - second * sine, second * cosine + first * sine], axis=-1
    )


def turn_back(values, tables):
    cosine, sine = tables
    return turn(values, (cosine, -sine))


def mm(left, right):
    return jnp.einsum("sti,io->sto", left, right, preferred_element_type=F32)


def mm_back(left, right):
    return jnp.einsum("sto,io->sti", left, right, preferred_element_type=F32)


def mm_grad(left, right):
    return jnp.einsum("sti,sto->io", left, right, preferred_element_type=F32)


def after(value, *others):
    for other in others:
        value = value + (0.0 * other[(0,) * other.ndim].astype(F32)).astype(value.dtype)
    return value


def on_device(
    inputs,
    out_cotangent,
    doc_lengths,
    ln1_gain,
    w_query,
    w_key,
    w_value,
    w_gate,
    w_out,
    ln2_gain,
    w_up,
    up_bias,
    w_down,
):
    n_dph, n_dpl, n_pb, n_ka = (lax.axis_size(a) for a in ("dph", "dpl", "pb", "ka"))
    at_dpl, at_pb, at_ka = (lax.axis_index(a) for a in ("dpl", "pb", "ka"))
    batch, length, width = inputs.shape
    span = n_ka * length
    rows = w_query.shape[0]
    wide_rows = w_down.shape[0]
    key_width = w_query.shape[1] // H
    value_width = w_value.shape[1] // H
    units = n_dph * n_pb * wide_rows
    group = n_dpl * n_ka
    heads_pb = H // (n_dpl * n_dph)

    chunk = n_ka * rows

    def pick(values, order):
        return jnp.concatenate(
            [values[..., i * chunk : (i + 1) * chunk] for i in order], axis=-1
        )

    inner = [
        (d * n_dpl + r) * n_pb + p
        for d in range(n_dph)
        for p in range(n_pb)
        for r in range(n_dpl)
    ]

    def to_inner(values):
        return pick(values, inner)

    def to_outer(values):
        return pick(values, [inner.index(i) for i in range(len(inner))])

    def by_head(weight):
        cut = weight.reshape(rows, H // (n_dpl * heads_pb), n_dpl, heads_pb, -1)
        return jnp.transpose(cut, (2, 1, 3, 0, 4)).reshape(group, rows, -1)

    def from_head(values):
        cut = values.reshape(n_dpl, H // (n_dpl * heads_pb), heads_pb, rows, -1)
        return jnp.transpose(cut, (3, 1, 0, 2, 4)).reshape(rows, -1)

    def by_unit(weight):
        cut = weight.reshape(rows, n_dph, n_dpl, n_pb, n_ka, wide_rows)
        return jnp.transpose(cut, (2, 4, 0, 1, 3, 5)).reshape(group, rows, units)

    def from_unit(values):
        cut = values.reshape(n_dpl, n_ka, rows, n_dph, n_pb, wide_rows)
        return jnp.transpose(cut, (2, 3, 0, 4, 1, 5)).reshape(rows, -1)

    def gather_line(values):
        return lax.all_gather(values, LINE, axis=0, tiled=True)

    def scatter_line(values):
        return lax.psum_scatter(values, LINE, scatter_dimension=0, tiled=True)

    line = "dph" if n_dph > 1 else "pb"

    gain_one = ln1_gain.astype(BF16).astype(F32)[:, None]
    gain_two = ln2_gain.astype(BF16).astype(F32)[:, None]
    firsts = [w.astype(BF16) for w in (w_query, w_key, w_value, w_gate)]
    up_low = w_up.astype(BF16)

    def scaled(weight, gain):
        return (weight.astype(F32) * gain).astype(BF16)

    query_pack, key_pack, value_pack, gate_pack = (by_head(scaled(w, gain_one)) for w in firsts)
    qkv_swapped, gate_swapped = to_owners(
        [jnp.concatenate([query_pack, key_pack, value_pack], axis=-1), gate_pack], 0
    )
    order = tuple(inner) if chunk % 128 == 0 else ()
    rows_in, rows_cot = inputs, out_cotangent
    if not order:
        rows_in, rows_cot = to_inner(inputs), to_inner(out_cotangent)
    head = (
        (at_ka // heads_pb) * (n_dpl * heads_pb) + at_dpl * heads_pb + at_ka % heads_pb
    ).astype(F32)
    log_gamma = jnp.log(1.0 - jnp.exp2(-5.0 - head))
    offsets = jnp.arange(span, dtype=jnp.int32)
    places = (at_pb * span + offsets).astype(F32)
    tables_q = turn_tables(places, key_width // 2, 1.0)
    tables_k = turn_tables(places, key_width // 2, -1.0)
    distance = offsets[:, None] - offsets[None, :]
    decay = jnp.where(
        distance >= 0, jnp.exp(jnp.maximum(distance, 0).astype(F32) * log_gamma), 0.0
    )
    decay_in = jnp.exp(offsets.astype(F32) * log_gamma)[:, None]
    decay_out = jnp.exp((span - offsets).astype(F32) * log_gamma)[:, None]
    decay_span = jnp.exp(span * log_gamma)
    lengths = lax.all_gather(doc_lengths, "dpl", axis=0, tiled=True)
    ends = jnp.cumsum(lengths, axis=-1)
    edge = at_pb * span

    def goes_on(start):
        return jnp.all(ends != start, axis=-1).astype(F32)

    coef_forward = jnp.stack([goes_on(edge), jnp.full((n_dpl * batch,), decay_span)])
    coef_backward = jnp.stack([goes_on(edge + span), jnp.full((n_dpl * batch,), decay_span)])

    down_pack = jnp.concatenate(
        [
            to_inner(w_down.astype(BF16)),
            jnp.broadcast_to(up_bias.astype(BF16)[:, None], (wide_rows, 128)),
        ],
        axis=-1,
    )
    normed_one_all, up_swapped, out_moved = open_plane(
        rows_in,
        by_unit(scaled(up_low, gain_two)),
        to_inner(w_out.astype(BF16)),
        line,
        order,
        1,
        qkv_swapped,
        down_pack,
        coef_forward,
        coef_backward,
        *tables_q,
        *tables_k,
        decay,
    )
    weight_qkv = gather_line(qkv_swapped.reshape(group * rows, -1))
    blocks = width // units
    gate_out = jnp.concatenate(
        [after(gate_swapped.reshape(group * rows, -1), normed_one_all)]
        + [out_moved[:, i * units : (i + 1) * units] for i in range(blocks)],
        axis=0,
    )
    gate_out = gather_line(gate_out)
    first = mm(normed_one_all, weight_qkv)
    query_pre = first[..., :key_width]
    key_pre = first[..., key_width : 2 * key_width]
    value = first[..., 2 * key_width :].astype(BF16)
    scale = key_width ** (-0.5)
    query = (turn(query_pre, tables_q) * scale).astype(BF16)
    key = turn(key_pre, tables_k).astype(BF16)
    key_out = (key.astype(F32) * decay_out).astype(BF16)
    state = jnp.einsum("smd,sme->sde", key_out, value, preferred_element_type=F32)
    carried, cot_all = line_scan(
        state, coef_forward, n_pb, True, order, 2, gathered=rows_cot
    )
    raw = jnp.einsum("snd,smd->snm", query, key, preferred_element_type=F32)
    scores = (raw * decay).astype(BF16)
    retained = jnp.einsum("snm,sme->sne", scores, value, preferred_element_type=F32)
    retained = retained + decay_in * jnp.einsum(
        "snd,sde->sne", query, carried, preferred_element_type=F32
    )
    gate_out = after(gate_out, retained).reshape(n_dph * n_pb, -1, units)
    weight_gate = gate_out[:, : group * rows].reshape(width, units)
    weight_out = (
        gate_out[:, group * rows :]
        .reshape(-1, n_pb // heads_pb, blocks, wide_rows, units)
        .transpose(1, 0, 3, 2, 4)
        .reshape(value_width, width)
    )
    weight_up = gather_line(after(up_swapped.reshape(group * rows, -1), weight_out))
    down_pack = gather_line(after(down_pack, weight_out))
    weight_down = down_pack[:, :width]
    bias_up = down_pack[:, width].astype(F32)
    normed_ret, inv_ret = normalize(retained)
    gate = mm(normed_one_all, weight_gate)
    opened = jax.nn.sigmoid(gate)
    silu = gate * opened
    gated = (silu * normed_ret).astype(BF16)
    middle, normed_two_all = plane_mix(gated, weight_out, rows_in, order, 3)
    up_pre = mm(normed_two_all, weight_up) + bias_up
    bell = 0.5 * (1.0 + lax.erf(up_pre * np.float32(math.sqrt(0.5))))
    active = (up_pre * bell).astype(BF16)

    slope = bell + up_pre * (
        jnp.exp(-0.5 * up_pre * up_pre) * np.float32(1.0 / math.sqrt(2.0 * math.pi))
    )
    grad_up_pre = (mm_back(cot_all, weight_down) * slope).astype(BF16)
    grad_bias = jnp.sum(grad_up_pre.astype(F32), axis=(0, 1)).astype(BF16)
    grad_down = jnp.concatenate(
        [
            mm_grad(active, cot_all).astype(BF16),
            jnp.broadcast_to(grad_bias[:, None], (units, 128)),
        ],
        axis=-1,
    )
    grad_up = mm_grad(normed_two_all, grad_up_pre).astype(BF16)
    grad_middle, grad_mid_all = plane_turn(
        grad_up_pre, weight_up, middle, rows_cot, order, 5, grad_down, grad_up
    )
    grad_down = scatter_line(grad_down)
    grad_up = scatter_line(grad_up)
    grad_gated = after(mm_back(grad_mid_all, weight_out), grad_up, grad_down)
    grad_gate = (grad_gated * normed_ret * (opened + silu * (1.0 - opened))).astype(BF16)
    grad_ret = normalize_back(normed_ret, inv_ret, grad_gated * silu).astype(BF16)
    query_in = (query.astype(F32) * decay_in).astype(BF16)
    grad_state = jnp.einsum("snd,sne->sde", query_in, grad_ret, preferred_element_type=F32)
    grad_out = mm_grad(gated, grad_mid_all).astype(BF16)
    grad_out = (
        grad_out.reshape(n_pb // heads_pb, -1, wide_rows, width)
        .swapaxes(0, 1)
        .reshape(value_width, width)
    )
    grad_gate_w = mm_grad(normed_one_all, grad_gate).astype(BF16)
    grad_carried = line_scan(
        grad_state,
        coef_backward,
        n_pb,
        False,
        order,
        7,
        grad_gate_w,
        grad_out,
    )
    grad_gate_w = scatter_line(grad_gate_w)
    grad_out = scatter_line(grad_out)
    grad_scores = (
        jnp.einsum("sne,sme->snm", grad_ret, value, preferred_element_type=F32) * decay
    ).astype(BF16)
    grad_query = jnp.einsum("snm,smd->snd", grad_scores, key, preferred_element_type=F32)
    grad_query = grad_query + decay_in * jnp.einsum(
        "sne,sde->snd", grad_ret, carried, preferred_element_type=F32
    )
    grad_key = jnp.einsum("snm,snd->smd", grad_scores, query, preferred_element_type=F32)
    grad_key = grad_key + decay_out * jnp.einsum(
        "sme,sde->smd", value, grad_carried, preferred_element_type=F32
    )
    grad_value = jnp.einsum("snm,sne->sme", scores, grad_ret, preferred_element_type=F32)
    grad_value = grad_value + decay_out * jnp.einsum(
        "smd,sde->sme", key, grad_carried, preferred_element_type=F32
    )
    grad_qkv = jnp.concatenate(
        [
            (turn_back(grad_query, tables_q) * scale).astype(BF16),
            turn_back(grad_key, tables_k).astype(BF16),
            grad_value.astype(BF16),
        ],
        axis=-1,
    )
    grad_qkv_w = mm_grad(normed_one_all, after(grad_qkv, grad_gate_w)).astype(BF16)
    grad_qkv_sum = scatter_line(grad_qkv_w)
    cut = (group, rows, -1)
    grad_inputs, output, back_up, back_gate = plane_last(
        (grad_qkv, weight_qkv, grad_gate, weight_gate),
        rows_in,
        grad_middle,
        (active, down_pack, middle),
        (grad_up.reshape(cut), grad_gate_w.reshape(cut)),
        order,
        8,
        grad_qkv_w,
    )
    if not order:
        output, grad_inputs = to_outer(output), to_outer(grad_inputs)

    shard_down = to_outer(grad_down[:, :width].astype(F32))
    shard_bias = grad_down[:, width].astype(F32)
    back, shard_out = to_owners(
        [grad_qkv_sum.reshape(cut)], 9, grad_inputs, line=line, traded=(grad_out,)
    )
    shard_out = to_outer(shard_out.astype(F32))
    shard_up = from_unit(back_up).astype(F32)
    shard_gate = from_head(back_gate).astype(F32)
    shard_query = from_head(back[..., :key_width]).astype(F32)
    shard_key = from_head(back[..., key_width : 2 * key_width]).astype(F32)
    shard_value = from_head(back[..., 2 * key_width :]).astype(F32)
    shards = (shard_query, shard_key, shard_value, shard_gate)
    shard_gain_one = sum(
        jnp.sum(low.astype(F32) * grad, axis=-1) for low, grad in zip(firsts, shards)
    )
    shard_gain_two = jnp.sum(up_low.astype(F32) * shard_up, axis=-1)
    shard_query, shard_key, shard_value, shard_gate = (gain_one * g for g in shards)
    return (
        output,
        grad_inputs,
        shard_gain_one,
        shard_query,
        shard_key,
        shard_value,
        shard_gate,
        shard_out,
        shard_gain_two,
        gain_two * shard_up,
        shard_bias,
        shard_down,
    )


def solution(mesh):
    dp, pb, ka = (mesh.shape[a] for a in ("dp", "pb", "ka"))
    fine = Mesh(mesh.devices.reshape(dp // 2, 2, pb, ka), ("dph", "dpl", "pb", "ka"))
    dp_axes = ("dph", "dpl")
    every = ("dph", "dpl", "pb", "ka")
    tokens = P(dp_axes, ("pb", "ka"), None)
    matrix = P(every, None)
    vector = P(every)
    return jax.shard_map(
        on_device,
        mesh=fine,
        in_specs=(
            tokens,
            tokens,
            P(dp_axes, None),
            vector,
            matrix,
            matrix,
            matrix,
            matrix,
            matrix,
            vector,
            matrix,
            vector,
            matrix,
        ),
        out_specs=(
            tokens,
            tokens,
            vector,
            matrix,
            matrix,
            matrix,
            matrix,
            matrix,
            vector,
            matrix,
            vector,
            matrix,
        ),
        check_vma=False,
    )
```

```python
import functools
import math

import jax
import jax.numpy as jnp
import numpy as np
from jax import lax
from jax.experimental import pallas as pl
from jax.experimental.pallas import tpu as pltpu
from jax.sharding import Mesh
from jax.sharding import PartitionSpec as P

H = 8
XPOS_BASE = 512.0
EPSILON = 1e-05
MESH = pl.DeviceIdType.MESH
F32 = jnp.float32
BF16 = jnp.bfloat16

PLANE = ("dpl", "ka")
LINE = ("dph", "pb")


def plane_ids():
    row = lax.axis_index("dpl")
    col = lax.axis_index("ka")
    other_row = 1 - row
    across = lax.rem(col + 2, 4)
    sibling = col + 1 - 2 * lax.rem(col, 2)
    return row, col, other_row, across, sibling


def greet(targets):
    barrier = pltpu.get_barrier_semaphore()
    for target in targets:
        pl.semaphore_signal(barrier, inc=1, device_id=target, device_id_type=MESH)
    pl.semaphore_wait(barrier, len(targets))


def gather_stages(shard, full, local_sem, send_sem, recv_sem, part=0, parts=1):
    batch, length, _ = shard.shape
    whole = length // parts
    first = part * whole
    half = whole // 2
    row, col, other_row, across, sibling = plane_ids()
    to_x = {"ka": across}
    to_y = {"dpl": other_row}
    to_s = {"ka": sibling}

    shard = shard.at[:, pl.ds(first, whole), :]

    def slot(r, c, start=0, size=whole):
        return full.at[pl.ds(r * batch, batch), pl.ds(c * length + first + start, size), :]

    def hop(index, target, dst, src=None):
        return pltpu.make_async_remote_copy(
            src_ref=dst if src is None else src,
            dst_ref=dst,
            send_sem=send_sem.at[part * 9 + index],
            recv_sem=recv_sem.at[part * 9 + index],
            device_id=target,
            device_id_type=MESH,
        )

    mine = pltpu.make_async_copy(shard, slot(row, col), local_sem.at[part])
    from_x = hop(0, to_x, slot(row, col), shard)
    from_y = hop(1, to_y, slot(row, col), shard)
    own_s = hop(2, to_s, slot(row, col), shard)
    diag_y = hop(3, to_y, slot(row, across, 0, half))
    relay_x = hop(4, to_s, slot(row, across))
    diag_x = hop(5, to_x, slot(other_row, col, half, half))
    relay_y = hop(6, to_s, slot(other_row, col))
    relay_a = hop(7, to_s, slot(other_row, across, 0, half))
    relay_b = hop(8, to_s, slot(other_row, across, half, half))

    def begin():
        from_x.start()
        from_y.start()
        own_s.start()
        mine.start()

    def relay():
        from_x.wait_recv()
        diag_y.start()
        relay_x.start()
        from_y.wait_recv()
        diag_x.start()
        relay_y.start()

    def diagonal():
        diag_y.wait_recv()
        relay_a.start()
        diag_x.wait_recv()
        relay_b.start()

    def end():
        for copy in (own_s, relay_x, relay_y, relay_a, relay_b):
            copy.wait_recv()
        for copy in (from_x, from_y, own_s, diag_y, relay_x, diag_x, relay_y, relay_a, relay_b):
            copy.wait_send()
        mine.wait()

    return (to_x, to_y, to_s), (begin, relay, diagonal, end)


GATHER_SCRATCH = (
    pltpu.SemaphoreType.DMA((2,)),
    pltpu.SemaphoreType.DMA((18,)),
    pltpu.SemaphoreType.DMA((18,)),
)


def gathered_shape(shard):
    batch, length, width = shard.shape
    return jax.ShapeDtypeStruct((2 * batch, 4 * length, width), shard.dtype)


def gather_kernel(shard, *refs):
    targets, stages = gather_stages(shard, *refs[-4:])
    greet(targets)
    for stage in stages:
        stage()


def read_rows(ref, b, at, order):
    if not order:
        return ref[b, at, :]
    size = ref.shape[-1] // len(order)
    return jnp.concatenate([ref[b, at, i * size : (i + 1) * size] for i in order], axis=-1)


def write_rows(ref, b, at, order, values):
    if not order:
        ref[b, at, :] = values
        return
    size = ref.shape[-1] // len(order)
    for j, i in enumerate(order):
        ref[b, at, i * size : (i + 1) * size] = values[:, j * size : (j + 1) * size]


def normalize_rows(source, target, order):
    batch, length, _ = source.shape
    step = 16

    def body(i, carry):
        at = pl.ds(i * step, step)
        for b in range(batch):
            normed, _ = normalize(read_rows(source, b, at, order).astype(F32))
            target[b, at, :] = normed.astype(BF16)
        return carry

    lax.fori_loop(0, length // step, body, 0)


def owners_stages(sources, targets, keep_sem, send_sem, recv_sem):
    row, col, other_row, _, _ = plane_ids()
    me = row * 4 + col
    peers = [(row, lax.rem(col + away, 4)) for away in (1, 2, 3)]
    peers += [(other_row, lax.rem(col + away, 4)) for away in (0, 1, 2, 3)]
    copies = []
    for a in range(len(sources)):
        copies.append(
            pltpu.make_async_copy(sources[a].at[me], targets[a].at[me], keep_sem.at[a])
        )
        for i in (6, 5, 4, 3, 2, 1, 0):
            r, c = peers[i]
            copies.append(
                pltpu.make_async_remote_copy(
                    src_ref=sources[a].at[r * 4 + c],
                    dst_ref=targets[a].at[me],
                    send_sem=send_sem.at[a, i],
                    recv_sem=recv_sem.at[a, i],
                    device_id={"dpl": r, "ka": c},
                    device_id_type=MESH,
                )
            )

    def begin():
        for copy in copies:
            copy.start()

    def end():
        for copy in copies:
            copy.wait()

    return [{"dpl": r, "ka": c} for r, c in peers], (begin, end)


def owners_scratch(count):
    return [
        pltpu.SemaphoreType.DMA((count,)),
        pltpu.SemaphoreType.DMA((count, 7)),
        pltpu.SemaphoreType.DMA((count, 7)),
    ]


def trade_stages(line, source, target, sems):
    place, col = lax.axis_index(line), lax.axis_index("ka")
    moves = place != col
    partner = {line: col, "ka": place}

    def trade():
        return pltpu.make_async_remote_copy(
            src_ref=source,
            dst_ref=target,
            send_sem=sems.at[0],
            recv_sem=sems.at[1],
            device_id=partner,
            device_id_type=MESH,
        )

    def keep():
        return pltpu.make_async_copy(source, target, sems.at[2])

    def greet_partner(barrier):
        @pl.when(moves)
        def _():
            pl.semaphore_signal(barrier, inc=1, device_id=partner, device_id_type=MESH)

        return moves.astype(jnp.int32)

    def begin():
        @pl.when(moves)
        def _():
            trade().start()

        @pl.when(jnp.logical_not(moves))
        def _():
            keep().start()

    def end():
        @pl.when(moves)
        def _():
            trade().wait()

        @pl.when(jnp.logical_not(moves))
        def _():
            keep().wait()

    return greet_partner, (begin, end)


TRADE_SCRATCH = (pltpu.SemaphoreType.DMA((3,)),)


def line_gather_stages(count, chunks, block, full, send_sem, recv_sem):
    here = lax.axis_index("pb")
    rows = block.shape[0]
    size = rows // chunks

    def hop(up, distance, c):
        owner = here - distance if up else here + distance
        place = full.at[pl.ds(owner * rows + c * size, size)]
        source = block.at[pl.ds(c * size, size)] if distance == 0 else place
        return pltpu.make_async_remote_copy(
            src_ref=source,
            dst_ref=place,
            send_sem=send_sem.at[int(up), distance, c],
            recv_sem=recv_sem.at[int(up), distance, c],
            device_id={"pb": here + 1 if up else here - 1},
            device_id_type=MESH,
        )

    def sends(up, distance):
        if up:
            return jnp.logical_and(here >= distance, here < count - 1)
        return jnp.logical_and(here + distance <= count - 1, here > 0)

    def arrives(up, distance):
        return here >= distance if up else here + distance <= count - 1

    def step(distance, c):
        for up in (True, False):
            if distance > 0:

                @pl.when(arrives(up, distance))
                def _():
                    hop(up, distance - 1, c).wait_recv()

            if distance < count - 1:

                @pl.when(sends(up, distance))
                def _():
                    hop(up, distance, c).start()

    def finish():
        for distance in range(count - 1):
            for c in range(chunks):
                for up in (True, False):

                    @pl.when(sends(up, distance))
                    def _():
                        hop(up, distance, c).wait_send()

    return step, finish


def open_kernel(
    count, chunks, order, moves, unit_moves, x, up, first, gate, out, down, bias, gain, *refs
):
    normed_all, up_mine, first_all, gate_out, down_pack, normed, up_low, down_low = refs[:8]
    sems = refs[8:]
    targets, owners = owners_stages((up_low if unit_moves else up,), (up_mine,), *sems[3:6])
    _, gather = gather_stages(normed, normed_all, *sems[:3])
    step, finish = line_gather_stages(count, chunks, first, first_all, *sems[6:8])
    here = lax.axis_index("pb")
    barrier = pltpu.get_barrier_semaphore()
    for target in targets:
        pl.semaphore_signal(barrier, inc=1, device_id=target, device_id_type=MESH)

    @pl.when(here > 0)
    def _():
        pl.semaphore_signal(barrier, inc=1, device_id={"pb": here - 1}, device_id_type=MESH)

    @pl.when(here < count - 1)
    def _():
        pl.semaphore_signal(barrier, inc=1, device_id={"pb": here + 1}, device_id_type=MESH)

    ends = (here > 0).astype(jnp.int32) + (here < count - 1).astype(jnp.int32)
    pl.semaphore_wait(barrier, len(targets) + ends)
    for c in range(chunks):
        step(0, c)
    normalize_rows(x, normed, order)
    gather[0]()
    for j, source, target, size in unit_moves:
        block = up[:, source : source + size].astype(BF16).astype(F32) * gain[...]
        up_low[j, :, target : target + size] = block.astype(BF16)
    owners[0]()
    height, lanes, wide = gate.shape[0], gate.shape[1], out.shape[0]
    for source, target, size in moves:
        down_low[:, target : target + size] = down[:, source : source + size].astype(BF16)
    down_low[:, down.shape[1] :] = jnp.broadcast_to(bias[...], (wide, 128)).astype(BF16)
    pairs = [
        (first, first_all.at[pl.ds(here * first.shape[0], first.shape[0])]),
        (gate, gate_out.at[pl.ds(0, height)]),
        (down_low, down_pack),
    ]
    for source, target, size in moves:
        pairs.append(
            (
                out.at[:, pl.ds(source, size)],
                gate_out.at[
                    pl.ds(height + target // lanes * wide, wide), pl.ds(target % lanes, size)
                ],
            )
        )
    copies = [pltpu.make_async_copy(a, b, sems[8].at[i]) for i, (a, b) in enumerate(pairs)]
    for copy in copies:
        copy.start()
    for c in range(chunks):
        step(1, c)
    gather[1]()
    for distance in range(2, count):
        for c in range(chunks):
            step(distance, c)
            if distance == 2 and c == chunks // 2:
                gather[2]()
    for copy in copies:
        copy.wait()
    gather[3]()
    owners[1]()
    finish()


def open_plane(x, up, first, gate, out, down, bias, gain, up_shape, order, moves, unit_moves, count, collective_id, *before):
    chunks = 4
    return pl.pallas_call(
        lambda *refs: open_kernel(
            count, chunks, order, moves, unit_moves, *refs[:8], *refs[8 + len(before) :]
        ),
        out_shape=[
            gathered_shape(x),
            jax.ShapeDtypeStruct(up_shape, BF16),
            jax.ShapeDtypeStruct((count * first.shape[0], first.shape[1]), BF16),
            jax.ShapeDtypeStruct((gate.shape[0] + out.size // gate.shape[1], gate.shape[1]), BF16),
            jax.ShapeDtypeStruct((down.shape[0], down.shape[1] + 128), BF16),
        ],
        in_specs=[VMEM, VMEM, ANY, ANY, ANY, VMEM, VMEM, VMEM] + [ANY] * len(before),
        out_specs=[ANY] * 5,
        scratch_shapes=[
            pltpu.VMEM(x.shape, BF16),
            pltpu.VMEM(up_shape, BF16),
            pltpu.VMEM((down.shape[0], down.shape[1] + 128), BF16),
            *GATHER_SCRATCH,
            *owners_scratch(1),
            pltpu.SemaphoreType.DMA((2, count, chunks)),
            pltpu.SemaphoreType.DMA((2, count, chunks)),
            pltpu.SemaphoreType.DMA((3 + len(moves),)),
        ],
        compiler_params=pltpu.CompilerParams(
            collective_id=collective_id,
            has_side_effects=True,
            vmem_limit_bytes=20 * 1024 * 1024,
        ),
        name="open_plane",
    )(x, up, first, gate, out, down, bias, gain, *before)


def scatter_stages(
    terms, finish, sent, own, sib, from_x, from_y, diag_a, diag_b, sems, recvs, even=False
):
    _, batch, length, width = own.shape
    half = length // 2
    row, col, other_row, across, sibling = plane_ids()
    across_s = lax.rem(sibling + 2, 4)
    to_x = {"ka": across}
    to_y = {"dpl": other_row}
    to_s = {"ka": sibling}
    mine = ((other_row, across), (row, across), (other_row, col), (row, col))
    theirs = ((other_row, across_s), (row, across_s), (other_row, sibling), (row, sibling))
    lower, upper = pl.ds(0, half), pl.ds(half, half)
    step = 16
    tile = 512

    def hop(src, dst, index, target):
        return pltpu.make_async_remote_copy(
            src_ref=src,
            dst_ref=dst,
            send_sem=sems.at[index],
            recv_sem=recvs.at[index],
            device_id=target,
            device_id_type=MESH,
        )

    swaps = [hop(sent.at[j], sib.at[j], j, to_s) for j in range(4)]
    first_a = hop(own.at[0, :, lower, :], diag_a, 4, to_x)
    first_b = hop(own.at[0, :, upper, :], diag_b, 5, to_y)
    x_lower = hop(own.at[1, :, lower, :], from_x.at[:, lower, :], 6, to_x)
    y_upper = hop(own.at[2, :, upper, :], from_y.at[:, upper, :], 7, to_y)
    x_upper = hop(own.at[1, :, upper, :], from_x.at[:, upper, :], 8, to_x)
    y_lower = hop(own.at[2, :, lower, :], from_y.at[:, lower, :], 9, to_y)

    def make(r, c, out):
        def body(n, carry):
            columns = pl.ds(pl.multiple_of(n * tile, tile), tile)
            value = 0.0
            for left, right, flipped in terms:
                block = left[pl.ds(r * batch, batch), pl.ds(c * length, length), :]
                block = block.reshape(batch * length, left.shape[2])
                if flipped:
                    value = value + lax.dot_general(
                        block,
                        right[columns, :],
                        (((1,), (1,)), ((), ())),
                        preferred_element_type=F32,
                    )
                else:
                    value = value + jnp.dot(
                        block, right[:, columns], preferred_element_type=F32
                    )
            out[:, :, columns] = value.reshape(batch, length, tile).astype(BF16)
            return carry

        lax.fori_loop(0, width // tile, body, 0)

    def give(j):
        make(*theirs[j], sent.at[j])
        swaps[j].start()

    def add(out_ref, out_start, parts, size):
        def body(i, carry):
            value = 0.0
            for ref, start in parts:
                value = value + ref[:, pl.ds(start + i * step, step), :].astype(F32)
            out_ref[:, pl.ds(out_start + i * step, step), :] = value.astype(out_ref.dtype)
            return carry

        lax.fori_loop(0, size // step, body, 0)

    def merge(j):
        swaps[j].wait_recv()
        add(own.at[j], 0, ((own.at[j], 0), (sib.at[j], 0)), length)

    def send_diag():
        merge(0)
        first_a.start()
        first_b.start()
        make(*mine[1], own.at[1])

    def send_x():
        merge(1)
        x_lower.start()
        make(*mine[2], own.at[2])

    def send_y():
        merge(2)
        if not even:
            y_upper.start()
        make(*mine[3], own.at[3])

    def stage_rest():
        if even:
            first_a.wait_recv()
            add(own.at[2], 0, ((own.at[2], 0), (diag_a, 0)), half)
            y_lower.start()
            y_upper.start()
        first_b.wait_recv()
        add(own.at[1], half, ((own.at[1], half), (diag_b, 0)), half)
        x_upper.start()
        if not even:
            first_a.wait_recv()
            add(own.at[2], 0, ((own.at[2], 0), (diag_a, 0)), half)
            y_lower.start()
        merge(3)

    def close(start):
        def body(i, carry):
            at = pl.ds(start + i * step, step)
            for b in range(batch):
                value = own[3, b, at, :].astype(F32)
                value = value + from_x[b, at, :].astype(F32) + from_y[b, at, :].astype(F32)
                finish(b, at, value)
            return carry

        lax.fori_loop(0, half // step, body, 0)

    def close_lower():
        x_lower.wait_recv()
        y_lower.wait_recv()
        close(0)

    def close_upper():
        y_upper.wait_recv()
        x_upper.wait_recv()
        close(half)
        for copy in (first_a, first_b, x_lower, x_upper, y_lower, y_upper):
            copy.wait_send()

    def stage_free():
        for copy in swaps:
            copy.wait_send()

    stages = (
        lambda: give(0),
        lambda: make(*mine[0], own.at[0]),
        lambda: give(1),
        send_diag,
        lambda: give(2),
        send_x,
        lambda: give(3),
        send_y,
        stage_rest,
        close_lower,
        close_upper,
        stage_free,
    )
    return (to_x, to_y, to_s), stages


def scatter_scratch(shape):
    batch, length, width = shape
    return [
        pltpu.VMEM((4,) + shape, BF16),
        pltpu.VMEM((4,) + shape, BF16),
        pltpu.VMEM((4,) + shape, BF16),
        pltpu.VMEM(shape, BF16),
        pltpu.VMEM(shape, BF16),
        pltpu.VMEM((batch, length // 2, width), BF16),
        pltpu.VMEM((batch, length // 2, width), BF16),
        pltpu.SemaphoreType.DMA((10,)),
        pltpu.SemaphoreType.DMA((10,)),
    ]


VMEM = pl.BlockSpec(memory_space=pltpu.VMEM)
ANY = pl.BlockSpec(memory_space=pl.ANY)


def mix_kernel(order, gated, weight, x, *refs):
    middle, normed_all, normed = refs[-15:-12]

    def finish(b, at, value):
        value = value + read_rows(x, b, at, order).astype(F32)
        middle[b, at, :] = value
        normed[b, at, :] = normalize(value)[0].astype(BF16)

    targets, stages = scatter_stages(((gated, weight, False),), finish, *refs[-12:-3], True)
    lower, upper = (gather_stages(normed, normed_all, *refs[-3:], i, 2)[1] for i in (0, 1))
    greet(targets)
    for stage in stages[:10] + lower[:1] + stages[10:11] + upper[:1]:
        stage()
    for pair in zip(lower[1:], upper[1:]):
        for stage in pair:
            stage()
    stages[11]()


def plane_mix(gated, weight, x, order, collective_id, *before):
    shape = x.shape
    return pl.pallas_call(
        functools.partial(mix_kernel, order),
        out_shape=[jax.ShapeDtypeStruct(shape, F32), gathered_shape(x)],
        in_specs=[VMEM] * 3 + [ANY] * len(before),
        out_specs=[VMEM, ANY],
        scratch_shapes=[
            pltpu.VMEM(shape, BF16),
            *scatter_scratch(shape),
            *GATHER_SCRATCH,
        ],
        compiler_params=pltpu.CompilerParams(
            collective_id=collective_id,
            has_side_effects=True,
            vmem_limit_bytes=48 * 1024 * 1024,
        ),
        name="plane_mix",
    )(gated, weight, x, *before)


def turn_kernel(order, grad, weight, middle, cot, *refs):
    grad_middle, grad_all, low = refs[-15:-12]

    def finish(b, at, value):
        normed, inv = normalize(middle[b, at, :])
        value = normalize_back(normed, inv, value)
        value = value + read_rows(cot, b, at, order).astype(F32)
        grad_middle[b, at, :] = value
        low[b, at, :] = value.astype(BF16)

    targets, stages = scatter_stages(((grad, weight, True),), finish, *refs[-12:-3], True)
    lower, upper = (gather_stages(low, grad_all, *refs[-3:], i, 2)[1] for i in (0, 1))
    greet(targets)
    for stage in stages[:10] + lower[:1] + stages[10:11] + upper[:1]:
        stage()
    for pair in zip(lower[1:], upper[1:]):
        for stage in pair:
            stage()
    stages[11]()


def plane_turn(grad, weight, middle, cot, order, collective_id, *before):
    shape = middle.shape
    return pl.pallas_call(
        functools.partial(turn_kernel, order),
        out_shape=[jax.ShapeDtypeStruct(shape, F32), gathered_shape(cot)],
        in_specs=[VMEM] * 4 + [ANY] * len(before),
        out_specs=[VMEM, ANY],
        scratch_shapes=[
            pltpu.VMEM(shape, BF16),
            *scatter_scratch(shape),
            *GATHER_SCRATCH,
        ],
        compiler_params=pltpu.CompilerParams(
            collective_id=collective_id,
            has_side_effects=True,
            vmem_limit_bytes=48 * 1024 * 1024,
        ),
        name="plane_turn",
    )(grad, weight, middle, cot, *before)


def put_back(landed, weight, gain, target, moves):
    total = 0.0
    for j, column, place, size in moves:
        value = landed[j, :, place : place + size].astype(F32)
        low = weight[:, column : column + size].astype(BF16).astype(F32)
        total = total + jnp.sum(low * value, axis=-1, keepdims=True)
        target[:, column : column + size] = gain[...] * value
    return total


def last_kernel(order, moves, *refs):
    grad_a, weight_a, grad_b, weight_b, x, grad_middle = refs[:6]
    owned, weights, gains = refs[6:8], refs[8:10], refs[10:12]
    grad_down = refs[12]
    scratch = refs[-14:]
    outs = refs[-20:-14]

    def finish(b, at, value):
        normed, inv = normalize(read_rows(x, b, at, order).astype(F32))
        value = grad_middle[b, at, :] + normalize_back(normed, inv, value)
        write_rows(outs[0], b, at, order, value)

    terms = ((grad_a, weight_a, True), (grad_b, weight_b, True))
    _, stages = scatter_stages(terms, finish, *scratch[:9])
    targets, owners = owners_stages(owned, scratch[9:11], *scratch[11:14])
    greet(targets)
    for stage in stages[:8] + owners[:1] + stages[8:9]:
        stage()
    size = outs[5].shape[1] // max(len(order), 1)
    for j, i in enumerate(order or (0,)):
        block = grad_down[:, j * size : (j + 1) * size]
        outs[5][:, i * size : (i + 1) * size] = block.astype(F32)
    for stage in stages[9:] + owners[1:]:
        stage()
    for i in (0, 1):
        if moves[i]:
            outs[3 + i][...] = put_back(scratch[9 + i], weights[i], gains[i], outs[1 + i], moves[i])
        else:
            outs[1 + i][...] = scratch[9 + i][...]
            outs[3 + i][...] = jnp.zeros(outs[3 + i].shape, F32)


def plane_last(
    terms, x, grad_middle, owned, weights, gains, grad_down, moves, order, collective_id, *before
):
    shape = x.shape
    column = jax.ShapeDtypeStruct(gains[0].shape, F32)
    plain = jax.ShapeDtypeStruct((grad_down.shape[0], shape[-1]), F32)
    return pl.pallas_call(
        functools.partial(last_kernel, order, moves),
        out_shape=[jax.ShapeDtypeStruct(shape, F32)]
        + [
            jax.ShapeDtypeStruct(w.shape, F32) if m else jax.ShapeDtypeStruct(o.shape, BF16)
            for o, w, m in zip(owned, weights, moves)
        ]
        + [column, column, plain],
        in_specs=[VMEM] * 6 + [ANY] * 2 + [VMEM] * 5 + [ANY] * len(before),
        out_specs=[VMEM] * 6,
        scratch_shapes=scatter_scratch(shape)
        + [pltpu.VMEM(o.shape, BF16) for o in owned]
        + owners_scratch(2),
        compiler_params=pltpu.CompilerParams(
            collective_id=collective_id,
            has_side_effects=True,
            vmem_limit_bytes=58 * 1024 * 1024,
        ),
        name="plane_last",
    )(*terms, x, grad_middle, *owned, *weights, *gains, grad_down, *before)


def scan_kernel(count, forward, cuts, gathers, order, state, coef, *refs):
    if gathers:
        moved = refs[0]
        total, result, message, landed, send_sem, recv_sem = refs[-11:-5]
        shard, shard_sem = refs[-5:-3]
        targets, stages = gather_stages(shard, result, *refs[-3:])
    else:
        left, right, middle = refs[:3]
        total, result, message, landed, send_sem, recv_sem = refs[-15:-9]

        def finish(b, at, value):
            write_rows(result, b, at, order, (middle[b, at, :] + value).astype(BF16))

        targets, stages = scatter_stages(((left, right, False),), finish, *refs[-9:])
    here = lax.axis_index("pb")
    place = here if forward else count - 1 - here
    step = 1 if forward else -1
    has_prev = place > 0
    has_next = place < count - 1
    barrier = pltpu.get_barrier_semaphore()

    @pl.when(has_prev)
    def _():
        pl.semaphore_signal(barrier, inc=1, device_id={"pb": here - step}, device_id_type=MESH)

    @pl.when(has_next)
    def _():
        pl.semaphore_signal(barrier, inc=1, device_id={"pb": here + step}, device_id_type=MESH)

    greeted = has_prev.astype(jnp.int32) + has_next.astype(jnp.int32)
    for target in targets:
        pl.semaphore_signal(barrier, inc=1, device_id=target, device_id_type=MESH)
    pl.semaphore_wait(barrier, greeted + len(targets))

    height = state.shape[1] // cuts
    pieces = [(s, c) for s in range(state.shape[0]) for c in range(cuts)]

    def hop(i):
        s, c = pieces[i]
        rows = pl.ds(c * height, height)
        return pltpu.make_async_remote_copy(
            src_ref=message.at[s, rows],
            dst_ref=landed.at[s, rows],
            send_sem=send_sem.at[i],
            recv_sem=recv_sem.at[i],
            device_id={"pb": here + step},
            device_id_type=MESH,
        )

    def emit(i):
        s, c = pieces[i]
        rows = pl.ds(c * height, height)

        @pl.when(jnp.logical_not(has_prev))
        def _():
            message[s, rows] = state[s, rows].astype(BF16)
            hop(i).start()
            total[s, rows] = jnp.zeros((height, state.shape[2]), BF16)

        @pl.when(has_prev)
        def _():
            hop(i).wait_recv()
            total[s, rows] = (coef[0, s] * landed[s, rows].astype(F32)).astype(BF16)

            @pl.when(has_next)
            def _():
                message[s, rows] = (
                    state[s, rows] + coef[1, s] * total[s, rows].astype(F32)
                ).astype(BF16)
                hop(i).start()

    emit(0)
    if gathers:
        size = shard.shape[-1] // max(len(order), 1)
        for move in (0, 1):
            for j, i in enumerate(order or (0,)):
                copy = pltpu.make_async_copy(
                    moved.at[:, :, pl.ds(i * size, size)],
                    shard.at[:, :, pl.ds(j * size, size)],
                    shard_sem.at[j],
                )
                if move:
                    copy.wait()
                else:
                    copy.start()
        stages[0]()
    count = len(pieces)
    places = {count // 2: 1, 3 * count // 4: 2} if gathers else {i + 1: i for i in range(8)}
    if not gathers:
        places[3 * count // 4] = 8
    for i in range(1, count):
        emit(i)
        if i in places:
            stages[places[i]]()
    for stage in stages[max(places.values()) + 1 :]:
        stage()

    @pl.when(has_next)
    def _():
        for i in range(len(pieces)):
            hop(i).wait_send()


def line_scan(state, coef, count, forward, order, collective_id, *before, gathered=None, summed=()):
    cuts = 4
    pieces = state.shape[0] * cuts
    scratch = [
        pltpu.VMEM(state.shape, BF16),
        pltpu.VMEM(state.shape, BF16),
        pltpu.SemaphoreType.DMA((pieces,)),
        pltpu.SemaphoreType.DMA((pieces,)),
    ]
    gathers = gathered is not None
    if gathers:
        operands, specs = (gathered,), [ANY]
        result, spec = gathered_shape(gathered), ANY
        scratch += [
            pltpu.VMEM(gathered.shape, gathered.dtype),
            pltpu.SemaphoreType.DMA((max(len(order), 1),)),
            *GATHER_SCRATCH,
        ]
    else:
        operands, specs = summed, [VMEM] * 3
        result, spec = jax.ShapeDtypeStruct(summed[2].shape, BF16), VMEM
        scratch += scatter_scratch(summed[2].shape)
    return pl.pallas_call(
        functools.partial(scan_kernel, count, forward, cuts, gathers, order),
        out_shape=[jax.ShapeDtypeStruct(state.shape, BF16), result],
        in_specs=[VMEM, pl.BlockSpec(memory_space=pltpu.SMEM)] + specs + [ANY] * len(before),
        out_specs=[VMEM, spec],
        scratch_shapes=scratch,
        compiler_params=pltpu.CompilerParams(
            collective_id=collective_id,
            has_side_effects=True,
            vmem_limit_bytes=48 * 1024 * 1024,
        ),
        name="line_scan",
    )(state, coef, *operands, *before)


def spread_kernel(line, moves, *refs):
    weights, gain, out, docs = refs[:4], refs[4], refs[5], refs[6]
    qkv_mine, gate_mine, out_mine, docs_all, qkv_pack, gate_pack, out_low = refs[-13:-6]
    scratch = refs[-6:]
    row, _, other_row, _, _ = plane_ids()
    targets, stages = owners_stages((qkv_pack, gate_pack), (qkv_mine, gate_mine), *scratch[:3])
    greet_partner, trade = trade_stages(line, out_low, out_mine, scratch[3])
    barrier = pltpu.get_barrier_semaphore()
    for target in targets:
        pl.semaphore_signal(barrier, inc=1, device_id=target, device_id_type=MESH)
    greeted = greet_partner(barrier) + len(targets)
    for i, blocks in enumerate(moves):
        for j, column, place, size in blocks:
            block = weights[i][:, column : column + size].astype(BF16).astype(F32) * gain[...]
            pack = qkv_pack if i < 3 else gate_pack
            pack[j, :, place : place + size] = block.astype(BF16)
    pl.semaphore_wait(barrier, greeted)
    stages[0]()
    give = pltpu.make_async_remote_copy(
        src_ref=docs,
        dst_ref=docs_all.at[row],
        send_sem=scratch[4].at[0],
        recv_sem=scratch[4].at[1],
        device_id={"dpl": other_row},
        device_id_type=MESH,
    )
    keep = pltpu.make_async_copy(docs, docs_all.at[row], scratch[4].at[2])
    give.start()
    keep.start()
    out_low[...] = out[...].astype(BF16)
    trade[0]()
    trade[1]()
    give.wait()
    keep.wait()
    stages[1]()


def plane_spread(weights, gain, out, docs, line, moves, group, collective_id):
    rows = gain.shape[0]
    first = sum(w.shape[1] for w in weights[:3]) // group
    gate = weights[3].shape[1] // group
    shapes = [
        jax.ShapeDtypeStruct((group, rows, first), BF16),
        jax.ShapeDtypeStruct((group, rows, gate), BF16),
        jax.ShapeDtypeStruct(out.shape, BF16),
    ]
    return pl.pallas_call(
        functools.partial(spread_kernel, line, moves),
        out_shape=shapes + [jax.ShapeDtypeStruct((2,) + docs.shape, docs.dtype)],
        in_specs=[VMEM] * 7,
        out_specs=[ANY] * 4,
        scratch_shapes=[pltpu.VMEM(shape.shape, BF16) for shape in shapes]
        + owners_scratch(2)
        + list(TRADE_SCRATCH)
        + [pltpu.SemaphoreType.DMA((3,)), pltpu.SemaphoreType.DMA((1,))],
        compiler_params=pltpu.CompilerParams(
            collective_id=collective_id,
            has_side_effects=True,
            vmem_limit_bytes=20 * 1024 * 1024,
        ),
        name="plane_spread",
    )(*weights, gain, out, docs)


def final_kernel(line, order, moves, grad, grad_out, *refs):
    weights, gain = refs[:3], refs[3]
    outs, out_out, sums, landed, out_landed = refs[-11:-8], refs[-8], refs[-7], refs[-6], refs[-5]
    targets, stages = owners_stages((grad,), (landed,), *refs[-4:-1])
    greet_partner, trade = trade_stages(line, grad_out, out_landed, refs[-1])
    barrier = pltpu.get_barrier_semaphore()
    for target in targets:
        pl.semaphore_signal(barrier, inc=1, device_id=target, device_id_type=MESH)
    pl.semaphore_wait(barrier, greet_partner(barrier) + len(targets))
    stages[0]()
    for stage in trade:
        stage()
    size = out_out.shape[1] // max(len(order), 1)
    for j, i in enumerate(order or (0,)):
        block = out_landed[:, j * size : (j + 1) * size]
        out_out[:, i * size : (i + 1) * size] = block.astype(F32)
    stages[1]()
    total = 0.0
    for weight, target, blocks in zip(weights, outs, moves):
        total = total + put_back(landed, weight, gain, target, blocks)
    sums[...] = total


def plane_final(grad, grad_out, weights, gain, line, order, moves, collective_id, *before):
    return pl.pallas_call(
        functools.partial(final_kernel, line, order, moves),
        out_shape=[jax.ShapeDtypeStruct(w.shape, F32) for w in weights]
        + [
            jax.ShapeDtypeStruct(grad_out.shape, F32),
            jax.ShapeDtypeStruct(gain.shape, F32),
        ],
        in_specs=[ANY] * 2 + [VMEM] * 4 + [ANY] * len(before),
        out_specs=[VMEM] * 5,
        scratch_shapes=[pltpu.VMEM(grad.shape, BF16), pltpu.VMEM(grad_out.shape, BF16)]
        + owners_scratch(1)
        + list(TRADE_SCRATCH),
        compiler_params=pltpu.CompilerParams(
            collective_id=collective_id,
            has_side_effects=True,
            vmem_limit_bytes=20 * 1024 * 1024,
        ),
        name="plane_final",
    )(grad, grad_out, *weights, gain, *before)


def normalize(values):
    mean = jnp.mean(values, axis=-1, keepdims=True)
    centered = values - mean
    inv = lax.rsqrt(jnp.mean(centered * centered, axis=-1, keepdims=True) + EPSILON)
    return centered * inv, inv


def normalize_back(normed, inv, grad):
    mean = jnp.mean(grad, axis=-1, keepdims=True)
    along = jnp.mean(grad * normed, axis=-1, keepdims=True)
    return inv * (grad - mean - normed * along)


def turn_tables(positions, half, direction):
    pair = jnp.arange(half, dtype=F32)
    frequency = jnp.exp(-jnp.log(10000.0) * pair / half)
    zeta = (pair / half + 0.4) / 1.4
    angles = positions[:, None] * frequency[None, :]
    factor = jnp.exp(direction * positions[:, None] / XPOS_BASE * jnp.log(zeta)[None, :])
    return jnp.cos(angles) * factor, jnp.sin(angles) * factor


def turn(values, tables):
    cosine, sine = tables
    half = values.shape[-1] // 2
    first, second = values[..., :half], values[..., half:]
    return jnp.concatenate(
        [first * cosine - second * sine, second * cosine + first * sine], axis=-1
    )


def turn_back(values, tables):
    cosine, sine = tables
    return turn(values, (cosine, -sine))


def mm(left, right):
    return jnp.einsum("sti,io->sto", left, right, preferred_element_type=F32)


def mm_back(left, right):
    return jnp.einsum("sto,io->sti", left, right, preferred_element_type=F32)


def mm_grad(left, right):
    return jnp.einsum("sti,sto->io", left, right, preferred_element_type=F32)


def after(value, *others):
    for other in others:
        value = value + (0.0 * other[(0,) * other.ndim].astype(F32)).astype(value.dtype)
    return value


def on_device(
    inputs,
    out_cotangent,
    doc_lengths,
    ln1_gain,
    w_query,
    w_key,
    w_value,
    w_gate,
    w_out,
    ln2_gain,
    w_up,
    up_bias,
    w_down,
):
    n_dph, n_dpl, n_pb, n_ka = (lax.axis_size(a) for a in ("dph", "dpl", "pb", "ka"))
    at_dpl, at_pb, at_ka = (lax.axis_index(a) for a in ("dpl", "pb", "ka"))
    batch, length, width = inputs.shape
    span = n_ka * length
    rows = w_query.shape[0]
    wide_rows = w_down.shape[0]
    key_width = w_query.shape[1] // H
    value_width = w_value.shape[1] // H
    units = n_dph * n_pb * wide_rows
    group = n_dpl * n_ka
    heads_pb = H // (n_dpl * n_dph)

    chunk = n_ka * rows

    def pick(values, order):
        return jnp.concatenate(
            [values[..., i * chunk : (i + 1) * chunk] for i in order], axis=-1
        )

    inner = [
        (d * n_dpl + r) * n_pb + p
        for d in range(n_dph)
        for p in range(n_pb)
        for r in range(n_dpl)
    ]

    def to_inner(values):
        return pick(values, inner)

    def to_outer(values):
        return pick(values, [inner.index(i) for i in range(len(inner))])

    def by_unit(weight):
        cut = weight.reshape(rows, n_dph, n_dpl, n_pb, n_ka, wide_rows)
        return jnp.transpose(cut, (2, 4, 0, 1, 3, 5)).reshape(group, rows, units)

    def from_unit(values):
        cut = values.reshape(n_dpl, n_ka, rows, n_dph, n_pb, wide_rows)
        return jnp.transpose(cut, (2, 3, 0, 4, 1, 5)).reshape(rows, -1)

    def gather_line(values):
        return lax.all_gather(values, LINE, axis=0, tiled=True)

    def scatter_line(values):
        return lax.psum_scatter(values, LINE, scatter_dimension=0, tiled=True)

    line = "dph" if n_dph > 1 else "pb"

    gain_one = ln1_gain.astype(BF16).astype(F32)[:, None]
    gain_two = ln2_gain.astype(BF16).astype(F32)[:, None]
    firsts = (w_query, w_key, w_value, w_gate)

    def head_of(j):
        r, c = j // n_ka, j % n_ka
        return (c // heads_pb) * (n_dpl * heads_pb) + r * heads_pb + c % heads_pb

    head_moves = [
        [(j, head_of(j) * size, place, size) for j in range(group)]
        for size, place in (
            (key_width, 0),
            (key_width, key_width),
            (value_width, 2 * key_width),
            (value_width, 0),
        )
    ]
    docs = jnp.pad(doc_lengths, ((0, 8 - batch), (0, 128 - doc_lengths.shape[1])))
    qkv_swapped, gate_swapped, out_moved, docs_all = plane_spread(
        firsts, gain_one, w_out, docs, line, head_moves, group, 0
    )
    order = tuple(inner) if chunk % 128 == 0 else ()
    rows_in, rows_cot = inputs, out_cotangent
    if not order:
        rows_in, rows_cot = to_inner(inputs), to_inner(out_cotangent)
    head = (
        (at_ka // heads_pb) * (n_dpl * heads_pb) + at_dpl * heads_pb + at_ka % heads_pb
    ).astype(F32)
    log_gamma = jnp.log(1.0 - jnp.exp2(-5.0 - head))
    offsets = jnp.arange(span, dtype=jnp.int32)
    places = (at_pb * span + offsets).astype(F32)
    tables_q = turn_tables(places, key_width // 2, 1.0)
    tables_k = turn_tables(places, key_width // 2, -1.0)
    distance = offsets[:, None] - offsets[None, :]
    decay = jnp.where(
        distance >= 0, jnp.exp(jnp.maximum(distance, 0).astype(F32) * log_gamma), 0.0
    )
    decay_in = jnp.exp(offsets.astype(F32) * log_gamma)[:, None]
    decay_out = jnp.exp((span - offsets).astype(F32) * log_gamma)[:, None]
    decay_span = jnp.exp(span * log_gamma)
    lengths = docs_all[:, :batch, : doc_lengths.shape[1]].reshape(n_dpl * batch, -1)
    ends = jnp.cumsum(lengths, axis=-1)
    edge = at_pb * span

    def goes_on(start):
        return jnp.all(ends != start, axis=-1).astype(F32)

    coef_forward = jnp.stack([goes_on(edge), jnp.full((n_dpl * batch,), decay_span)])
    coef_backward = jnp.stack([goes_on(edge + span), jnp.full((n_dpl * batch,), decay_span)])

    down_in, up_in, unit_moves = w_down, w_up, []
    if order:
        moves = [(i * chunk, j * chunk, chunk) for j, i in enumerate(order)]
        for j in range(group):
            for q in range(n_dph * n_pb):
                block = (q // n_pb * n_dpl + j // n_ka) * n_pb + q % n_pb
                column = (block * n_ka + j % n_ka) * wide_rows
                unit_moves.append((j, column, q * wide_rows, wide_rows))
    else:
        moves = [(i * units, i * units, units) for i in range(width // units)]
        out_moved, down_in = to_inner(out_moved), to_inner(w_down)
        up_in = by_unit((w_up.astype(BF16).astype(F32) * gain_two).astype(BF16))
    normed_one_all, up_swapped, weight_qkv, gate_out, down_pack = open_plane(
        rows_in,
        up_in,
        qkv_swapped.reshape(group * rows, -1),
        gate_swapped.reshape(group * rows, -1),
        out_moved,
        down_in,
        up_bias[:, None],
        gain_two,
        (group, rows, units),
        order,
        moves,
        unit_moves,
        n_pb,
        1,
    )
    if n_dph > 1:
        weight_qkv = lax.all_gather(weight_qkv, "dph", axis=0, tiled=True)
    blocks = width // units
    gate_out = gather_line(gate_out)
    first = mm(normed_one_all, weight_qkv)
    query_pre = first[..., :key_width]
    key_pre = first[..., key_width : 2 * key_width]
    value = first[..., 2 * key_width :].astype(BF16)
    scale = key_width ** (-0.5)
    query = (turn(query_pre, tables_q) * scale).astype(BF16)
    key = turn(key_pre, tables_k).astype(BF16)
    key_out = (key.astype(F32) * decay_out).astype(BF16)
    state = jnp.einsum("smd,sme->sde", key_out, value, preferred_element_type=F32)
    carried, cot_all = line_scan(
        state, coef_forward, n_pb, True, order, 2, gathered=rows_cot
    )
    raw = jnp.einsum("snd,smd->snm", query, key, preferred_element_type=F32)
    scores = (raw * decay).astype(BF16)
    retained = jnp.einsum("snm,sme->sne", scores, value, preferred_element_type=F32)
    retained = retained + decay_in * jnp.einsum(
        "snd,sde->sne", query, carried, preferred_element_type=F32
    )
    gate_out = after(gate_out, retained).reshape(n_dph * n_pb, -1, units)
    weight_gate = gate_out[:, : group * rows].reshape(width, units)
    weight_out = (
        gate_out[:, group * rows :]
        .reshape(-1, n_pb // heads_pb, blocks, wide_rows, units)
        .transpose(1, 0, 3, 2, 4)
        .reshape(value_width, width)
    )
    weight_up = gather_line(after(up_swapped.reshape(group * rows, -1), gate_out))
    down_pack = gather_line(after(down_pack, gate_out))
    weight_down = down_pack[:, :width]
    bias_up = down_pack[:, width].astype(F32)
    normed_ret, inv_ret = normalize(retained)
    gate = mm(normed_one_all, weight_gate)
    opened = jax.nn.sigmoid(gate)
    silu = gate * opened
    gated = (silu * normed_ret).astype(BF16)
    middle, normed_two_all = plane_mix(gated, weight_out, rows_in, order, 3)
    up_pre = mm(normed_two_all, weight_up) + bias_up
    bell = 0.5 * (1.0 + lax.erf(up_pre * np.float32(math.sqrt(0.5))))
    active = (up_pre * bell).astype(BF16)

    slope = bell + up_pre * (
        jnp.exp(-0.5 * up_pre * up_pre) * np.float32(1.0 / math.sqrt(2.0 * math.pi))
    )
    grad_up_pre = (mm_back(cot_all, weight_down) * slope).astype(BF16)
    ones = jnp.ones((n_dpl * batch, span, 128), BF16)
    grad_down = jnp.concatenate(
        [mm_grad(active, cot_all).astype(BF16), mm_grad(grad_up_pre, ones).astype(BF16)], axis=-1
    )
    grad_up = mm_grad(normed_two_all, grad_up_pre).astype(BF16)
    grad_middle, grad_mid_all = plane_turn(
        grad_up_pre, weight_up, middle, rows_cot, order, 5, grad_down, grad_up
    )
    grad_down = scatter_line(grad_down)
    grad_up = scatter_line(grad_up)
    grad_gated = after(mm_back(grad_mid_all, weight_out), grad_up, grad_down)
    grad_gate = (grad_gated * normed_ret * (opened + silu * (1.0 - opened))).astype(BF16)
    grad_ret = normalize_back(normed_ret, inv_ret, grad_gated * silu).astype(BF16)
    query_in = (query.astype(F32) * decay_in).astype(BF16)
    grad_state = jnp.einsum("snd,sne->sde", query_in, grad_ret, preferred_element_type=F32)
    grad_out = mm_grad(gated, grad_mid_all).astype(BF16)
    grad_out = (
        grad_out.reshape(n_pb // heads_pb, -1, wide_rows, width)
        .swapaxes(0, 1)
        .reshape(value_width, width)
    )
    grad_gate_w = mm_grad(normed_one_all, grad_gate).astype(BF16)
    grad_carried, output = line_scan(
        grad_state,
        coef_backward,
        n_pb,
        False,
        order,
        7,
        grad_gate_w,
        grad_out,
        summed=(active, down_pack, middle),
    )
    grad_gate_w = scatter_line(grad_gate_w)
    grad_out = scatter_line(grad_out)
    grad_scores = (
        jnp.einsum("sne,sme->snm", grad_ret, value, preferred_element_type=F32) * decay
    ).astype(BF16)
    grad_query = jnp.einsum("snm,smd->snd", grad_scores, key, preferred_element_type=F32)
    grad_query = grad_query + decay_in * jnp.einsum(
        "sne,sde->snd", grad_ret, carried, preferred_element_type=F32
    )
    grad_key = jnp.einsum("snm,snd->smd", grad_scores, query, preferred_element_type=F32)
    grad_key = grad_key + decay_out * jnp.einsum(
        "sme,sde->smd", value, grad_carried, preferred_element_type=F32
    )
    grad_value = jnp.einsum("snm,sne->sme", scores, grad_ret, preferred_element_type=F32)
    grad_value = grad_value + decay_out * jnp.einsum(
        "smd,sde->sme", key, grad_carried, preferred_element_type=F32
    )
    grad_qkv = jnp.concatenate(
        [
            (turn_back(grad_query, tables_q) * scale).astype(BF16),
            turn_back(grad_key, tables_k).astype(BF16),
            grad_value.astype(BF16),
        ],
        axis=-1,
    )
    grad_qkv_w = mm_grad(normed_one_all, after(grad_qkv, grad_gate_w)).astype(BF16)
    grad_qkv_sum = scatter_line(grad_qkv_w)
    cut = (group, rows, -1)
    grad_inputs, shard_gate, shard_up, sums_gate, sums_up, shard_down = plane_last(
        (grad_qkv, weight_qkv, grad_gate, weight_gate),
        rows_in,
        grad_middle,
        (grad_gate_w.reshape(cut), grad_up.reshape(cut)),
        (w_gate, w_up),
        (gain_one, gain_two),
        grad_down,
        (head_moves[3], unit_moves),
        order,
        8,
        grad_qkv_w,
    )
    if not order:
        output, grad_inputs = to_outer(output), to_outer(grad_inputs)
        shard_up = from_unit(shard_up).astype(F32)
        sums_up = jnp.sum(w_up.astype(BF16).astype(F32) * shard_up, axis=-1, keepdims=True)
        shard_up = gain_two * shard_up

    shard_query, shard_key, shard_value, shard_out, sums_qkv = plane_final(
        grad_qkv_sum.reshape(cut),
        grad_out,
        firsts[:3],
        gain_one,
        line,
        order,
        head_moves[:3],
        9,
        grad_inputs,
    )
    if not order:
        shard_out, shard_down = to_outer(shard_out), to_outer(shard_down)
    shard_bias = grad_down[:, width].astype(F32)
    return (
        output,
        grad_inputs,
        (sums_qkv + sums_gate)[:, 0],
        shard_query,
        shard_key,
        shard_value,
        shard_gate,
        shard_out,
        sums_up[:, 0],
        shard_up,
        shard_bias,
        shard_down,
    )


def solution(mesh):
    dp, pb, ka = (mesh.shape[a] for a in ("dp", "pb", "ka"))
    fine = Mesh(mesh.devices.reshape(dp // 2, 2, pb, ka), ("dph", "dpl", "pb", "ka"))
    dp_axes = ("dph", "dpl")
    every = ("dph", "dpl", "pb", "ka")
    tokens = P(dp_axes, ("pb", "ka"), None)
    matrix = P(every, None)
    vector = P(every)
    return jax.shard_map(
        on_device,
        mesh=fine,
        in_specs=(
            tokens,
            tokens,
            P(dp_axes, None),
            vector,
            matrix,
            matrix,
            matrix,
            matrix,
            matrix,
            vector,
            matrix,
            vector,
            matrix,
        ),
        out_specs=(
            tokens,
            tokens,
            vector,
            matrix,
            matrix,
            matrix,
            matrix,
            matrix,
            vector,
            matrix,
            vector,
            matrix,
        ),
        check_vma=False,
    )
```

```python
import functools
import math

import jax
import jax.numpy as jnp
import numpy as np
from jax import lax
from jax.experimental import pallas as pl
from jax.experimental.pallas import tpu as pltpu
from jax.sharding import Mesh
from jax.sharding import PartitionSpec as P

H = 8
XPOS_BASE = 512.0
EPSILON = 1e-05
MESH = pl.DeviceIdType.MESH
F32 = jnp.float32
BF16 = jnp.bfloat16

PLANE = ("dpl", "ka")
LINE = ("dph", "pb")


def plane_ids():
    row = lax.axis_index("dpl")
    col = lax.axis_index("ka")
    other_row = 1 - row
    across = lax.rem(col + 2, 4)
    sibling = col + 1 - 2 * lax.rem(col, 2)
    return row, col, other_row, across, sibling


def greet(targets):
    barrier = pltpu.get_barrier_semaphore()
    for target in targets:
        pl.semaphore_signal(barrier, inc=1, device_id=target, device_id_type=MESH)
    pl.semaphore_wait(barrier, len(targets))


def gather_stages(shard, full, local_sem, send_sem, recv_sem, part=0, parts=1):
    batch, length, _ = shard.shape
    whole = length // parts
    first = part * whole
    half = whole // 2
    row, col, other_row, across, sibling = plane_ids()
    to_x = {"ka": across}
    to_y = {"dpl": other_row}
    to_s = {"ka": sibling}

    shard = shard.at[:, pl.ds(first, whole), :]

    def slot(r, c, start=0, size=whole):
        return full.at[pl.ds(r * batch, batch), pl.ds(c * length + first + start, size), :]

    def hop(index, target, dst, src=None):
        return pltpu.make_async_remote_copy(
            src_ref=dst if src is None else src,
            dst_ref=dst,
            send_sem=send_sem.at[part * 9 + index],
            recv_sem=recv_sem.at[part * 9 + index],
            device_id=target,
            device_id_type=MESH,
        )

    mine = pltpu.make_async_copy(shard, slot(row, col), local_sem.at[part])
    from_x = hop(0, to_x, slot(row, col), shard)
    from_y = hop(1, to_y, slot(row, col), shard)
    own_s = hop(2, to_s, slot(row, col), shard)
    diag_y = hop(3, to_y, slot(row, across, 0, half))
    relay_x = hop(4, to_s, slot(row, across))
    diag_x = hop(5, to_x, slot(other_row, col, half, half))
    relay_y = hop(6, to_s, slot(other_row, col))
    relay_a = hop(7, to_s, slot(other_row, across, 0, half))
    relay_b = hop(8, to_s, slot(other_row, across, half, half))

    def begin():
        from_x.start()
        from_y.start()
        own_s.start()
        mine.start()

    def relay():
        from_x.wait_recv()
        diag_y.start()
        relay_x.start()
        from_y.wait_recv()
        diag_x.start()
        relay_y.start()

    def diagonal():
        diag_y.wait_recv()
        relay_a.start()
        diag_x.wait_recv()
        relay_b.start()

    def end():
        for copy in (own_s, relay_x, relay_y, relay_a, relay_b):
            copy.wait_recv()
        for copy in (from_x, from_y, own_s, diag_y, relay_x, diag_x, relay_y, relay_a, relay_b):
            copy.wait_send()
        mine.wait()

    return (to_x, to_y, to_s), (begin, relay, diagonal, end)


GATHER_SCRATCH = (
    pltpu.SemaphoreType.DMA((2,)),
    pltpu.SemaphoreType.DMA((18,)),
    pltpu.SemaphoreType.DMA((18,)),
)


def gathered_shape(shard):
    batch, length, width = shard.shape
    return jax.ShapeDtypeStruct((2 * batch, 4 * length, width), shard.dtype)


def gather_kernel(shard, *refs):
    targets, stages = gather_stages(shard, *refs[-4:])
    greet(targets)
    for stage in stages:
        stage()


def read_rows(ref, b, at, order):
    if not order:
        return ref[b, at, :]
    size = ref.shape[-1] // len(order)
    return jnp.concatenate([ref[b, at, i * size : (i + 1) * size] for i in order], axis=-1)


def write_rows(ref, b, at, order, values):
    if not order:
        ref[b, at, :] = values
        return
    size = ref.shape[-1] // len(order)
    for j, i in enumerate(order):
        ref[b, at, i * size : (i + 1) * size] = values[:, j * size : (j + 1) * size]


def normalize_rows(source, target, order):
    batch, length, _ = source.shape
    step = 16

    def body(i, carry):
        at = pl.ds(i * step, step)
        for b in range(batch):
            normed, _ = normalize(read_rows(source, b, at, order).astype(F32))
            target[b, at, :] = normed.astype(BF16)
        return carry

    lax.fori_loop(0, length // step, body, 0)


def owners_stages(sources, targets, keep_sem, send_sem, recv_sem):
    row, col, other_row, _, _ = plane_ids()
    me = row * 4 + col
    peers = [(row, lax.rem(col + away, 4)) for away in (1, 2, 3)]
    peers += [(other_row, lax.rem(col + away, 4)) for away in (0, 1, 2, 3)]
    copies = []
    for a in range(len(sources)):
        copies.append(
            pltpu.make_async_copy(sources[a].at[me], targets[a](me), keep_sem.at[a])
        )
        for i in (6, 5, 4, 3, 2, 1, 0):
            r, c = peers[i]
            copies.append(
                pltpu.make_async_remote_copy(
                    src_ref=sources[a].at[r * 4 + c],
                    dst_ref=targets[a](me),
                    send_sem=send_sem.at[a, i],
                    recv_sem=recv_sem.at[a, i],
                    device_id={"dpl": r, "ka": c},
                    device_id_type=MESH,
                )
            )

    def begin():
        for copy in copies:
            copy.start()

    def end():
        for copy in copies:
            copy.wait()

    return [{"dpl": r, "ka": c} for r, c in peers], (begin, end)


def blocks_of(ref):
    return lambda j: ref.at[j]


def owners_scratch(count):
    return [
        pltpu.SemaphoreType.DMA((count,)),
        pltpu.SemaphoreType.DMA((count, 7)),
        pltpu.SemaphoreType.DMA((count, 7)),
    ]


def trade_stages(line, source, target, sems):
    place, col = lax.axis_index(line), lax.axis_index("ka")
    moves = place != col
    partner = {line: col, "ka": place}

    def trade():
        return pltpu.make_async_remote_copy(
            src_ref=source,
            dst_ref=target,
            send_sem=sems.at[0],
            recv_sem=sems.at[1],
            device_id=partner,
            device_id_type=MESH,
        )

    def keep():
        return pltpu.make_async_copy(source, target, sems.at[2])

    def greet_partner(barrier):
        @pl.when(moves)
        def _():
            pl.semaphore_signal(barrier, inc=1, device_id=partner, device_id_type=MESH)

        return moves.astype(jnp.int32)

    def begin():
        @pl.when(moves)
        def _():
            trade().start()

        @pl.when(jnp.logical_not(moves))
        def _():
            keep().start()

    def end():
        @pl.when(moves)
        def _():
            trade().wait()

        @pl.when(jnp.logical_not(moves))
        def _():
            keep().wait()

    return greet_partner, (begin, end)


TRADE_SCRATCH = (pltpu.SemaphoreType.DMA((3,)),)


def line_gather_stages(count, chunks, full, send_sem, recv_sem):
    here = lax.axis_index("pb")
    rows = full.shape[0] // count
    size = rows // chunks

    def hop(up, distance, c):
        owner = here - distance if up else here + distance
        place = full.at[pl.ds(owner * rows + c * size, size)]
        return pltpu.make_async_remote_copy(
            src_ref=place,
            dst_ref=place,
            send_sem=send_sem.at[int(up), distance, c],
            recv_sem=recv_sem.at[int(up), distance, c],
            device_id={"pb": here + 1 if up else here - 1},
            device_id_type=MESH,
        )

    def sends(up, distance):
        if up:
            return jnp.logical_and(here >= distance, here < count - 1)
        return jnp.logical_and(here + distance <= count - 1, here > 0)

    def arrives(up, distance):
        return here >= distance if up else here + distance <= count - 1

    def step(distance, c):
        for up in (True, False):
            if distance > 0:

                @pl.when(arrives(up, distance))
                def _():
                    hop(up, distance - 1, c).wait_recv()

            if distance < count - 1:

                @pl.when(sends(up, distance))
                def _():
                    hop(up, distance, c).start()

    def finish():
        for distance in range(count - 1):
            for c in range(chunks):
                for up in (True, False):

                    @pl.when(sends(up, distance))
                    def _():
                        hop(up, distance, c).wait_send()

    return step, finish


def open_kernel(count, chunks, line, order, moves, unit_moves, head_moves, *refs):
    weights, gain_one, out, docs, x, up, down, bias, gain_two = refs[:4], *refs[4:12]
    normed_all, up_mine, first_all, gate_out, down_pack, docs_all = refs[-28:-22]
    qkv_pack, gate_pack, out_low, out_mine, normed, up_low, down_low, bias_low = refs[-22:-14]
    sems = refs[-14:]
    row, _, other_row, _, _ = plane_ids()
    here = lax.axis_index("pb")
    group, rows, _ = qkv_pack.shape

    def first_block(j):
        return first_all.at[pl.ds(here * (group * rows) + j * rows, rows)]

    def gate_block(j):
        return gate_out.at[pl.ds(j * rows, rows)]

    _, gather = gather_stages(normed, normed_all, *sems[:3])
    targets, first = owners_stages((qkv_pack,), (first_block,), *sems[3:6])
    _, second = owners_stages((gate_pack,), (gate_block,), *sems[6:9])
    _, third = owners_stages(
        (up_low if unit_moves else up,),
        (blocks_of(up_mine),),
        sems[9].at[pl.ds(0, 1)],
        sems[10].at[pl.ds(0, 1)],
        sems[10].at[pl.ds(1, 1)],
    )
    greet_partner, trade = trade_stages(line, out_low, out_mine, sems[9].at[pl.ds(1, 3)])
    step, finish = line_gather_stages(count, chunks, first_all, *sems[11:13])

    def pack(i, target):
        for j, column, place, size in head_moves[i]:
            block = weights[i][:, column : column + size].astype(BF16).astype(F32)
            target[j, :, place : place + size] = (block * gain_one[...]).astype(BF16)

    barrier = pltpu.get_barrier_semaphore()
    for target in targets:
        pl.semaphore_signal(barrier, inc=1, device_id=target, device_id_type=MESH)

    @pl.when(here > 0)
    def _():
        pl.semaphore_signal(barrier, inc=1, device_id={"pb": here - 1}, device_id_type=MESH)

    @pl.when(here < count - 1)
    def _():
        pl.semaphore_signal(barrier, inc=1, device_id={"pb": here + 1}, device_id_type=MESH)

    ends = (here > 0).astype(jnp.int32) + (here < count - 1).astype(jnp.int32)
    greeted = greet_partner(barrier) + len(targets) + ends
    for i in (0, 1, 2):
        pack(i, qkv_pack)
    pl.semaphore_wait(barrier, greeted)
    first[0]()
    give = pltpu.make_async_remote_copy(
        src_ref=docs,
        dst_ref=docs_all.at[row],
        send_sem=sems[9].at[4],
        recv_sem=sems[9].at[5],
        device_id={"dpl": other_row},
        device_id_type=MESH,
    )
    keep = pltpu.make_async_copy(docs, docs_all.at[row], sems[9].at[6])
    give.start()
    keep.start()
    out_low[...] = out[...].astype(BF16)
    trade[0]()
    first[1]()
    for c in range(chunks):
        step(0, c)
    normalize_rows(x, normed, order)
    gather[0]()
    pack(3, gate_pack)
    second[0]()
    for j, source, target, size in unit_moves:
        block = up[:, source : source + size].astype(BF16).astype(F32) * gain_two[...]
        up_low[j, :, target : target + size] = block.astype(BF16)
    third[0]()
    lanes, wide = gate_out.shape[1], out.shape[0]
    for source, target, size in moves:
        down_low[:, target : target + size] = down[:, source : source + size].astype(BF16)
    bias_low[...] = jnp.zeros(bias_low.shape, BF16)
    bias_low[0:1, 0:wide] = bias[...].astype(BF16)
    trade[1]()
    edge = gate_out.shape[0] - bias_low.shape[0]
    pairs = [(down_low, down_pack), (bias_low, gate_out.at[pl.ds(edge, bias_low.shape[0])])]
    for source, target, size in moves:
        place = pl.ds(group * rows + target // lanes * wide, wide)
        pairs.append(
            (out_mine.at[:, pl.ds(source, size)], gate_out.at[place, pl.ds(target % lanes, size)])
        )
    copies = [pltpu.make_async_copy(a, b, sems[13].at[i]) for i, (a, b) in enumerate(pairs)]
    for copy in copies:
        copy.start()
    for c in range(chunks):
        step(1, c)
    gather[1]()
    for distance in range(2, count):
        for c in range(chunks):
            step(distance, c)
            if distance == 2 and c == chunks // 2:
                gather[2]()
    give.wait()
    keep.wait()
    for copy in copies:
        copy.wait()
    second[1]()
    gather[3]()
    third[1]()
    finish()


def open_plane(
    weights, gain_one, out, docs, x, up, down, bias, gain_two, line, order, moves, unit_moves, head_moves, units, count, collective_id
):
    chunks = 4
    group = len(head_moves[0])
    rows = gain_one.shape[0]
    first = sum(w.shape[1] for w in weights[:3]) // group
    edge = 16
    return pl.pallas_call(
        functools.partial(
            open_kernel, count, chunks, line, order, moves, unit_moves, head_moves
        ),
        out_shape=[
            gathered_shape(x),
            jax.ShapeDtypeStruct((group, rows, units), BF16),
            jax.ShapeDtypeStruct((count * group * rows, first), BF16),
            jax.ShapeDtypeStruct((group * rows + out.size // units + edge, units), BF16),
            jax.ShapeDtypeStruct(down.shape, BF16),
            jax.ShapeDtypeStruct((2,) + docs.shape, docs.dtype),
        ],
        in_specs=[VMEM] * 12,
        out_specs=[ANY] * 6,
        scratch_shapes=[
            pltpu.VMEM((group, rows, first), BF16),
            pltpu.VMEM((group, rows, units), BF16),
            pltpu.VMEM(out.shape, BF16),
            pltpu.VMEM(out.shape, BF16),
            pltpu.VMEM(x.shape, BF16),
            pltpu.VMEM((group, rows, units), BF16),
            pltpu.VMEM(down.shape, BF16),
            pltpu.VMEM((edge, units), BF16),
            *GATHER_SCRATCH,
            *owners_scratch(1),
            *owners_scratch(1),
            pltpu.SemaphoreType.DMA((7,)),
            pltpu.SemaphoreType.DMA((2, 7)),
            pltpu.SemaphoreType.DMA((2, count, chunks)),
            pltpu.SemaphoreType.DMA((2, count, chunks)),
            pltpu.SemaphoreType.DMA((2 + len(moves),)),
        ],
        compiler_params=pltpu.CompilerParams(
            collective_id=collective_id,
            has_side_effects=True,
            vmem_limit_bytes=32 * 1024 * 1024,
        ),
        name="open_plane",
    )(*weights, gain_one, out, docs, x, up, down, bias, gain_two)


def scatter_stages(
    terms, finish, sent, own, sib, from_x, from_y, diag_a, diag_b, sems, recvs, even=False
):
    _, batch, length, width = own.shape
    half = length // 2
    row, col, other_row, across, sibling = plane_ids()
    across_s = lax.rem(sibling + 2, 4)
    to_x = {"ka": across}
    to_y = {"dpl": other_row}
    to_s = {"ka": sibling}
    mine = ((other_row, across), (row, across), (other_row, col), (row, col))
    theirs = ((other_row, across_s), (row, across_s), (other_row, sibling), (row, sibling))
    lower, upper = pl.ds(0, half), pl.ds(half, half)
    step = 16
    tile = 512

    def hop(src, dst, index, target):
        return pltpu.make_async_remote_copy(
            src_ref=src,
            dst_ref=dst,
            send_sem=sems.at[index],
            recv_sem=recvs.at[index],
            device_id=target,
            device_id_type=MESH,
        )

    swaps = [hop(sent.at[j], sib.at[j], j, to_s) for j in range(1, 4)]
    heads = [
        hop(sent.at[0, :, part, :], sib.at[0, :, part, :], i, to_s)
        for part, i in ((lower, 0), (upper, 10))
    ]
    first_a = hop(own.at[0, :, lower, :], diag_a, 4, to_x)
    first_b = hop(own.at[0, :, upper, :], diag_b, 5, to_y)
    x_lower = hop(own.at[1, :, lower, :], from_x.at[:, lower, :], 6, to_x)
    y_upper = hop(own.at[2, :, upper, :], from_y.at[:, upper, :], 7, to_y)
    x_upper = hop(own.at[1, :, upper, :], from_x.at[:, upper, :], 8, to_x)
    y_lower = hop(own.at[2, :, lower, :], from_y.at[:, lower, :], 9, to_y)

    def make(r, c, out, start=0, size=length):
        def body(n, carry):
            columns = pl.ds(pl.multiple_of(n * tile, tile), tile)
            value = 0.0
            for left, right, flipped in terms:
                block = left[pl.ds(r * batch, batch), pl.ds(c * length + start, size), :]
                block = block.reshape(batch * size, left.shape[2])
                if flipped:
                    value = value + lax.dot_general(
                        block,
                        right[columns, :],
                        (((1,), (1,)), ((), ())),
                        preferred_element_type=F32,
                    )
                else:
                    value = value + jnp.dot(
                        block, right[:, columns], preferred_element_type=F32
                    )
            out[:, pl.ds(start, size), columns] = value.reshape(batch, size, tile).astype(BF16)
            return carry

        lax.fori_loop(0, width // tile, body, 0)

    def give(j):
        make(*theirs[j], sent.at[j])
        swaps[j - 1].start()

    def give_head(i):
        make(*theirs[0], sent.at[0], i * half, half)
        heads[i].start()

    def own_head(i):
        make(*mine[0], own.at[0], i * half, half)

    def merge_head(i):
        heads[i].wait_recv()
        add(own.at[0], i * half, ((own.at[0], i * half), (sib.at[0], i * half)), half)

    def add(out_ref, out_start, parts, size):
        def body(i, carry):
            value = 0.0
            for ref, start in parts:
                value = value + ref[:, pl.ds(start + i * step, step), :].astype(F32)
            out_ref[:, pl.ds(out_start + i * step, step), :] = value.astype(out_ref.dtype)
            return carry

        lax.fori_loop(0, size // step, body, 0)

    def merge(j):
        swaps[j - 1].wait_recv()
        add(own.at[j], 0, ((own.at[j], 0), (sib.at[j], 0)), length)

    def open_heads():
        give_head(0)
        own_head(0)
        give_head(1)

    def send_head():
        merge_head(0)
        first_a.start()
        own_head(1)

    def send_diag():
        merge_head(1)
        first_b.start()
        make(*mine[1], own.at[1])

    def send_x():
        merge(1)
        x_lower.start()
        make(*mine[2], own.at[2])

    def send_y():
        merge(2)
        if not even:
            y_upper.start()
        make(*mine[3], own.at[3])

    def stage_rest():
        if even:
            first_a.wait_recv()
            add(own.at[2], 0, ((own.at[2], 0), (diag_a, 0)), half)
            y_lower.start()
            y_upper.start()
        first_b.wait_recv()
        add(own.at[1], half, ((own.at[1], half), (diag_b, 0)), half)
        x_upper.start()
        if not even:
            first_a.wait_recv()
            add(own.at[2], 0, ((own.at[2], 0), (diag_a, 0)), half)
            y_lower.start()
        merge(3)

    def close(start):
        def body(i, carry):
            at = pl.ds(start + i * step, step)
            for b in range(batch):
                value = own[3, b, at, :].astype(F32)
                value = value + from_x[b, at, :].astype(F32) + from_y[b, at, :].astype(F32)
                finish(b, at, value)
            return carry

        lax.fori_loop(0, half // step, body, 0)

    def close_lower():
        x_lower.wait_recv()
        y_lower.wait_recv()
        close(0)

    def close_upper():
        y_upper.wait_recv()
        x_upper.wait_recv()
        close(half)
        for copy in (first_a, first_b, x_lower, x_upper, y_lower, y_upper):
            copy.wait_send()

    def stage_free():
        for copy in heads + swaps:
            copy.wait_send()

    stages = (
        open_heads,
        send_head,
        lambda: give(1),
        send_diag,
        lambda: give(2),
        send_x,
        lambda: give(3),
        send_y,
        stage_rest,
        close_lower,
        close_upper,
        stage_free,
    )
    return (to_x, to_y, to_s), stages


def scatter_scratch(shape):
    batch, length, width = shape
    return [
        pltpu.VMEM((4,) + shape, BF16),
        pltpu.VMEM((4,) + shape, BF16),
        pltpu.VMEM((4,) + shape, BF16),
        pltpu.VMEM(shape, BF16),
        pltpu.VMEM(shape, BF16),
        pltpu.VMEM((batch, length // 2, width), BF16),
        pltpu.VMEM((batch, length // 2, width), BF16),
        pltpu.SemaphoreType.DMA((11,)),
        pltpu.SemaphoreType.DMA((11,)),
    ]


VMEM = pl.BlockSpec(memory_space=pltpu.VMEM)
ANY = pl.BlockSpec(memory_space=pl.ANY)


def mix_kernel(order, places, gated, x, gate_out, *refs):
    middle, normed_all, weight, normed, load_sem = refs[-17:-12]
    loads = [
        pltpu.make_async_copy(
            gate_out.at[pl.ds(source, rows)],
            weight.at[pl.ds(row, rows), pl.ds(column, gate_out.shape[1])],
            load_sem.at[i],
        )
        for i, (source, row, column, rows) in enumerate(places)
    ]
    for load in loads:
        load.start()

    def finish(b, at, value):
        value = value + read_rows(x, b, at, order).astype(F32)
        middle[b, at, :] = value
        normed[b, at, :] = normalize(value)[0].astype(BF16)

    targets, stages = scatter_stages(((gated, weight, False),), finish, *refs[-12:-3], True)
    lower, upper = (gather_stages(normed, normed_all, *refs[-3:], i, 2)[1] for i in (0, 1))
    greet(targets)
    for load in loads:
        load.wait()
    for stage in stages[:10] + lower[:1] + stages[10:11] + upper[:1]:
        stage()
    for pair in zip(lower[1:], upper[1:]):
        for stage in pair:
            stage()
    stages[11]()


def plane_mix(gated, x, gate_out, places, order, collective_id, *before):
    shape = x.shape
    return pl.pallas_call(
        functools.partial(mix_kernel, order, places),
        out_shape=[
            jax.ShapeDtypeStruct(shape, F32),
            gathered_shape(x),
            jax.ShapeDtypeStruct((gated.shape[2], shape[2]), BF16),
        ],
        in_specs=[VMEM] * 2 + [ANY] * (1 + len(before)),
        out_specs=[VMEM, ANY, VMEM],
        scratch_shapes=[
            pltpu.VMEM(shape, BF16),
            pltpu.SemaphoreType.DMA((len(places),)),
            *scatter_scratch(shape),
            *GATHER_SCRATCH,
        ],
        compiler_params=pltpu.CompilerParams(
            collective_id=collective_id,
            has_side_effects=True,
            vmem_limit_bytes=48 * 1024 * 1024,
        ),
        name="plane_mix",
    )(gated, x, gate_out, *before)


def turn_kernel(order, grad, weight, middle, cot, *refs):
    grad_middle, grad_all, low = refs[-15:-12]

    def finish(b, at, value):
        normed, inv = normalize(middle[b, at, :])
        value = normalize_back(normed, inv, value)
        value = value + read_rows(cot, b, at, order).astype(F32)
        grad_middle[b, at, :] = value
        low[b, at, :] = value.astype(BF16)

    targets, stages = scatter_stages(((grad, weight, True),), finish, *refs[-12:-3], True)
    lower, upper = (gather_stages(low, grad_all, *refs[-3:], i, 2)[1] for i in (0, 1))
    greet(targets)
    for stage in stages[:10] + lower[:1] + stages[10:11] + upper[:1]:
        stage()
    for pair in zip(lower[1:], upper[1:]):
        for stage in pair:
            stage()
    stages[11]()


def plane_turn(grad, weight, middle, cot, order, collective_id, *before):
    shape = middle.shape
    return pl.pallas_call(
        functools.partial(turn_kernel, order),
        out_shape=[jax.ShapeDtypeStruct(shape, F32), gathered_shape(cot)],
        in_specs=[VMEM] * 4 + [ANY] * len(before),
        out_specs=[VMEM, ANY],
        scratch_shapes=[
            pltpu.VMEM(shape, BF16),
            *scatter_scratch(shape),
            *GATHER_SCRATCH,
        ],
        compiler_params=pltpu.CompilerParams(
            collective_id=collective_id,
            has_side_effects=True,
            vmem_limit_bytes=48 * 1024 * 1024,
        ),
        name="plane_turn",
    )(grad, weight, middle, cot, *before)


def put_back(landed, weight, gain, target, moves):
    total = 0.0
    for j, column, place, size in moves:
        value = landed[j, :, place : place + size].astype(F32)
        low = weight[:, column : column + size].astype(BF16).astype(F32)
        total = total + jnp.sum(low * value, axis=-1, keepdims=True)
        target[:, column : column + size] = gain[...] * value
    return total


def last_kernel(order, moves, *refs):
    parts, weight_a, grad_b, weight_b, x, grad_middle = refs[:3], *refs[3:8]
    owned, weights, gains = refs[8:10], refs[10:12], refs[12:14]
    grad_down = refs[14]
    scratch = refs[-14:]
    outs = refs[-20:-14]

    def finish(b, at, value):
        normed, inv = normalize(read_rows(x, b, at, order).astype(F32))
        value = grad_middle[b, at, :] + normalize_back(normed, inv, value)
        write_rows(outs[0], b, at, order, value)

    terms, place = [(grad_b, weight_b, True)], 0
    for part in parts:
        columns = pl.ds(place, part.shape[2])
        terms.append((part, weight_a.at[:, columns], True))
        place += part.shape[2]
    _, stages = scatter_stages(terms, finish, *scratch[:9])
    targets, owners = owners_stages(owned, [blocks_of(ref) for ref in scratch[9:11]], *scratch[11:14])
    greet(targets)
    for stage in owners[:1] + stages[:9]:
        stage()
    size = outs[5].shape[1] // max(len(order), 1)
    for j, i in enumerate(order or (0,)):
        block = grad_down[:, j * size : (j + 1) * size]
        outs[5][:, i * size : (i + 1) * size] = block.astype(F32)
    for stage in stages[9:] + owners[1:]:
        stage()
    for i in (0, 1):
        if moves[i]:
            outs[3 + i][...] = put_back(scratch[9 + i], weights[i], gains[i], outs[1 + i], moves[i])
        else:
            outs[1 + i][...] = scratch[9 + i][...]
            outs[3 + i][...] = jnp.zeros(outs[3 + i].shape, F32)


def plane_last(
    terms, x, grad_middle, owned, weights, gains, grad_down, moves, order, collective_id, *before
):
    shape = x.shape
    column = jax.ShapeDtypeStruct(gains[0].shape, F32)
    plain = jax.ShapeDtypeStruct((grad_down.shape[0], shape[-1]), F32)
    return pl.pallas_call(
        functools.partial(last_kernel, order, moves),
        out_shape=[jax.ShapeDtypeStruct(shape, F32)]
        + [
            jax.ShapeDtypeStruct(w.shape, F32) if m else jax.ShapeDtypeStruct(o.shape, BF16)
            for o, w, m in zip(owned, weights, moves)
        ]
        + [column, column, plain],
        in_specs=[VMEM] * 8 + [ANY] * 2 + [VMEM] * 5 + [ANY] * len(before),
        out_specs=[VMEM] * 6,
        scratch_shapes=scatter_scratch(shape)
        + [pltpu.VMEM(o.shape, BF16) for o in owned]
        + owners_scratch(2),
        compiler_params=pltpu.CompilerParams(
            collective_id=collective_id,
            has_side_effects=True,
            vmem_limit_bytes=58 * 1024 * 1024,
        ),
        name="plane_last",
    )(*terms, x, grad_middle, *owned, *weights, *gains, grad_down, *before)


def scan_kernel(count, forward, cuts, gathers, order, state, coef, *refs):
    if gathers:
        moved = refs[0]
        total, result, message, landed, send_sem, recv_sem = refs[-11:-5]
        shard, shard_sem = refs[-5:-3]
        targets, stages = gather_stages(shard, result, *refs[-3:])
    else:
        left, right, middle = refs[:3]
        query, key, value, grad, scores, carried = refs[3:9]
        decay, decay_in, decay_out, cos_q, sin_q, cos_k, sin_k = refs[9:16]
        total, result, out_q, out_k, out_v = refs[-20:-15]
        sum_k, sum_v, message, landed, send_sem, recv_sem = refs[-15:-9]
        scale = query.shape[2] ** (-0.5)

        def dot(a, b, contract):
            return lax.dot_general(
                a, b, ((contract[:1], contract[1:]), ((), ())), preferred_element_type=F32
            )

        def within(s):
            low = (dot(grad[s], value[s], (1, 1)) * decay[...]).astype(BF16)
            part = dot(low, key[s], (1, 0))
            part = part + decay_in[...] * dot(grad[s], carried[s], (1, 1))
            part = turn_back(part, (cos_q[...], sin_q[...]))
            out_q[s] = (part * scale).astype(BF16)
            sum_k[s] = dot(low, query[s], (0, 0))
            sum_v[s] = dot(scores[s], grad[s], (0, 0))

        def across(s):
            part = sum_k[s] + decay_out[...] * dot(value[s], total[s], (1, 1))
            out_k[s] = turn_back(part, (cos_k[...], sin_k[...])).astype(BF16)
            part = sum_v[s] + decay_out[...] * dot(key[s], total[s], (1, 0))
            out_v[s] = part.astype(BF16)

        def finish(b, at, value):
            write_rows(result, b, at, order, (middle[b, at, :] + value).astype(BF16))

        targets, stages = scatter_stages(((left, right, False),), finish, *refs[-9:])
    here = lax.axis_index("pb")
    place = here if forward else count - 1 - here
    step = 1 if forward else -1
    has_prev = place > 0
    has_next = place < count - 1
    barrier = pltpu.get_barrier_semaphore()

    @pl.when(has_prev)
    def _():
        pl.semaphore_signal(barrier, inc=1, device_id={"pb": here - step}, device_id_type=MESH)

    @pl.when(has_next)
    def _():
        pl.semaphore_signal(barrier, inc=1, device_id={"pb": here + step}, device_id_type=MESH)

    greeted = has_prev.astype(jnp.int32) + has_next.astype(jnp.int32)
    for target in targets:
        pl.semaphore_signal(barrier, inc=1, device_id=target, device_id_type=MESH)
    pl.semaphore_wait(barrier, greeted + len(targets))

    height = state.shape[1] // cuts
    pieces = [(s, c) for s in range(state.shape[0]) for c in range(cuts)]

    def hop(i):
        s, c = pieces[i]
        rows = pl.ds(c * height, height)
        return pltpu.make_async_remote_copy(
            src_ref=message.at[s, rows],
            dst_ref=landed.at[s, rows],
            send_sem=send_sem.at[i],
            recv_sem=recv_sem.at[i],
            device_id={"pb": here + step},
            device_id_type=MESH,
        )

    def emit(i):
        s, c = pieces[i]
        rows = pl.ds(c * height, height)

        @pl.when(jnp.logical_not(has_prev))
        def _():
            message[s, rows] = state[s, rows].astype(BF16)
            hop(i).start()
            total[s, rows] = jnp.zeros((height, state.shape[2]), BF16)

        @pl.when(has_prev)
        def _():
            hop(i).wait_recv()
            total[s, rows] = (coef[0, s] * landed[s, rows].astype(F32)).astype(BF16)

            @pl.when(has_next)
            def _():
                message[s, rows] = (
                    state[s, rows] + coef[1, s] * total[s, rows].astype(F32)
                ).astype(BF16)
                hop(i).start()

    emit(0)
    if gathers:
        size = shard.shape[-1] // max(len(order), 1)
        for move in (0, 1):
            for j, i in enumerate(order or (0,)):
                copy = pltpu.make_async_copy(
                    moved.at[:, :, pl.ds(i * size, size)],
                    shard.at[:, :, pl.ds(j * size, size)],
                    shard_sem.at[j],
                )
                if move:
                    copy.wait()
                else:
                    copy.start()
        stages[0]()
    count = len(pieces)
    if gathers:
        jobs = {count // 2: stages[1:2], 3 * count // 4: stages[2:3]}
        rest = stages[3:]
    else:
        jobs = {i + 1: [stage] for i, stage in enumerate(stages[:8])}
        seqs = range(state.shape[0])
        inner = [functools.partial(within, s) for s in seqs]
        outer = [functools.partial(across, s) for s in seqs]
        late = [*inner[:3], stages[8], *inner[3:]]
        for i, job in enumerate(late):
            jobs.setdefault(min(9 + i, count - 1), []).append(job)
        rest = [*outer[:-1], *stages[9:], *outer[-1:]]
    for i in range(1, count):
        emit(i)
        for job in jobs.get(i, ()):
            job()
    for job in rest:
        job()

    @pl.when(has_next)
    def _():
        for i in range(len(pieces)):
            hop(i).wait_send()


def line_scan(state, coef, count, forward, order, collective_id, *before, gathered=None, summed=(), local=()):
    cuts = 4
    pieces = state.shape[0] * cuts
    scratch = [
        pltpu.VMEM(state.shape, BF16),
        pltpu.VMEM(state.shape, BF16),
        pltpu.SemaphoreType.DMA((pieces,)),
        pltpu.SemaphoreType.DMA((pieces,)),
    ]
    gathers = gathered is not None
    shapes = [jax.ShapeDtypeStruct(state.shape, BF16)]
    if gathers:
        operands, specs = (gathered,), [ANY]
        shapes.append(gathered_shape(gathered))
        outs = [VMEM, ANY]
        scratch += [
            pltpu.VMEM(gathered.shape, gathered.dtype),
            pltpu.SemaphoreType.DMA((max(len(order), 1),)),
            *GATHER_SCRATCH,
        ]
    else:
        operands = (*summed, *local)
        specs = [VMEM] * len(operands)
        shapes.append(jax.ShapeDtypeStruct(summed[2].shape, BF16))
        shapes += [jax.ShapeDtypeStruct(local[i].shape, BF16) for i in range(3)]
        outs = [VMEM] * 5
        scratch = [pltpu.VMEM(local[i].shape, F32) for i in (1, 2)] + scratch
        scratch += scatter_scratch(summed[2].shape)
    return pl.pallas_call(
        functools.partial(scan_kernel, count, forward, cuts, gathers, order),
        out_shape=shapes,
        in_specs=[VMEM, pl.BlockSpec(memory_space=pltpu.SMEM)] + specs + [ANY] * len(before),
        out_specs=outs,
        scratch_shapes=scratch,
        compiler_params=pltpu.CompilerParams(
            collective_id=collective_id,
            has_side_effects=True,
            vmem_limit_bytes=(16 if gathers else 58) * 1024 * 1024,
        ),
        name="line_scan",
    )(state, coef, *operands, *before)


def final_kernel(line, order, moves, grad, grad_out, *refs):
    weights, gain = refs[:3], refs[3]
    outs, out_out, sums, landed, out_landed = refs[-11:-8], refs[-8], refs[-7], refs[-6], refs[-5]
    targets, stages = owners_stages((grad,), (blocks_of(landed),), *refs[-4:-1])
    greet_partner, trade = trade_stages(line, grad_out, out_landed, refs[-1])
    barrier = pltpu.get_barrier_semaphore()
    for target in targets:
        pl.semaphore_signal(barrier, inc=1, device_id=target, device_id_type=MESH)
    pl.semaphore_wait(barrier, greet_partner(barrier) + len(targets))
    stages[0]()
    for stage in trade:
        stage()
    size = out_out.shape[1] // max(len(order), 1)
    for j, i in enumerate(order or (0,)):
        block = out_landed[:, j * size : (j + 1) * size]
        out_out[:, i * size : (i + 1) * size] = block.astype(F32)
    stages[1]()
    total = 0.0
    for weight, target, blocks in zip(weights, outs, moves):
        total = total + put_back(landed, weight, gain, target, blocks)
    sums[...] = total


def plane_final(grad, grad_out, weights, gain, line, order, moves, collective_id, *before):
    return pl.pallas_call(
        functools.partial(final_kernel, line, order, moves),
        out_shape=[jax.ShapeDtypeStruct(w.shape, F32) for w in weights]
        + [
            jax.ShapeDtypeStruct(grad_out.shape, F32),
            jax.ShapeDtypeStruct(gain.shape, F32),
        ],
        in_specs=[ANY] * 2 + [VMEM] * 4 + [ANY] * len(before),
        out_specs=[VMEM] * 5,
        scratch_shapes=[pltpu.VMEM(grad.shape, BF16), pltpu.VMEM(grad_out.shape, BF16)]
        + owners_scratch(1)
        + list(TRADE_SCRATCH),
        compiler_params=pltpu.CompilerParams(
            collective_id=collective_id,
            has_side_effects=True,
            vmem_limit_bytes=20 * 1024 * 1024,
        ),
        name="plane_final",
    )(grad, grad_out, *weights, gain, *before)


def normalize(values):
    mean = jnp.mean(values, axis=-1, keepdims=True)
    centered = values - mean
    inv = lax.rsqrt(jnp.mean(centered * centered, axis=-1, keepdims=True) + EPSILON)
    return centered * inv, inv


def normalize_back(normed, inv, grad):
    mean = jnp.mean(grad, axis=-1, keepdims=True)
    along = jnp.mean(grad * normed, axis=-1, keepdims=True)
    return inv * (grad - mean - normed * along)


def turn_tables(positions, half, direction):
    pair = jnp.arange(half, dtype=F32)
    frequency = jnp.exp(-jnp.log(10000.0) * pair / half)
    zeta = (pair / half + 0.4) / 1.4
    angles = positions[:, None] * frequency[None, :]
    factor = jnp.exp(direction * positions[:, None] / XPOS_BASE * jnp.log(zeta)[None, :])
    return jnp.cos(angles) * factor, jnp.sin(angles) * factor


def turn(values, tables):
    cosine, sine = tables
    half = values.shape[-1] // 2
    first, second = values[..., :half], values[..., half:]
    return jnp.concatenate(
        [first * cosine - second * sine, second * cosine + first * sine], axis=-1
    )


def turn_back(values, tables):
    cosine, sine = tables
    return turn(values, (cosine, -sine))


def mm(left, right):
    return jnp.einsum("sti,io->sto", left, right, preferred_element_type=F32)


def mm_back(left, right):
    return jnp.einsum("sto,io->sti", left, right, preferred_element_type=F32)


def mm_grad(left, right):
    return jnp.einsum("sti,sto->io", left, right, preferred_element_type=F32)


def after(value, *others):
    for other in others:
        value = value + (0.0 * other[(0,) * other.ndim].astype(F32)).astype(value.dtype)
    return value


def on_device(
    inputs,
    out_cotangent,
    doc_lengths,
    ln1_gain,
    w_query,
    w_key,
    w_value,
    w_gate,
    w_out,
    ln2_gain,
    w_up,
    up_bias,
    w_down,
):
    n_dph, n_dpl, n_pb, n_ka = (lax.axis_size(a) for a in ("dph", "dpl", "pb", "ka"))
    at_dpl, at_pb, at_ka = (lax.axis_index(a) for a in ("dpl", "pb", "ka"))
    batch, length, width = inputs.shape
    span = n_ka * length
    rows = w_query.shape[0]
    wide_rows = w_down.shape[0]
    key_width = w_query.shape[1] // H
    value_width = w_value.shape[1] // H
    units = n_dph * n_pb * wide_rows
    group = n_dpl * n_ka
    heads_pb = H // (n_dpl * n_dph)

    chunk = n_ka * rows

    def pick(values, order):
        return jnp.concatenate(
            [values[..., i * chunk : (i + 1) * chunk] for i in order], axis=-1
        )

    inner = [
        (d * n_dpl + r) * n_pb + p
        for d in range(n_dph)
        for p in range(n_pb)
        for r in range(n_dpl)
    ]

    def to_inner(values):
        return pick(values, inner)

    def to_outer(values):
        return pick(values, [inner.index(i) for i in range(len(inner))])

    def by_unit(weight):
        cut = weight.reshape(rows, n_dph, n_dpl, n_pb, n_ka, wide_rows)
        return jnp.transpose(cut, (2, 4, 0, 1, 3, 5)).reshape(group, rows, units)

    def from_unit(values):
        cut = values.reshape(n_dpl, n_ka, rows, n_dph, n_pb, wide_rows)
        return jnp.transpose(cut, (2, 3, 0, 4, 1, 5)).reshape(rows, -1)

    def gather_line(values):
        return lax.all_gather(values, LINE, axis=0, tiled=True)

    def scatter_line(values):
        return lax.psum_scatter(values, LINE, scatter_dimension=0, tiled=True)

    line = "dph" if n_dph > 1 else "pb"

    gain_one = ln1_gain.astype(BF16).astype(F32)[:, None]
    gain_two = ln2_gain.astype(BF16).astype(F32)[:, None]
    firsts = (w_query, w_key, w_value, w_gate)

    def head_of(j):
        r, c = j // n_ka, j % n_ka
        return (c // heads_pb) * (n_dpl * heads_pb) + r * heads_pb + c % heads_pb

    head_moves = [
        [(j, head_of(j) * size, place, size) for j in range(group)]
        for size, place in (
            (key_width, 0),
            (key_width, key_width),
            (value_width, 2 * key_width),
            (value_width, 0),
        )
    ]
    docs = jnp.pad(doc_lengths, ((0, 8 - batch), (0, 128 - doc_lengths.shape[1])))
    order = tuple(inner) if chunk % 128 == 0 else ()
    rows_in, rows_cot = inputs, out_cotangent
    if not order:
        rows_in, rows_cot = to_inner(inputs), to_inner(out_cotangent)
    out_in, down_in, up_in, unit_moves = w_out, w_down, w_up, []
    if order:
        moves = [(i * chunk, j * chunk, chunk) for j, i in enumerate(order)]
        for j in range(group):
            for q in range(n_dph * n_pb):
                block = (q // n_pb * n_dpl + j // n_ka) * n_pb + q % n_pb
                column = (block * n_ka + j % n_ka) * wide_rows
                unit_moves.append((j, column, q * wide_rows, wide_rows))
    else:
        moves = [(i * units, i * units, units) for i in range(width // units)]
        out_in, down_in = to_inner(w_out), to_inner(w_down)
        up_in = by_unit((w_up.astype(BF16).astype(F32) * gain_two).astype(BF16))
    normed_one_all, up_swapped, weight_qkv, gate_out, down_pack, docs_all = open_plane(
        firsts,
        gain_one,
        out_in,
        docs,
        rows_in,
        up_in,
        down_in,
        up_bias[None, :],
        gain_two,
        line,
        order,
        moves,
        unit_moves,
        head_moves,
        units,
        n_pb,
        0,
    )
    head = (
        (at_ka // heads_pb) * (n_dpl * heads_pb) + at_dpl * heads_pb + at_ka % heads_pb
    ).astype(F32)
    log_gamma = jnp.log(1.0 - jnp.exp2(-5.0 - head))
    offsets = jnp.arange(span, dtype=jnp.int32)
    places = (at_pb * span + offsets).astype(F32)
    tables_q = turn_tables(places, key_width // 2, 1.0)
    tables_k = turn_tables(places, key_width // 2, -1.0)
    distance = offsets[:, None] - offsets[None, :]
    decay = jnp.where(
        distance >= 0, jnp.exp(jnp.maximum(distance, 0).astype(F32) * log_gamma), 0.0
    )
    decay_in = jnp.exp(offsets.astype(F32) * log_gamma)[:, None]
    decay_out = jnp.exp((span - offsets).astype(F32) * log_gamma)[:, None]
    decay_span = jnp.exp(span * log_gamma)
    lengths = docs_all[:, :batch, : doc_lengths.shape[1]].reshape(n_dpl * batch, -1)
    ends = jnp.cumsum(lengths, axis=-1)
    edge = at_pb * span

    def goes_on(start):
        return jnp.all(ends != start, axis=-1).astype(F32)

    coef_forward = jnp.stack([goes_on(edge), jnp.full((n_dpl * batch,), decay_span)])
    coef_backward = jnp.stack([goes_on(edge + span), jnp.full((n_dpl * batch,), decay_span)])

    if n_dph > 1:
        weight_qkv = lax.all_gather(weight_qkv, "dph", axis=0, tiled=True)
    blocks = width // units
    gate_out = gather_line(gate_out)
    first = mm(normed_one_all, weight_qkv)
    query_pre = first[..., :key_width]
    key_pre = first[..., key_width : 2 * key_width]
    value = first[..., 2 * key_width :].astype(BF16)
    scale = key_width ** (-0.5)
    query = (turn(query_pre, tables_q) * scale).astype(BF16)
    key = turn(key_pre, tables_k).astype(BF16)
    key_out = (key.astype(F32) * decay_out).astype(BF16)
    state = jnp.einsum("smd,sme->sde", key_out, value, preferred_element_type=F32)
    carried, cot_all = line_scan(
        state, coef_forward, n_pb, True, order, 2, gathered=rows_cot
    )
    raw = jnp.einsum("snd,smd->snm", query, key, preferred_element_type=F32)
    scores = (raw * decay).astype(BF16)
    retained = jnp.einsum("snm,sme->sne", scores, value, preferred_element_type=F32)
    retained = retained + decay_in * jnp.einsum(
        "snd,sde->sne", query, carried, preferred_element_type=F32
    )
    normed_ret, inv_ret = normalize(retained)
    stride = gate_out.shape[0] // (n_dph * n_pb)
    spread = n_pb // heads_pb
    out_places = []
    for q in range(n_dph * n_pb):
        row = (q % spread * (n_dph * n_pb // spread) + q // spread) * wide_rows
        for i in range(blocks):
            source = q * stride + group * rows + i * wide_rows
            out_places.append((source, row, i * units, wide_rows))
    cut_out = gate_out.reshape(n_dph * n_pb, stride, units)
    bias_up = cut_out[:, stride - 16, :wide_rows].reshape(units).astype(F32)
    weight_up = gather_line(after(up_swapped.reshape(group * rows, -1), gate_out, inv_ret))
    weight_gate = after(cut_out[:, : group * rows].reshape(width, units), inv_ret)
    gate = mm(normed_one_all, weight_gate)
    gated = (gate * jax.nn.sigmoid(gate) * normed_ret).astype(BF16)
    weight_down = gather_line(after(down_pack, gated))
    gate_low = gate.astype(BF16)
    middle, normed_two_all, weight_out = plane_mix(
        gated, rows_in, gate_out, out_places, order, 3, value, query, key, scores, decay_in, decay_out
    )
    up_pre = mm(normed_two_all, weight_up) + bias_up
    bell = 0.5 * (1.0 + lax.erf(up_pre * np.float32(math.sqrt(0.5))))
    active = (up_pre * bell).astype(BF16)

    slope = bell + up_pre * (
        jnp.exp(-0.5 * up_pre * up_pre) * np.float32(1.0 / math.sqrt(2.0 * math.pi))
    )
    grad_up_pre = (mm_back(cot_all, weight_down) * slope).astype(BF16)
    ones = jnp.ones((n_dpl * batch, span, 128), BF16)
    grad_down = jnp.concatenate(
        [mm_grad(active, cot_all).astype(BF16), mm_grad(grad_up_pre, ones).astype(BF16)], axis=-1
    )
    grad_up = mm_grad(normed_two_all, grad_up_pre).astype(BF16)
    grad_middle, grad_mid_all = plane_turn(
        grad_up_pre, weight_up, middle, rows_cot, order, 5, grad_down, grad_up
    )
    grad_down = scatter_line(grad_down)
    grad_up = scatter_line(grad_up)
    grad_gated = after(mm_back(grad_mid_all, weight_out), grad_up)
    gate_again = gate_low.astype(F32)
    opened = jax.nn.sigmoid(gate_again)
    silu = gate_again * opened
    grad_gate = (grad_gated * normed_ret * (opened + silu * (1.0 - opened))).astype(BF16)
    grad_ret = normalize_back(normed_ret, inv_ret, grad_gated * silu).astype(BF16)
    query_in = (query.astype(F32) * decay_in).astype(BF16)
    grad_state = jnp.einsum("snd,sne->sde", query_in, grad_ret, preferred_element_type=F32)
    grad_out = after(mm_grad(gated, grad_mid_all), grad_down).astype(BF16)
    grad_out = (
        grad_out.reshape(n_pb // heads_pb, -1, wide_rows, width)
        .swapaxes(0, 1)
        .reshape(value_width, width)
    )
    grad_gate_w = mm_grad(normed_one_all, grad_gate).astype(BF16)
    _, output, *grad_parts = line_scan(
        grad_state,
        coef_backward,
        n_pb,
        False,
        order,
        7,
        grad_gate_w,
        grad_out,
        summed=(active, weight_down, middle),
        local=(
            query,
            key,
            value,
            grad_ret,
            scores,
            carried,
            decay,
            decay_in,
            decay_out,
            *tables_q,
            *tables_k,
        ),
    )
    grad_gate_w = scatter_line(grad_gate_w)
    grad_out = scatter_line(grad_out)
    grad_qkv = jnp.concatenate(grad_parts, axis=-1)
    grad_qkv_w = mm_grad(normed_one_all, after(grad_qkv, grad_gate_w)).astype(BF16)
    grad_qkv_sum = scatter_line(grad_qkv_w)
    cut = (group, rows, -1)
    grad_inputs, shard_gate, shard_up, sums_gate, sums_up, shard_down = plane_last(
        (*grad_parts, weight_qkv, grad_gate, weight_gate),
        rows_in,
        grad_middle,
        (grad_gate_w.reshape(cut), grad_up.reshape(cut)),
        (w_gate, w_up),
        (gain_one, gain_two),
        grad_down,
        (head_moves[3], unit_moves),
        order,
        8,
        grad_qkv_w,
    )
    if not order:
        output, grad_inputs, shard_down = (to_outer(a) for a in (output, grad_inputs, shard_down))
        shard_up = from_unit(shard_up).astype(F32)
        sums_up = jnp.sum(w_up.astype(BF16).astype(F32) * shard_up, axis=-1, keepdims=True)
        shard_up = gain_two * shard_up

    shard_query, shard_key, shard_value, shard_out, sums_qkv = plane_final(
        grad_qkv_sum.reshape(cut),
        grad_out,
        firsts[:3],
        gain_one,
        line,
        order,
        head_moves[:3],
        9,
        grad_inputs,
    )
    if not order:
        shard_out = to_outer(shard_out)
    shard_bias = grad_down[:, width].astype(F32)
    return (
        output,
        grad_inputs,
        (sums_qkv + sums_gate)[:, 0],
        shard_query,
        shard_key,
        shard_value,
        shard_gate,
        shard_out,
        sums_up[:, 0],
        shard_up,
        shard_bias,
        shard_down,
    )


def solution(mesh):
    dp, pb, ka = (mesh.shape[a] for a in ("dp", "pb", "ka"))
    fine = Mesh(mesh.devices.reshape(dp // 2, 2, pb, ka), ("dph", "dpl", "pb", "ka"))
    dp_axes = ("dph", "dpl")
    every = ("dph", "dpl", "pb", "ka")
    tokens = P(dp_axes, ("pb", "ka"), None)
    matrix = P(every, None)
    vector = P(every)
    return jax.shard_map(
        on_device,
        mesh=fine,
        in_specs=(
            tokens,
            tokens,
            P(dp_axes, None),
            vector,
            matrix,
            matrix,
            matrix,
            matrix,
            matrix,
            vector,
            matrix,
            vector,
            matrix,
        ),
        out_specs=(
            tokens,
            tokens,
            vector,
            matrix,
            matrix,
            matrix,
            matrix,
            matrix,
            vector,
            matrix,
            vector,
            matrix,
        ),
        check_vma=False,
    )
```

```python
import functools
import math

import jax
import jax.numpy as jnp
import numpy as np
from jax import lax
from jax.experimental import pallas as pl
from jax.experimental.pallas import tpu as pltpu
from jax.sharding import Mesh
from jax.sharding import PartitionSpec as P

H = 8
XPOS_BASE = 512.0
EPSILON = 1e-05
MESH = pl.DeviceIdType.MESH
F32 = jnp.float32
BF16 = jnp.bfloat16

PLANE = ("dpl", "ka")
LINE = ("dph", "pb")


def plane_ids():
    row = lax.axis_index("dpl")
    col = lax.axis_index("ka")
    other_row = 1 - row
    across = lax.rem(col + 2, 4)
    sibling = col + 1 - 2 * lax.rem(col, 2)
    return row, col, other_row, across, sibling


def greet(targets):
    barrier = pltpu.get_barrier_semaphore()
    for target in targets:
        pl.semaphore_signal(barrier, inc=1, device_id=target, device_id_type=MESH)
    pl.semaphore_wait(barrier, len(targets))


def gather_stages(shard, full, local_sem, send_sem, recv_sem, part=0, parts=1):
    batch, length, _ = shard.shape
    whole = length // parts
    first = part * whole
    half = whole // 2
    row, col, other_row, across, sibling = plane_ids()
    to_x = {"ka": across}
    to_y = {"dpl": other_row}
    to_s = {"ka": sibling}

    shard = shard.at[:, pl.ds(first, whole), :]

    def slot(r, c, start=0, size=whole):
        return full.at[pl.ds(r * batch, batch), pl.ds(c * length + first + start, size), :]

    def hop(index, target, dst, src=None):
        return pltpu.make_async_remote_copy(
            src_ref=dst if src is None else src,
            dst_ref=dst,
            send_sem=send_sem.at[part * 9 + index],
            recv_sem=recv_sem.at[part * 9 + index],
            device_id=target,
            device_id_type=MESH,
        )

    mine = pltpu.make_async_copy(shard, slot(row, col), local_sem.at[part])
    from_x = hop(0, to_x, slot(row, col), shard)
    from_y = hop(1, to_y, slot(row, col), shard)
    own_s = hop(2, to_s, slot(row, col), shard)
    diag_y = hop(3, to_y, slot(row, across, 0, half))
    relay_x = hop(4, to_s, slot(row, across))
    diag_x = hop(5, to_x, slot(other_row, col, half, half))
    relay_y = hop(6, to_s, slot(other_row, col))
    relay_a = hop(7, to_s, slot(other_row, across, 0, half))
    relay_b = hop(8, to_s, slot(other_row, across, half, half))

    def begin():
        from_x.start()
        from_y.start()
        own_s.start()
        mine.start()

    def relay():
        from_x.wait_recv()
        diag_y.start()
        relay_x.start()
        from_y.wait_recv()
        diag_x.start()
        relay_y.start()

    def diagonal():
        diag_y.wait_recv()
        relay_a.start()
        diag_x.wait_recv()
        relay_b.start()

    def end():
        for copy in (own_s, relay_x, relay_y, relay_a, relay_b):
            copy.wait_recv()
        for copy in (from_x, from_y, own_s, diag_y, relay_x, diag_x, relay_y, relay_a, relay_b):
            copy.wait_send()
        mine.wait()

    return (to_x, to_y, to_s), (begin, relay, diagonal, end)


GATHER_SCRATCH = (
    pltpu.SemaphoreType.DMA((2,)),
    pltpu.SemaphoreType.DMA((18,)),
    pltpu.SemaphoreType.DMA((18,)),
)


def gathered_shape(shard):
    batch, length, width = shard.shape
    return jax.ShapeDtypeStruct((2 * batch, 4 * length, width), shard.dtype)


def gather_kernel(shard, *refs):
    targets, stages = gather_stages(shard, *refs[-4:])
    greet(targets)
    for stage in stages:
        stage()


def read_rows(ref, b, at, order):
    if not order:
        return ref[b, at, :]
    size = ref.shape[-1] // len(order)
    return jnp.concatenate([ref[b, at, i * size : (i + 1) * size] for i in order], axis=-1)


def write_rows(ref, b, at, order, values):
    if not order:
        ref[b, at, :] = values
        return
    size = ref.shape[-1] // len(order)
    for j, i in enumerate(order):
        ref[b, at, i * size : (i + 1) * size] = values[:, j * size : (j + 1) * size]


def normalize_rows(source, target, order):
    batch, length, _ = source.shape
    step = 16

    def body(i, carry):
        at = pl.ds(i * step, step)
        for b in range(batch):
            normed, _ = normalize(read_rows(source, b, at, order).astype(F32))
            target[b, at, :] = normed.astype(BF16)
        return carry

    lax.fori_loop(0, length // step, body, 0)


def owners_stages(sources, targets, keep_sem, send_sem, recv_sem):
    row, col, other_row, _, _ = plane_ids()
    me = row * 4 + col
    peers = [(row, lax.rem(col + away, 4)) for away in (1, 2, 3)]
    peers += [(other_row, lax.rem(col + away, 4)) for away in (0, 1, 2, 3)]
    copies = []
    for a in range(len(sources)):
        copies.append(
            pltpu.make_async_copy(sources[a].at[me], targets[a](me), keep_sem.at[a])
        )
        for i in (6, 5, 4, 3, 2, 1, 0):
            r, c = peers[i]
            copies.append(
                pltpu.make_async_remote_copy(
                    src_ref=sources[a].at[r * 4 + c],
                    dst_ref=targets[a](me),
                    send_sem=send_sem.at[a, i],
                    recv_sem=recv_sem.at[a, i],
                    device_id={"dpl": r, "ka": c},
                    device_id_type=MESH,
                )
            )

    def begin():
        for copy in copies:
            copy.start()

    def end():
        for copy in copies:
            copy.wait()

    def arrive(r, c, across_rows):
        away = lax.rem(col - c + 4, 4)
        pltpu.make_async_remote_copy(
            src_ref=sources[0].at[me],
            dst_ref=targets[0](r * 4 + c),
            send_sem=send_sem.at[0, 0],
            recv_sem=recv_sem.at[0, away + 3 if across_rows else away - 1],
            device_id={"dpl": other_row, "ka": col},
            device_id_type=MESH,
        ).wait_recv()

    def leave():
        for copy in copies[1:]:
            copy.wait_send()

    near = (copies[0].wait, arrive, leave) if len(sources) == 1 else None
    return [{"dpl": r, "ka": c} for r, c in peers], (begin, end, near)


def blocks_of(ref):
    return lambda j: ref.at[j]


def owners_scratch(count):
    return [
        pltpu.SemaphoreType.DMA((count,)),
        pltpu.SemaphoreType.DMA((count, 7)),
        pltpu.SemaphoreType.DMA((count, 7)),
    ]


def trade_stages(line, source, target, sems):
    place, col = lax.axis_index(line), lax.axis_index("ka")
    moves = place != col
    partner = {line: col, "ka": place}

    def trade():
        return pltpu.make_async_remote_copy(
            src_ref=source,
            dst_ref=target,
            send_sem=sems.at[0],
            recv_sem=sems.at[1],
            device_id=partner,
            device_id_type=MESH,
        )

    def keep():
        return pltpu.make_async_copy(source, target, sems.at[2])

    def greet_partner(barrier):
        @pl.when(moves)
        def _():
            pl.semaphore_signal(barrier, inc=1, device_id=partner, device_id_type=MESH)

        return moves.astype(jnp.int32)

    def begin():
        @pl.when(moves)
        def _():
            trade().start()

        @pl.when(jnp.logical_not(moves))
        def _():
            keep().start()

    def end():
        @pl.when(moves)
        def _():
            trade().wait()

        @pl.when(jnp.logical_not(moves))
        def _():
            keep().wait()

    return greet_partner, (begin, end)


TRADE_SCRATCH = (pltpu.SemaphoreType.DMA((3,)),)


def line_gather_stages(count, chunks, full, send_sem, recv_sem):
    here = lax.axis_index("pb")
    rows = full.shape[0] // count
    size = rows // chunks

    def hop(up, distance, c):
        owner = here - distance if up else here + distance
        place = full.at[pl.ds(owner * rows + c * size, size)]
        return pltpu.make_async_remote_copy(
            src_ref=place,
            dst_ref=place,
            send_sem=send_sem.at[int(up), distance, c],
            recv_sem=recv_sem.at[int(up), distance, c],
            device_id={"pb": here + 1 if up else here - 1},
            device_id_type=MESH,
        )

    def sends(up, distance):
        if up:
            return jnp.logical_and(here >= distance, here < count - 1)
        return jnp.logical_and(here + distance <= count - 1, here > 0)

    def arrives(up, distance):
        return here >= distance if up else here + distance <= count - 1

    def step(distance, c):
        for up in (True, False):
            if distance > 0:

                @pl.when(arrives(up, distance))
                def _():
                    hop(up, distance - 1, c).wait_recv()

            if distance < count - 1:

                @pl.when(sends(up, distance))
                def _():
                    hop(up, distance, c).start()

    def finish():
        for distance in range(count - 1):
            for c in range(chunks):
                for up in (True, False):

                    @pl.when(sends(up, distance))
                    def _():
                        hop(up, distance, c).wait_send()

    return step, finish


def open_kernel(count, chunks, line, order, moves, unit_moves, head_moves, *refs):
    weights, gain_one, out, docs, x, up, down, bias, gain_two = refs[:4], *refs[4:12]
    normed_all, up_mine, first_all, gate_out, down_pack, docs_all = refs[-28:-22]
    qkv_pack, gate_pack, out_low, out_mine, normed, up_low, down_low, bias_low = refs[-22:-14]
    sems = refs[-14:]
    row, _, other_row, _, _ = plane_ids()
    here = lax.axis_index("pb")
    group, rows, _ = qkv_pack.shape

    def first_block(j):
        return first_all.at[pl.ds(here * (group * rows) + j * rows, rows)]

    def gate_block(j):
        return gate_out.at[pl.ds(j * rows, rows)]

    _, gather = gather_stages(normed, normed_all, *sems[:3])
    targets, first = owners_stages((qkv_pack,), (first_block,), *sems[3:6])
    _, second = owners_stages((gate_pack,), (gate_block,), *sems[6:9])
    _, third = owners_stages(
        (up_low if unit_moves else up,),
        (blocks_of(up_mine),),
        sems[9].at[pl.ds(0, 1)],
        sems[10].at[pl.ds(0, 1)],
        sems[10].at[pl.ds(1, 1)],
    )
    greet_partner, trade = trade_stages(line, out_low, out_mine, sems[9].at[pl.ds(1, 3)])
    step, finish = line_gather_stages(count, chunks, first_all, *sems[11:13])

    def pack(i, target):
        for j, column, place, size in head_moves[i]:
            block = weights[i][:, column : column + size].astype(BF16).astype(F32)
            target[j, :, place : place + size] = (block * gain_one[...]).astype(BF16)

    barrier = pltpu.get_barrier_semaphore()
    for target in targets:
        pl.semaphore_signal(barrier, inc=1, device_id=target, device_id_type=MESH)

    @pl.when(here > 0)
    def _():
        pl.semaphore_signal(barrier, inc=1, device_id={"pb": here - 1}, device_id_type=MESH)

    @pl.when(here < count - 1)
    def _():
        pl.semaphore_signal(barrier, inc=1, device_id={"pb": here + 1}, device_id_type=MESH)

    ends = (here > 0).astype(jnp.int32) + (here < count - 1).astype(jnp.int32)
    greeted = greet_partner(barrier) + len(targets) + ends
    for i in (0, 1, 2):
        pack(i, qkv_pack)
    pl.semaphore_wait(barrier, greeted)
    first[0]()
    give = pltpu.make_async_remote_copy(
        src_ref=docs,
        dst_ref=docs_all.at[row],
        send_sem=sems[9].at[4],
        recv_sem=sems[9].at[5],
        device_id={"dpl": other_row},
        device_id_type=MESH,
    )
    keep = pltpu.make_async_copy(docs, docs_all.at[row], sems[9].at[6])
    give.start()
    keep.start()
    out_low[...] = out[...].astype(BF16)
    trade[0]()
    _, col, _, across, sibling = plane_ids()
    across_s = lax.rem(sibling + 2, 4)
    kept, arrive, leave = first[2]
    kept()
    arrive(row, sibling, False)
    nearest = [row * 2 + col // 2]
    step(0, nearest[0])
    for r, c, d, far in (
        (row, across, across_s, False),
        (other_row, col, sibling, True),
        (other_row, across, across_s, True),
    ):
        arrive(r, c, far)
        arrive(r, d, far)
        nearest.append(r * 2 + c // 2)
        step(0, nearest[-1])
    normalize_rows(x, normed, order)
    gather[0]()
    pack(3, gate_pack)
    second[0]()
    for j, source, target, size in unit_moves:
        block = up[:, source : source + size].astype(BF16).astype(F32) * gain_two[...]
        up_low[j, :, target : target + size] = block.astype(BF16)
    third[0]()
    lanes, wide = gate_out.shape[1], out.shape[0]
    for source, target, size in moves:
        down_low[:, target : target + size] = down[:, source : source + size].astype(BF16)
    bias_low[...] = jnp.zeros(bias_low.shape, BF16)
    bias_low[0:1, 0:wide] = bias[...].astype(BF16)
    trade[1]()
    edge = gate_out.shape[0] - bias_low.shape[0]
    pairs = [(down_low, down_pack), (bias_low, gate_out.at[pl.ds(edge, bias_low.shape[0])])]
    for source, target, size in moves:
        place = pl.ds(group * rows + target // lanes * wide, wide)
        pairs.append(
            (out_mine.at[:, pl.ds(source, size)], gate_out.at[place, pl.ds(target % lanes, size)])
        )
    copies = [pltpu.make_async_copy(a, b, sems[13].at[i]) for i, (a, b) in enumerate(pairs)]
    for copy in copies:
        copy.start()
    for c in nearest:
        step(1, c)
    gather[1]()
    for distance in range(2, count):
        for i, c in enumerate(nearest):
            step(distance, c)
            if distance == 2 and i == chunks // 2:
                gather[2]()
    leave()
    give.wait()
    keep.wait()
    for copy in copies:
        copy.wait()
    second[1]()
    gather[3]()
    third[1]()
    finish()


def open_plane(
    weights, gain_one, out, docs, x, up, down, bias, gain_two, line, order, moves, unit_moves, head_moves, units, count, collective_id
):
    chunks = 4
    group = len(head_moves[0])
    rows = gain_one.shape[0]
    first = sum(w.shape[1] for w in weights[:3]) // group
    edge = 16
    return pl.pallas_call(
        functools.partial(
            open_kernel, count, chunks, line, order, moves, unit_moves, head_moves
        ),
        out_shape=[
            gathered_shape(x),
            jax.ShapeDtypeStruct((group, rows, units), BF16),
            jax.ShapeDtypeStruct((count * group * rows, first), BF16),
            jax.ShapeDtypeStruct((group * rows + out.size // units + edge, units), BF16),
            jax.ShapeDtypeStruct(down.shape, BF16),
            jax.ShapeDtypeStruct((2,) + docs.shape, docs.dtype),
        ],
        in_specs=[VMEM] * 12,
        out_specs=[ANY] * 6,
        scratch_shapes=[
            pltpu.VMEM((group, rows, first), BF16),
            pltpu.VMEM((group, rows, units), BF16),
            pltpu.VMEM(out.shape, BF16),
            pltpu.VMEM(out.shape, BF16),
            pltpu.VMEM(x.shape, BF16),
            pltpu.VMEM((group, rows, units), BF16),
            pltpu.VMEM(down.shape, BF16),
            pltpu.VMEM((edge, units), BF16),
            *GATHER_SCRATCH,
            *owners_scratch(1),
            *owners_scratch(1),
            pltpu.SemaphoreType.DMA((7,)),
            pltpu.SemaphoreType.DMA((2, 7)),
            pltpu.SemaphoreType.DMA((2, count, chunks)),
            pltpu.SemaphoreType.DMA((2, count, chunks)),
            pltpu.SemaphoreType.DMA((2 + len(moves),)),
        ],
        compiler_params=pltpu.CompilerParams(
            collective_id=collective_id,
            has_side_effects=True,
            vmem_limit_bytes=32 * 1024 * 1024,
        ),
        name="open_plane",
    )(*weights, gain_one, out, docs, x, up, down, bias, gain_two)


def scatter_stages(
    terms, finish, sent, own, sib, from_x, from_y, diag_a, diag_b, sems, recvs, even=False
):
    _, batch, length, width = own.shape
    half = length // 2
    row, col, other_row, across, sibling = plane_ids()
    across_s = lax.rem(sibling + 2, 4)
    to_x = {"ka": across}
    to_y = {"dpl": other_row}
    to_s = {"ka": sibling}
    mine = ((other_row, across), (row, across), (other_row, col), (row, col))
    theirs = ((other_row, across_s), (row, across_s), (other_row, sibling), (row, sibling))
    lower, upper = pl.ds(0, half), pl.ds(half, half)
    step = 16
    tile = 512

    def hop(src, dst, index, target):
        return pltpu.make_async_remote_copy(
            src_ref=src,
            dst_ref=dst,
            send_sem=sems.at[index],
            recv_sem=recvs.at[index],
            device_id=target,
            device_id_type=MESH,
        )

    swaps = [hop(sent.at[j], sib.at[j], j, to_s) for j in range(1, 4)]
    heads = [
        hop(sent.at[0, :, part, :], sib.at[0, :, part, :], i, to_s)
        for part, i in ((lower, 0), (upper, 10))
    ]
    first_a = hop(own.at[0, :, lower, :], diag_a, 4, to_x)
    first_b = hop(own.at[0, :, upper, :], diag_b, 5, to_y)
    x_lower = hop(own.at[1, :, lower, :], from_x.at[:, lower, :], 6, to_x)
    y_upper = hop(own.at[2, :, upper, :], from_y.at[:, upper, :], 7, to_y)
    x_upper = hop(own.at[1, :, upper, :], from_x.at[:, upper, :], 8, to_x)
    y_lower = hop(own.at[2, :, lower, :], from_y.at[:, lower, :], 9, to_y)

    def make(r, c, out, start=0, size=length):
        def body(n, carry):
            columns = pl.ds(pl.multiple_of(n * tile, tile), tile)
            value = 0.0
            for left, right, flipped in terms:
                block = left[pl.ds(r * batch, batch), pl.ds(c * length + start, size), :]
                block = block.reshape(batch * size, left.shape[2])
                if flipped:
                    value = value + lax.dot_general(
                        block,
                        right[columns, :],
                        (((1,), (1,)), ((), ())),
                        preferred_element_type=F32,
                    )
                else:
                    value = value + jnp.dot(
                        block, right[:, columns], preferred_element_type=F32
                    )
            out[:, pl.ds(start, size), columns] = value.reshape(batch, size, tile).astype(BF16)
            return carry

        lax.fori_loop(0, width // tile, body, 0)

    def give(j):
        make(*theirs[j], sent.at[j])
        swaps[j - 1].start()

    def give_head(i):
        make(*theirs[0], sent.at[0], i * half, half)
        heads[i].start()

    def own_head(i):
        make(*mine[0], own.at[0], i * half, half)

    def merge_head(i):
        heads[i].wait_recv()
        add(own.at[0], i * half, ((own.at[0], i * half), (sib.at[0], i * half)), half)

    def add(out_ref, out_start, parts, size):
        def body(i, carry):
            value = 0.0
            for ref, start in parts:
                value = value + ref[:, pl.ds(start + i * step, step), :].astype(F32)
            out_ref[:, pl.ds(out_start + i * step, step), :] = value.astype(out_ref.dtype)
            return carry

        lax.fori_loop(0, size // step, body, 0)

    def merge(j):
        swaps[j - 1].wait_recv()
        add(own.at[j], 0, ((own.at[j], 0), (sib.at[j], 0)), length)

    def open_heads():
        give_head(0)
        own_head(0)
        give_head(1)

    def send_head():
        merge_head(0)
        first_a.start()
        own_head(1)

    def send_diag():
        merge_head(1)
        first_b.start()
        make(*mine[1], own.at[1])

    def send_x():
        merge(1)
        x_lower.start()
        make(*mine[2], own.at[2])

    def send_y():
        merge(2)
        if not even:
            y_upper.start()
        make(*mine[3], own.at[3])

    def stage_rest():
        if even:
            first_a.wait_recv()
            add(own.at[2], 0, ((own.at[2], 0), (diag_a, 0)), half)
            y_lower.start()
            y_upper.start()
        first_b.wait_recv()
        add(own.at[1], half, ((own.at[1], half), (diag_b, 0)), half)
        x_upper.start()
        if not even:
            first_a.wait_recv()
            add(own.at[2], 0, ((own.at[2], 0), (diag_a, 0)), half)
            y_lower.start()
        merge(3)

    def close(start):
        def body(i, carry):
            at = pl.ds(start + i * step, step)
            for b in range(batch):
                value = own[3, b, at, :].astype(F32)
                value = value + from_x[b, at, :].astype(F32) + from_y[b, at, :].astype(F32)
                finish(b, at, value)
            return carry

        lax.fori_loop(0, half // step, body, 0)

    def close_lower():
        x_lower.wait_recv()
        y_lower.wait_recv()
        close(0)

    def close_upper():
        y_upper.wait_recv()
        x_upper.wait_recv()
        close(half)
        for copy in (first_a, first_b, x_lower, x_upper, y_lower, y_upper):
            copy.wait_send()

    def stage_free():
        for copy in heads + swaps:
            copy.wait_send()

    stages = (
        open_heads,
        send_head,
        lambda: give(1),
        send_diag,
        lambda: give(2),
        send_x,
        lambda: give(3),
        send_y,
        stage_rest,
        close_lower,
        close_upper,
        stage_free,
    )
    return (to_x, to_y, to_s), stages


def scatter_scratch(shape):
    batch, length, width = shape
    return [
        pltpu.VMEM((4,) + shape, BF16),
        pltpu.VMEM((4,) + shape, BF16),
        pltpu.VMEM((4,) + shape, BF16),
        pltpu.VMEM(shape, BF16),
        pltpu.VMEM(shape, BF16),
        pltpu.VMEM((batch, length // 2, width), BF16),
        pltpu.VMEM((batch, length // 2, width), BF16),
        pltpu.SemaphoreType.DMA((11,)),
        pltpu.SemaphoreType.DMA((11,)),
    ]


VMEM = pl.BlockSpec(memory_space=pltpu.VMEM)
ANY = pl.BlockSpec(memory_space=pl.ANY)


def mix_kernel(order, places, gated, x, gate_out, *refs):
    middle, normed_all, weight, normed, load_sem = refs[-17:-12]
    loads = [
        pltpu.make_async_copy(
            gate_out.at[pl.ds(source, rows)],
            weight.at[pl.ds(row, rows), pl.ds(column, gate_out.shape[1])],
            load_sem.at[i],
        )
        for i, (source, row, column, rows) in enumerate(places)
    ]
    for load in loads:
        load.start()

    def finish(b, at, value):
        value = value + read_rows(x, b, at, order).astype(F32)
        middle[b, at, :] = value
        normed[b, at, :] = normalize(value)[0].astype(BF16)

    targets, stages = scatter_stages(((gated, weight, False),), finish, *refs[-12:-3], True)
    lower, upper = (gather_stages(normed, normed_all, *refs[-3:], i, 2)[1] for i in (0, 1))
    greet(targets)
    for load in loads:
        load.wait()
    for stage in stages[:10] + lower[:1] + stages[10:11] + upper[:1]:
        stage()
    for pair in zip(lower[1:], upper[1:]):
        for stage in pair:
            stage()
    stages[11]()


def plane_mix(gated, x, gate_out, places, order, collective_id, *before):
    shape = x.shape
    return pl.pallas_call(
        functools.partial(mix_kernel, order, places),
        out_shape=[
            jax.ShapeDtypeStruct(shape, F32),
            gathered_shape(x),
            jax.ShapeDtypeStruct((gated.shape[2], shape[2]), BF16),
        ],
        in_specs=[VMEM] * 2 + [ANY] * (1 + len(before)),
        out_specs=[VMEM, ANY, VMEM],
        scratch_shapes=[
            pltpu.VMEM(shape, BF16),
            pltpu.SemaphoreType.DMA((len(places),)),
            *scatter_scratch(shape),
            *GATHER_SCRATCH,
        ],
        compiler_params=pltpu.CompilerParams(
            collective_id=collective_id,
            has_side_effects=True,
            vmem_limit_bytes=48 * 1024 * 1024,
        ),
        name="plane_mix",
    )(gated, x, gate_out, *before)


def turn_kernel(order, grad, weight, middle, cot, *refs):
    grad_middle, grad_all, low = refs[-15:-12]

    def finish(b, at, value):
        normed, inv = normalize(middle[b, at, :])
        value = normalize_back(normed, inv, value)
        value = value + read_rows(cot, b, at, order).astype(F32)
        grad_middle[b, at, :] = value
        low[b, at, :] = value.astype(BF16)

    targets, stages = scatter_stages(((grad, weight, True),), finish, *refs[-12:-3], True)
    lower, upper = (gather_stages(low, grad_all, *refs[-3:], i, 2)[1] for i in (0, 1))
    greet(targets)
    for stage in stages[:10] + lower[:1] + stages[10:11] + upper[:1]:
        stage()
    for pair in zip(lower[1:], upper[1:]):
        for stage in pair:
            stage()
    stages[11]()


def plane_turn(grad, weight, middle, cot, order, collective_id, *before):
    shape = middle.shape
    return pl.pallas_call(
        functools.partial(turn_kernel, order),
        out_shape=[jax.ShapeDtypeStruct(shape, F32), gathered_shape(cot)],
        in_specs=[VMEM] * 4 + [ANY] * len(before),
        out_specs=[VMEM, ANY],
        scratch_shapes=[
            pltpu.VMEM(shape, BF16),
            *scatter_scratch(shape),
            *GATHER_SCRATCH,
        ],
        compiler_params=pltpu.CompilerParams(
            collective_id=collective_id,
            has_side_effects=True,
            vmem_limit_bytes=48 * 1024 * 1024,
        ),
        name="plane_turn",
    )(grad, weight, middle, cot, *before)


def put_back(landed, weight, gain, target, moves):
    total = 0.0
    for j, column, place, size in moves:
        value = landed[j, :, place : place + size].astype(F32)
        low = weight[:, column : column + size].astype(BF16).astype(F32)
        total = total + jnp.sum(low * value, axis=-1, keepdims=True)
        target[:, column : column + size] = gain[...] * value
    return total


def last_kernel(order, moves, *refs):
    parts, weight_a, grad_b, weight_b, x, grad_middle = refs[:3], *refs[3:8]
    owned, weights, gains = refs[8:10], refs[10:12], refs[12:14]
    grad_down = refs[14]
    scratch = refs[-14:]
    outs = refs[-20:-14]

    def finish(b, at, value):
        normed, inv = normalize(read_rows(x, b, at, order).astype(F32))
        value = grad_middle[b, at, :] + normalize_back(normed, inv, value)
        write_rows(outs[0], b, at, order, value)

    terms, place = [(grad_b, weight_b, True)], 0
    for part in parts:
        columns = pl.ds(place, part.shape[2])
        terms.append((part, weight_a.at[:, columns], True))
        place += part.shape[2]
    _, stages = scatter_stages(terms, finish, *scratch[:9])
    targets, owners = owners_stages(owned, [blocks_of(ref) for ref in scratch[9:11]], *scratch[11:14])
    greet(targets)
    for stage in owners[:1] + stages[:9]:
        stage()
    size = outs[5].shape[1] // max(len(order), 1)
    for j, i in enumerate(order or (0,)):
        block = grad_down[:, j * size : (j + 1) * size]
        outs[5][:, i * size : (i + 1) * size] = block.astype(F32)
    for stage in stages[9:] + owners[1:2]:
        stage()
    for i in (0, 1):
        if moves[i]:
            outs[3 + i][...] = put_back(scratch[9 + i], weights[i], gains[i], outs[1 + i], moves[i])
        else:
            outs[1 + i][...] = scratch[9 + i][...]
            outs[3 + i][...] = jnp.zeros(outs[3 + i].shape, F32)


def plane_last(
    terms, x, grad_middle, owned, weights, gains, grad_down, moves, order, collective_id, *before
):
    shape = x.shape
    column = jax.ShapeDtypeStruct(gains[0].shape, F32)
    plain = jax.ShapeDtypeStruct((grad_down.shape[0], shape[-1]), F32)
    return pl.pallas_call(
        functools.partial(last_kernel, order, moves),
        out_shape=[jax.ShapeDtypeStruct(shape, F32)]
        + [
            jax.ShapeDtypeStruct(w.shape, F32) if m else jax.ShapeDtypeStruct(o.shape, BF16)
            for o, w, m in zip(owned, weights, moves)
        ]
        + [column, column, plain],
        in_specs=[VMEM] * 8 + [ANY] * 2 + [VMEM] * 5 + [ANY] * len(before),
        out_specs=[VMEM] * 6,
        scratch_shapes=scatter_scratch(shape)
        + [pltpu.VMEM(o.shape, BF16) for o in owned]
        + owners_scratch(2),
        compiler_params=pltpu.CompilerParams(
            collective_id=collective_id,
            has_side_effects=True,
            vmem_limit_bytes=58 * 1024 * 1024,
        ),
        name="plane_last",
    )(*terms, x, grad_middle, *owned, *weights, *gains, grad_down, *before)


def scan_kernel(count, forward, cuts, gathers, order, state, coef, *refs):
    if gathers:
        moved = refs[0]
        total, result, message, landed, send_sem, recv_sem = refs[-11:-5]
        shard, shard_sem = refs[-5:-3]
        targets, stages = gather_stages(shard, result, *refs[-3:])
    else:
        left, right, middle = refs[:3]
        query, key, value, grad, scores, carried = refs[3:9]
        decay, decay_in, decay_out, cos_q, sin_q, cos_k, sin_k = refs[9:16]
        total, result, out_q, out_k, out_v = refs[-20:-15]
        sum_k, sum_v, message, landed, send_sem, recv_sem = refs[-15:-9]
        scale = query.shape[2] ** (-0.5)

        def dot(a, b, contract):
            return lax.dot_general(
                a, b, ((contract[:1], contract[1:]), ((), ())), preferred_element_type=F32
            )

        def within(s):
            low = (dot(grad[s], value[s], (1, 1)) * decay[...]).astype(BF16)
            part = dot(low, key[s], (1, 0))
            part = part + decay_in[...] * dot(grad[s], carried[s], (1, 1))
            part = turn_back(part, (cos_q[...], sin_q[...]))
            out_q[s] = (part * scale).astype(BF16)
            sum_k[s] = dot(low, query[s], (0, 0))
            sum_v[s] = dot(scores[s], grad[s], (0, 0))

        def across(s):
            part = sum_k[s] + decay_out[...] * dot(value[s], total[s], (1, 1))
            out_k[s] = turn_back(part, (cos_k[...], sin_k[...])).astype(BF16)
            part = sum_v[s] + decay_out[...] * dot(key[s], total[s], (1, 0))
            out_v[s] = part.astype(BF16)

        def finish(b, at, value):
            write_rows(result, b, at, order, (middle[b, at, :] + value).astype(BF16))

        targets, stages = scatter_stages(((left, right, False),), finish, *refs[-9:])
    here = lax.axis_index("pb")
    place = here if forward else count - 1 - here
    step = 1 if forward else -1
    has_prev = place > 0
    has_next = place < count - 1
    barrier = pltpu.get_barrier_semaphore()

    @pl.when(has_prev)
    def _():
        pl.semaphore_signal(barrier, inc=1, device_id={"pb": here - step}, device_id_type=MESH)

    @pl.when(has_next)
    def _():
        pl.semaphore_signal(barrier, inc=1, device_id={"pb": here + step}, device_id_type=MESH)

    greeted = has_prev.astype(jnp.int32) + has_next.astype(jnp.int32)
    for target in targets:
        pl.semaphore_signal(barrier, inc=1, device_id=target, device_id_type=MESH)
    pl.semaphore_wait(barrier, greeted + len(targets))

    height = state.shape[1] // cuts
    pieces = [(s, c) for s in range(state.shape[0]) for c in range(cuts)]

    def hop(i):
        s, c = pieces[i]
        rows = pl.ds(c * height, height)
        return pltpu.make_async_remote_copy(
            src_ref=message.at[s, rows],
            dst_ref=landed.at[s, rows],
            send_sem=send_sem.at[i],
            recv_sem=recv_sem.at[i],
            device_id={"pb": here + step},
            device_id_type=MESH,
        )

    def emit(i):
        s, c = pieces[i]
        rows = pl.ds(c * height, height)

        @pl.when(jnp.logical_not(has_prev))
        def _():
            message[s, rows] = state[s, rows].astype(BF16)
            hop(i).start()
            total[s, rows] = jnp.zeros((height, state.shape[2]), BF16)

        @pl.when(has_prev)
        def _():
            hop(i).wait_recv()
            total[s, rows] = (coef[0, s] * landed[s, rows].astype(F32)).astype(BF16)

            @pl.when(has_next)
            def _():
                message[s, rows] = (
                    state[s, rows] + coef[1, s] * total[s, rows].astype(F32)
                ).astype(BF16)
                hop(i).start()

    emit(0)
    if gathers:
        size = shard.shape[-1] // max(len(order), 1)
        for move in (0, 1):
            for j, i in enumerate(order or (0,)):
                copy = pltpu.make_async_copy(
                    moved.at[:, :, pl.ds(i * size, size)],
                    shard.at[:, :, pl.ds(j * size, size)],
                    shard_sem.at[j],
                )
                if move:
                    copy.wait()
                else:
                    copy.start()
        stages[0]()
    count = len(pieces)
    if gathers:
        jobs = {count // 2: stages[1:2], 3 * count // 4: stages[2:3]}
        rest = stages[3:]
    else:
        jobs = {i + 1: [stage] for i, stage in enumerate(stages[:8])}
        seqs = range(state.shape[0])
        inner = [functools.partial(within, s) for s in seqs]
        outer = [functools.partial(across, s) for s in seqs]
        late = [*inner[:3], stages[8], *inner[3:]]
        for i, job in enumerate(late):
            jobs.setdefault(min(9 + i, count - 1), []).append(job)
        rest = [*outer[:-1], *stages[9:], *outer[-1:]]
    for i in range(1, count):
        emit(i)
        for job in jobs.get(i, ()):
            job()
    for job in rest:
        job()

    @pl.when(has_next)
    def _():
        for i in range(len(pieces)):
            hop(i).wait_send()


def line_scan(state, coef, count, forward, order, collective_id, *before, gathered=None, summed=(), local=()):
    cuts = 4
    pieces = state.shape[0] * cuts
    scratch = [
        pltpu.VMEM(state.shape, BF16),
        pltpu.VMEM(state.shape, BF16),
        pltpu.SemaphoreType.DMA((pieces,)),
        pltpu.SemaphoreType.DMA((pieces,)),
    ]
    gathers = gathered is not None
    shapes = [jax.ShapeDtypeStruct(state.shape, BF16)]
    if gathers:
        operands, specs = (gathered,), [ANY]
        shapes.append(gathered_shape(gathered))
        outs = [VMEM, ANY]
        scratch += [
            pltpu.VMEM(gathered.shape, gathered.dtype),
            pltpu.SemaphoreType.DMA((max(len(order), 1),)),
            *GATHER_SCRATCH,
        ]
    else:
        operands = (*summed, *local)
        specs = [VMEM] * len(operands)
        shapes.append(jax.ShapeDtypeStruct(summed[2].shape, BF16))
        shapes += [jax.ShapeDtypeStruct(local[i].shape, BF16) for i in range(3)]
        outs = [VMEM] * 5
        scratch = [pltpu.VMEM(local[i].shape, F32) for i in (1, 2)] + scratch
        scratch += scatter_scratch(summed[2].shape)
    return pl.pallas_call(
        functools.partial(scan_kernel, count, forward, cuts, gathers, order),
        out_shape=shapes,
        in_specs=[VMEM, pl.BlockSpec(memory_space=pltpu.SMEM)] + specs + [ANY] * len(before),
        out_specs=outs,
        scratch_shapes=scratch,
        compiler_params=pltpu.CompilerParams(
            collective_id=collective_id,
            has_side_effects=True,
            vmem_limit_bytes=(16 if gathers else 58) * 1024 * 1024,
        ),
        name="line_scan",
    )(state, coef, *operands, *before)


def final_kernel(line, order, moves, grad, grad_out, *refs):
    weights, gain = refs[:3], refs[3]
    outs, out_out, sums, landed, out_landed = refs[-11:-8], refs[-8], refs[-7], refs[-6], refs[-5]
    targets, stages = owners_stages((grad,), (blocks_of(landed),), *refs[-4:-1])
    greet_partner, trade = trade_stages(line, grad_out, out_landed, refs[-1])
    barrier = pltpu.get_barrier_semaphore()
    for target in targets:
        pl.semaphore_signal(barrier, inc=1, device_id=target, device_id_type=MESH)
    pl.semaphore_wait(barrier, greet_partner(barrier) + len(targets))
    stages[0]()
    for stage in trade:
        stage()
    size = out_out.shape[1] // max(len(order), 1)
    for j, i in enumerate(order or (0,)):
        block = out_landed[:, j * size : (j + 1) * size]
        out_out[:, i * size : (i + 1) * size] = block.astype(F32)
    stages[1]()
    total = 0.0
    for weight, target, blocks in zip(weights, outs, moves):
        total = total + put_back(landed, weight, gain, target, blocks)
    sums[...] = total


def plane_final(grad, grad_out, weights, gain, line, order, moves, collective_id, *before):
    return pl.pallas_call(
        functools.partial(final_kernel, line, order, moves),
        out_shape=[jax.ShapeDtypeStruct(w.shape, F32) for w in weights]
        + [
            jax.ShapeDtypeStruct(grad_out.shape, F32),
            jax.ShapeDtypeStruct(gain.shape, F32),
        ],
        in_specs=[ANY] * 2 + [VMEM] * 4 + [ANY] * len(before),
        out_specs=[VMEM] * 5,
        scratch_shapes=[pltpu.VMEM(grad.shape, BF16), pltpu.VMEM(grad_out.shape, BF16)]
        + owners_scratch(1)
        + list(TRADE_SCRATCH),
        compiler_params=pltpu.CompilerParams(
            collective_id=collective_id,
            has_side_effects=True,
            vmem_limit_bytes=20 * 1024 * 1024,
        ),
        name="plane_final",
    )(grad, grad_out, *weights, gain, *before)


def normalize(values):
    mean = jnp.mean(values, axis=-1, keepdims=True)
    centered = values - mean
    inv = lax.rsqrt(jnp.mean(centered * centered, axis=-1, keepdims=True) + EPSILON)
    return centered * inv, inv


def normalize_back(normed, inv, grad):
    mean = jnp.mean(grad, axis=-1, keepdims=True)
    along = jnp.mean(grad * normed, axis=-1, keepdims=True)
    return inv * (grad - mean - normed * along)


def turn_tables(positions, half, direction):
    pair = jnp.arange(half, dtype=F32)
    frequency = jnp.exp(-jnp.log(10000.0) * pair / half)
    zeta = (pair / half + 0.4) / 1.4
    angles = positions[:, None] * frequency[None, :]
    factor = jnp.exp(direction * positions[:, None] / XPOS_BASE * jnp.log(zeta)[None, :])
    return jnp.cos(angles) * factor, jnp.sin(angles) * factor


def turn(values, tables):
    cosine, sine = tables
    half = values.shape[-1] // 2
    first, second = values[..., :half], values[..., half:]
    return jnp.concatenate(
        [first * cosine - second * sine, second * cosine + first * sine], axis=-1
    )


def turn_back(values, tables):
    cosine, sine = tables
    return turn(values, (cosine, -sine))


def mm(left, right):
    return jnp.einsum("sti,io->sto", left, right, preferred_element_type=F32)


def mm_back(left, right):
    return jnp.einsum("sto,io->sti", left, right, preferred_element_type=F32)


def mm_grad(left, right):
    return jnp.einsum("sti,sto->io", left, right, preferred_element_type=F32)


def after(value, *others):
    for other in others:
        value = value + (0.0 * other[(0,) * other.ndim].astype(F32)).astype(value.dtype)
    return value


def on_device(
    inputs,
    out_cotangent,
    doc_lengths,
    ln1_gain,
    w_query,
    w_key,
    w_value,
    w_gate,
    w_out,
    ln2_gain,
    w_up,
    up_bias,
    w_down,
):
    n_dph, n_dpl, n_pb, n_ka = (lax.axis_size(a) for a in ("dph", "dpl", "pb", "ka"))
    at_dpl, at_pb, at_ka = (lax.axis_index(a) for a in ("dpl", "pb", "ka"))
    batch, length, width = inputs.shape
    span = n_ka * length
    rows = w_query.shape[0]
    wide_rows = w_down.shape[0]
    key_width = w_query.shape[1] // H
    value_width = w_value.shape[1] // H
    units = n_dph * n_pb * wide_rows
    group = n_dpl * n_ka
    heads_pb = H // (n_dpl * n_dph)

    chunk = n_ka * rows

    def pick(values, order):
        return jnp.concatenate(
            [values[..., i * chunk : (i + 1) * chunk] for i in order], axis=-1
        )

    inner = [
        (d * n_dpl + r) * n_pb + p
        for d in range(n_dph)
        for p in range(n_pb)
        for r in range(n_dpl)
    ]

    def to_inner(values):
        return pick(values, inner)

    def to_outer(values):
        return pick(values, [inner.index(i) for i in range(len(inner))])

    def by_unit(weight):
        cut = weight.reshape(rows, n_dph, n_dpl, n_pb, n_ka, wide_rows)
        return jnp.transpose(cut, (2, 4, 0, 1, 3, 5)).reshape(group, rows, units)

    def from_unit(values):
        cut = values.reshape(n_dpl, n_ka, rows, n_dph, n_pb, wide_rows)
        return jnp.transpose(cut, (2, 3, 0, 4, 1, 5)).reshape(rows, -1)

    def gather_line(values):
        return lax.all_gather(values, LINE, axis=0, tiled=True)

    def scatter_line(values):
        return lax.psum_scatter(values, LINE, scatter_dimension=0, tiled=True)

    line = "dph" if n_dph > 1 else "pb"

    gain_one = ln1_gain.astype(BF16).astype(F32)[:, None]
    gain_two = ln2_gain.astype(BF16).astype(F32)[:, None]
    firsts = (w_query, w_key, w_value, w_gate)

    def head_of(j):
        r, c = j // n_ka, j % n_ka
        return (c // heads_pb) * (n_dpl * heads_pb) + r * heads_pb + c % heads_pb

    head_moves = [
        [(j, head_of(j) * size, place, size) for j in range(group)]
        for size, place in (
            (key_width, 0),
            (key_width, key_width),
            (value_width, 2 * key_width),
            (value_width, 0),
        )
    ]
    docs = jnp.pad(doc_lengths, ((0, 8 - batch), (0, 128 - doc_lengths.shape[1])))
    order = tuple(inner) if chunk % 128 == 0 else ()
    rows_in, rows_cot = inputs, out_cotangent
    if not order:
        rows_in, rows_cot = to_inner(inputs), to_inner(out_cotangent)
    out_in, down_in, up_in, unit_moves = w_out, w_down, w_up, []
    if order:
        moves = [(i * chunk, j * chunk, chunk) for j, i in enumerate(order)]
        for j in range(group):
            for q in range(n_dph * n_pb):
                block = (q // n_pb * n_dpl + j // n_ka) * n_pb + q % n_pb
                column = (block * n_ka + j % n_ka) * wide_rows
                unit_moves.append((j, column, q * wide_rows, wide_rows))
    else:
        moves = [(i * units, i * units, units) for i in range(width // units)]
        out_in, down_in = to_inner(w_out), to_inner(w_down)
        up_in = by_unit((w_up.astype(BF16).astype(F32) * gain_two).astype(BF16))
    normed_one_all, up_swapped, weight_qkv, gate_out, down_pack, docs_all = open_plane(
        firsts,
        gain_one,
        out_in,
        docs,
        rows_in,
        up_in,
        down_in,
        up_bias[None, :],
        gain_two,
        line,
        order,
        moves,
        unit_moves,
        head_moves,
        units,
        n_pb,
        0,
    )
    head = (
        (at_ka // heads_pb) * (n_dpl * heads_pb) + at_dpl * heads_pb + at_ka % heads_pb
    ).astype(F32)
    log_gamma = jnp.log(1.0 - jnp.exp2(-5.0 - head))
    offsets = jnp.arange(span, dtype=jnp.int32)
    places = (at_pb * span + offsets).astype(F32)
    tables_q = turn_tables(places, key_width // 2, 1.0)
    tables_k = turn_tables(places, key_width // 2, -1.0)
    distance = offsets[:, None] - offsets[None, :]
    decay = jnp.where(
        distance >= 0, jnp.exp(jnp.maximum(distance, 0).astype(F32) * log_gamma), 0.0
    )
    decay_in = jnp.exp(offsets.astype(F32) * log_gamma)[:, None]
    decay_out = jnp.exp((span - offsets).astype(F32) * log_gamma)[:, None]
    decay_span = jnp.exp(span * log_gamma)
    lengths = docs_all[:, :batch, : doc_lengths.shape[1]].reshape(n_dpl * batch, -1)
    ends = jnp.cumsum(lengths, axis=-1)
    edge = at_pb * span

    def goes_on(start):
        return jnp.all(ends != start, axis=-1).astype(F32)

    coef_forward = jnp.stack([goes_on(edge), jnp.full((n_dpl * batch,), decay_span)])
    coef_backward = jnp.stack([goes_on(edge + span), jnp.full((n_dpl * batch,), decay_span)])

    if n_dph > 1:
        weight_qkv = lax.all_gather(weight_qkv, "dph", axis=0, tiled=True)
    blocks = width // units
    gate_out = gather_line(gate_out)
    first = mm(normed_one_all, weight_qkv)
    query_pre = first[..., :key_width]
    key_pre = first[..., key_width : 2 * key_width]
    value = first[..., 2 * key_width :].astype(BF16)
    scale = key_width ** (-0.5)
    query = (turn(query_pre, tables_q) * scale).astype(BF16)
    key = turn(key_pre, tables_k).astype(BF16)
    key_out = (key.astype(F32) * decay_out).astype(BF16)
    state = jnp.einsum("smd,sme->sde", key_out, value, preferred_element_type=F32)
    carried, cot_all = line_scan(
        state, coef_forward, n_pb, True, order, 2, value, query, key, gathered=rows_cot
    )
    raw = jnp.einsum("snd,smd->snm", query, key, preferred_element_type=F32)
    scores = (raw * decay).astype(BF16)
    retained = jnp.einsum("snm,sme->sne", scores, value, preferred_element_type=F32)
    retained = retained + decay_in * jnp.einsum(
        "snd,sde->sne", query, carried, preferred_element_type=F32
    )
    normed_ret, inv_ret = normalize(retained)
    stride = gate_out.shape[0] // (n_dph * n_pb)
    spread = n_pb // heads_pb
    out_places = []
    for q in range(n_dph * n_pb):
        row = (q % spread * (n_dph * n_pb // spread) + q // spread) * wide_rows
        for i in range(blocks):
            source = q * stride + group * rows + i * wide_rows
            out_places.append((source, row, i * units, wide_rows))
    cut_out = gate_out.reshape(n_dph * n_pb, stride, units)
    bias_up = cut_out[:, stride - 16, :wide_rows].reshape(units).astype(F32)
    weight_up = gather_line(after(up_swapped.reshape(group * rows, -1), gate_out, inv_ret))
    weight_gate = after(cut_out[:, : group * rows].reshape(width, units), inv_ret)
    gate = mm(normed_one_all, weight_gate)
    gated = (gate * jax.nn.sigmoid(gate) * normed_ret).astype(BF16)
    weight_down = gather_line(after(down_pack, gated))
    gate_low = gate.astype(BF16)
    middle, normed_two_all, weight_out = plane_mix(
        gated, rows_in, gate_out, out_places, order, 3, scores, decay_in, decay_out
    )
    up_pre = mm(normed_two_all, weight_up) + bias_up
    bell = 0.5 * (1.0 + lax.erf(up_pre * np.float32(math.sqrt(0.5))))
    active = (up_pre * bell).astype(BF16)

    slope = bell + up_pre * (
        jnp.exp(-0.5 * up_pre * up_pre) * np.float32(1.0 / math.sqrt(2.0 * math.pi))
    )
    grad_up_pre = (mm_back(cot_all, weight_down) * slope).astype(BF16)
    ones = jnp.ones((n_dpl * batch, span, 128), BF16)
    grad_down = jnp.concatenate(
        [mm_grad(active, cot_all).astype(BF16), mm_grad(grad_up_pre, ones).astype(BF16)], axis=-1
    )
    grad_up = mm_grad(normed_two_all, grad_up_pre).astype(BF16)
    grad_middle, grad_mid_all = plane_turn(
        grad_up_pre, weight_up, middle, rows_cot, order, 5, grad_down, grad_up
    )
    grad_down = scatter_line(grad_down)
    grad_up = scatter_line(grad_up)
    grad_gated = after(mm_back(grad_mid_all, weight_out), grad_up)
    gate_again = gate_low.astype(F32)
    opened = jax.nn.sigmoid(gate_again)
    silu = gate_again * opened
    grad_gate = (grad_gated * normed_ret * (opened + silu * (1.0 - opened))).astype(BF16)
    grad_ret = normalize_back(normed_ret, inv_ret, grad_gated * silu).astype(BF16)
    query_in = (query.astype(F32) * decay_in).astype(BF16)
    grad_state = jnp.einsum("snd,sne->sde", query_in, grad_ret, preferred_element_type=F32)
    grad_out = after(mm_grad(gated, grad_mid_all), grad_down).astype(BF16)
    grad_out = (
        grad_out.reshape(n_pb // heads_pb, -1, wide_rows, width)
        .swapaxes(0, 1)
        .reshape(value_width, width)
    )
    grad_gate_w = mm_grad(normed_one_all, grad_gate).astype(BF16)
    _, output, *grad_parts = line_scan(
        grad_state,
        coef_backward,
        n_pb,
        False,
        order,
        7,
        grad_gate_w,
        grad_out,
        summed=(active, weight_down, middle),
        local=(
            query,
            key,
            value,
            grad_ret,
            scores,
            carried,
            decay,
            decay_in,
            decay_out,
            *tables_q,
            *tables_k,
        ),
    )
    grad_gate_w = scatter_line(grad_gate_w)
    grad_out = scatter_line(grad_out)
    grad_qkv = jnp.concatenate(grad_parts, axis=-1)
    grad_qkv_w = mm_grad(normed_one_all, after(grad_qkv, grad_gate_w)).astype(BF16)
    grad_qkv_sum = scatter_line(grad_qkv_w)
    cut = (group, rows, -1)
    grad_inputs, shard_gate, shard_up, sums_gate, sums_up, shard_down = plane_last(
        (*grad_parts, weight_qkv, grad_gate, weight_gate),
        rows_in,
        grad_middle,
        (grad_gate_w.reshape(cut), grad_up.reshape(cut)),
        (w_gate, w_up),
        (gain_one, gain_two),
        grad_down,
        (head_moves[3], unit_moves),
        order,
        8,
        grad_qkv_w,
    )
    if not order:
        output, grad_inputs, shard_down = (to_outer(a) for a in (output, grad_inputs, shard_down))
        shard_up = from_unit(shard_up).astype(F32)
        sums_up = jnp.sum(w_up.astype(BF16).astype(F32) * shard_up, axis=-1, keepdims=True)
        shard_up = gain_two * shard_up

    shard_query, shard_key, shard_value, shard_out, sums_qkv = plane_final(
        grad_qkv_sum.reshape(cut),
        grad_out,
        firsts[:3],
        gain_one,
        line,
        order,
        head_moves[:3],
        9,
        grad_inputs,
    )
    if not order:
        shard_out = to_outer(shard_out)
    shard_bias = grad_down[:, width].astype(F32)
    return (
        output,
        grad_inputs,
        (sums_qkv + sums_gate)[:, 0],
        shard_query,
        shard_key,
        shard_value,
        shard_gate,
        shard_out,
        sums_up[:, 0],
        shard_up,
        shard_bias,
        shard_down,
    )


def solution(mesh):
    dp, pb, ka = (mesh.shape[a] for a in ("dp", "pb", "ka"))
    fine = Mesh(mesh.devices.reshape(dp // 2, 2, pb, ka), ("dph", "dpl", "pb", "ka"))
    dp_axes = ("dph", "dpl")
    every = ("dph", "dpl", "pb", "ka")
    tokens = P(dp_axes, ("pb", "ka"), None)
    matrix = P(every, None)
    vector = P(every)
    return jax.shard_map(
        on_device,
        mesh=fine,
        in_specs=(
            tokens,
            tokens,
            P(dp_axes, None),
            vector,
            matrix,
            matrix,
            matrix,
            matrix,
            matrix,
            vector,
            matrix,
            vector,
            matrix,
        ),
        out_specs=(
            tokens,
            tokens,
            vector,
            matrix,
            matrix,
            matrix,
            matrix,
            matrix,
            vector,
            matrix,
            vector,
            matrix,
        ),
        check_vma=False,
    )
```

```python
import functools
import math

import jax
import jax.numpy as jnp
import numpy as np
from jax import lax
from jax.experimental import pallas as pl
from jax.experimental.pallas import tpu as pltpu
from jax.sharding import Mesh
from jax.sharding import PartitionSpec as P

H = 8
XPOS_BASE = 512.0
EPSILON = 1e-05
MESH = pl.DeviceIdType.MESH
F32 = jnp.float32
BF16 = jnp.bfloat16

PLANE = ("dpl", "ka")
LINE = ("dph", "pb")


def plane_ids():
    row = lax.axis_index("dpl")
    col = lax.axis_index("ka")
    other_row = 1 - row
    across = lax.rem(col + 2, 4)
    sibling = col + 1 - 2 * lax.rem(col, 2)
    return row, col, other_row, across, sibling


def greet(targets):
    barrier = pltpu.get_barrier_semaphore()
    for target in targets:
        pl.semaphore_signal(barrier, inc=1, device_id=target, device_id_type=MESH)
    pl.semaphore_wait(barrier, len(targets))


def gather_stages(shard, full, local_sem, send_sem, recv_sem, part=0, parts=1):
    batch, length, _ = shard.shape
    whole = length // parts
    first = part * whole
    half = whole // 2
    row, col, other_row, across, sibling = plane_ids()
    to_x = {"ka": across}
    to_y = {"dpl": other_row}
    to_s = {"ka": sibling}

    shard = shard.at[:, pl.ds(first, whole), :]

    def slot(r, c, start=0, size=whole):
        return full.at[pl.ds(r * batch, batch), pl.ds(c * length + first + start, size), :]

    def hop(index, target, dst, src=None):
        return pltpu.make_async_remote_copy(
            src_ref=dst if src is None else src,
            dst_ref=dst,
            send_sem=send_sem.at[part * 9 + index],
            recv_sem=recv_sem.at[part * 9 + index],
            device_id=target,
            device_id_type=MESH,
        )

    mine = pltpu.make_async_copy(shard, slot(row, col), local_sem.at[part])
    from_x = hop(0, to_x, slot(row, col), shard)
    from_y = hop(1, to_y, slot(row, col), shard)
    own_s = hop(2, to_s, slot(row, col), shard)
    diag_y = hop(3, to_y, slot(row, across, 0, half))
    relay_x = hop(4, to_s, slot(row, across))
    diag_x = hop(5, to_x, slot(other_row, col, half, half))
    relay_y = hop(6, to_s, slot(other_row, col))
    relay_a = hop(7, to_s, slot(other_row, across, 0, half))
    relay_b = hop(8, to_s, slot(other_row, across, half, half))

    def begin():
        from_x.start()
        from_y.start()
        own_s.start()
        mine.start()

    def relay():
        from_x.wait_recv()
        diag_y.start()
        relay_x.start()
        from_y.wait_recv()
        diag_x.start()
        relay_y.start()

    def diagonal():
        diag_y.wait_recv()
        relay_a.start()
        diag_x.wait_recv()
        relay_b.start()

    def end():
        for copy in (own_s, relay_x, relay_y, relay_a, relay_b):
            copy.wait_recv()
        for copy in (from_x, from_y, own_s, diag_y, relay_x, diag_x, relay_y, relay_a, relay_b):
            copy.wait_send()
        mine.wait()

    return (to_x, to_y, to_s), (begin, relay, diagonal, end)


GATHER_SCRATCH = (
    pltpu.SemaphoreType.DMA((2,)),
    pltpu.SemaphoreType.DMA((18,)),
    pltpu.SemaphoreType.DMA((18,)),
)


def gathered_shape(shard):
    batch, length, width = shard.shape
    return jax.ShapeDtypeStruct((2 * batch, 4 * length, width), shard.dtype)


def gather_kernel(shard, *refs):
    targets, stages = gather_stages(shard, *refs[-4:])
    greet(targets)
    for stage in stages:
        stage()


def read_rows(ref, b, at, order):
    if not order:
        return ref[b, at, :]
    size = ref.shape[-1] // len(order)
    return jnp.concatenate([ref[b, at, i * size : (i + 1) * size] for i in order], axis=-1)


def write_rows(ref, b, at, order, values):
    if not order:
        ref[b, at, :] = values
        return
    size = ref.shape[-1] // len(order)
    for j, i in enumerate(order):
        ref[b, at, i * size : (i + 1) * size] = values[:, j * size : (j + 1) * size]


def normalize_rows(source, target, order):
    batch, length, _ = source.shape
    step = 16

    def body(i, carry):
        at = pl.ds(i * step, step)
        for b in range(batch):
            normed, _ = normalize(read_rows(source, b, at, order).astype(F32))
            target[b, at, :] = normed.astype(BF16)
        return carry

    lax.fori_loop(0, length // step, body, 0)


def owners_stages(sources, targets, keep_sem, send_sem, recv_sem):
    row, col, other_row, _, _ = plane_ids()
    me = row * 4 + col
    peers = [(row, lax.rem(col + away, 4)) for away in (1, 2, 3)]
    peers += [(other_row, lax.rem(col + away, 4)) for away in (0, 1, 2, 3)]
    copies = []
    for a in range(len(sources)):
        copies.append(
            pltpu.make_async_copy(sources[a].at[me], targets[a](me), keep_sem.at[a])
        )
        for i in (6, 5, 4, 3, 2, 1, 0):
            r, c = peers[i]
            copies.append(
                pltpu.make_async_remote_copy(
                    src_ref=sources[a].at[r * 4 + c],
                    dst_ref=targets[a](me),
                    send_sem=send_sem.at[a, i],
                    recv_sem=recv_sem.at[a, i],
                    device_id={"dpl": r, "ka": c},
                    device_id_type=MESH,
                )
            )

    def begin():
        for copy in copies:
            copy.start()

    def end():
        for copy in copies:
            copy.wait()

    def arrive(r, c, across_rows):
        away = lax.rem(col - c + 4, 4)
        pltpu.make_async_remote_copy(
            src_ref=sources[0].at[me],
            dst_ref=targets[0](r * 4 + c),
            send_sem=send_sem.at[0, 0],
            recv_sem=recv_sem.at[0, away + 3 if across_rows else away - 1],
            device_id={"dpl": other_row, "ka": col},
            device_id_type=MESH,
        ).wait_recv()

    def leave():
        for copy in copies[1:]:
            copy.wait_send()

    near = (copies[0].wait, arrive, leave) if len(sources) == 1 else None
    return [{"dpl": r, "ka": c} for r, c in peers], (begin, end, near)


def blocks_of(ref):
    return lambda j: ref.at[j]


def owners_scratch(count):
    return [
        pltpu.SemaphoreType.DMA((count,)),
        pltpu.SemaphoreType.DMA((count, 7)),
        pltpu.SemaphoreType.DMA((count, 7)),
    ]


def trade_stages(line, source, target, sems):
    place, col = lax.axis_index(line), lax.axis_index("ka")
    moves = place != col
    partner = {line: col, "ka": place}

    def trade():
        return pltpu.make_async_remote_copy(
            src_ref=source,
            dst_ref=target,
            send_sem=sems.at[0],
            recv_sem=sems.at[1],
            device_id=partner,
            device_id_type=MESH,
        )

    def keep():
        return pltpu.make_async_copy(source, target, sems.at[2])

    def greet_partner(barrier):
        @pl.when(moves)
        def _():
            pl.semaphore_signal(barrier, inc=1, device_id=partner, device_id_type=MESH)

        return moves.astype(jnp.int32)

    def begin():
        @pl.when(moves)
        def _():
            trade().start()

        @pl.when(jnp.logical_not(moves))
        def _():
            keep().start()

    def end():
        @pl.when(moves)
        def _():
            trade().wait()

        @pl.when(jnp.logical_not(moves))
        def _():
            keep().wait()

    return greet_partner, (begin, end)


TRADE_SCRATCH = (pltpu.SemaphoreType.DMA((3,)),)


def line_gather_stages(count, chunks, full, send_sem, recv_sem):
    here = lax.axis_index("pb")
    rows = full.shape[0] // count
    size = rows // chunks

    def hop(up, distance, c):
        owner = here - distance if up else here + distance
        place = full.at[pl.ds(owner * rows + c * size, size)]
        return pltpu.make_async_remote_copy(
            src_ref=place,
            dst_ref=place,
            send_sem=send_sem.at[int(up), distance, c],
            recv_sem=recv_sem.at[int(up), distance, c],
            device_id={"pb": here + 1 if up else here - 1},
            device_id_type=MESH,
        )

    def sends(up, distance):
        if up:
            return jnp.logical_and(here >= distance, here < count - 1)
        return jnp.logical_and(here + distance <= count - 1, here > 0)

    def arrives(up, distance):
        return here >= distance if up else here + distance <= count - 1

    def step(distance, c):
        for up in (True, False):
            if distance > 0:

                @pl.when(arrives(up, distance))
                def _():
                    hop(up, distance - 1, c).wait_recv()

            if distance < count - 1:

                @pl.when(sends(up, distance))
                def _():
                    hop(up, distance, c).start()

    def finish():
        for distance in range(count - 1):
            for c in range(chunks):
                for up in (True, False):

                    @pl.when(sends(up, distance))
                    def _():
                        hop(up, distance, c).wait_send()

    return step, finish


def open_kernel(count, chunks, line, order, moves, unit_moves, head_moves, *refs):
    gain_one, docs, bias, gain_two = refs[4], refs[6], refs[10], refs[11]
    fetched = [i for i in range(10) if i not in (4, 6)]
    held, fetch_sem = refs[-9:-1], refs[-1]
    fetches = [
        pltpu.make_async_copy(refs[i], ref, fetch_sem.at[n])
        for n, (i, ref) in enumerate(zip(fetched, held))
    ]
    for copy in fetches:
        copy.start()
    refs = refs[:-9]
    weights, out, x, up, down = held[:4], *held[4:]
    normed_all, up_mine, first_all, gate_out, down_pack, docs_all = refs[-28:-22]
    qkv_pack, gate_pack, out_low, out_mine, normed, up_low, down_low, bias_low = refs[-22:-14]
    sems = refs[-14:]
    row, _, other_row, _, _ = plane_ids()
    here = lax.axis_index("pb")
    group, rows, _ = qkv_pack.shape

    def first_block(j):
        return first_all.at[pl.ds(here * (group * rows) + j * rows, rows)]

    def gate_block(j):
        return gate_out.at[pl.ds(j * rows, rows)]

    _, gather = gather_stages(normed, normed_all, *sems[:3])
    targets, first = owners_stages((qkv_pack,), (first_block,), *sems[3:6])
    _, second = owners_stages((gate_pack,), (gate_block,), *sems[6:9])
    _, third = owners_stages(
        (up_low if unit_moves else up,),
        (blocks_of(up_mine),),
        sems[9].at[pl.ds(0, 1)],
        sems[10].at[pl.ds(0, 1)],
        sems[10].at[pl.ds(1, 1)],
    )
    greet_partner, trade = trade_stages(line, out_low, out_mine, sems[9].at[pl.ds(1, 3)])
    step, finish = line_gather_stages(count, chunks, first_all, *sems[11:13])

    def pack(i, target):
        for j, column, place, size in head_moves[i]:
            block = weights[i][:, column : column + size].astype(BF16).astype(F32)
            target[j, :, place : place + size] = (block * gain_one[...]).astype(BF16)

    barrier = pltpu.get_barrier_semaphore()
    for target in targets:
        pl.semaphore_signal(barrier, inc=1, device_id=target, device_id_type=MESH)

    @pl.when(here > 0)
    def _():
        pl.semaphore_signal(barrier, inc=1, device_id={"pb": here - 1}, device_id_type=MESH)

    @pl.when(here < count - 1)
    def _():
        pl.semaphore_signal(barrier, inc=1, device_id={"pb": here + 1}, device_id_type=MESH)

    ends = (here > 0).astype(jnp.int32) + (here < count - 1).astype(jnp.int32)
    greeted = greet_partner(barrier) + len(targets) + ends
    for i in (0, 1, 2):
        fetches[i].wait()
        pack(i, qkv_pack)
    pl.semaphore_wait(barrier, greeted)
    first[0]()
    give = pltpu.make_async_remote_copy(
        src_ref=docs,
        dst_ref=docs_all.at[row],
        send_sem=sems[9].at[4],
        recv_sem=sems[9].at[5],
        device_id={"dpl": other_row},
        device_id_type=MESH,
    )
    keep = pltpu.make_async_copy(docs, docs_all.at[row], sems[9].at[6])
    give.start()
    keep.start()
    for copy in fetches[3:]:
        copy.wait()
    out_low[...] = out[...].astype(BF16)
    trade[0]()
    _, col, _, across, sibling = plane_ids()
    across_s = lax.rem(sibling + 2, 4)
    kept, arrive, leave = first[2]
    kept()
    arrive(row, sibling, False)
    nearest = [row * 2 + col // 2]
    step(0, nearest[0])
    for r, c, d, far in (
        (row, across, across_s, False),
        (other_row, col, sibling, True),
        (other_row, across, across_s, True),
    ):
        arrive(r, c, far)
        arrive(r, d, far)
        nearest.append(r * 2 + c // 2)
        step(0, nearest[-1])
    normalize_rows(x, normed, order)
    gather[0]()
    pack(3, gate_pack)
    second[0]()
    for j, source, target, size in unit_moves:
        block = up[:, source : source + size].astype(BF16).astype(F32) * gain_two[...]
        up_low[j, :, target : target + size] = block.astype(BF16)
    third[0]()
    lanes, wide = gate_out.shape[1], out.shape[0]
    for source, target, size in moves:
        down_low[:, target : target + size] = down[:, source : source + size].astype(BF16)
    bias_low[...] = jnp.zeros(bias_low.shape, BF16)
    bias_low[0:1, 0:wide] = bias[...].astype(BF16)
    trade[1]()
    edge = gate_out.shape[0] - bias_low.shape[0]
    pairs = [(down_low, down_pack), (bias_low, gate_out.at[pl.ds(edge, bias_low.shape[0])])]
    for source, target, size in moves:
        place = pl.ds(group * rows + target // lanes * wide, wide)
        pairs.append(
            (out_mine.at[:, pl.ds(source, size)], gate_out.at[place, pl.ds(target % lanes, size)])
        )
    copies = [pltpu.make_async_copy(a, b, sems[13].at[i]) for i, (a, b) in enumerate(pairs)]
    for copy in copies:
        copy.start()
    for c in nearest:
        step(1, c)
    gather[1]()
    for distance in range(2, count):
        for i, c in enumerate(nearest):
            step(distance, c)
            if distance == 2 and i == chunks // 2:
                gather[2]()
    leave()
    give.wait()
    keep.wait()
    for copy in copies:
        copy.wait()
    second[1]()
    gather[3]()
    third[1]()
    finish()


def open_plane(
    weights, gain_one, out, docs, x, up, down, bias, gain_two, line, order, moves, unit_moves, head_moves, units, count, collective_id
):
    chunks = 4
    group = len(head_moves[0])
    rows = gain_one.shape[0]
    first = sum(w.shape[1] for w in weights[:3]) // group
    edge = 16
    return pl.pallas_call(
        functools.partial(
            open_kernel, count, chunks, line, order, moves, unit_moves, head_moves
        ),
        out_shape=[
            gathered_shape(x),
            jax.ShapeDtypeStruct((group, rows, units), BF16),
            jax.ShapeDtypeStruct((count * group * rows, first), BF16),
            jax.ShapeDtypeStruct((group * rows + out.size // units + edge, units), BF16),
            jax.ShapeDtypeStruct(down.shape, BF16),
            jax.ShapeDtypeStruct((2,) + docs.shape, docs.dtype),
        ],
        in_specs=[ANY] * 4 + [VMEM, ANY, VMEM, ANY, ANY, ANY, VMEM, VMEM],
        out_specs=[ANY] * 6,
        scratch_shapes=[
            pltpu.VMEM((group, rows, first), BF16),
            pltpu.VMEM((group, rows, units), BF16),
            pltpu.VMEM(out.shape, BF16),
            pltpu.VMEM(out.shape, BF16),
            pltpu.VMEM(x.shape, BF16),
            pltpu.VMEM((group, rows, units), BF16),
            pltpu.VMEM(down.shape, BF16),
            pltpu.VMEM((edge, units), BF16),
            *GATHER_SCRATCH,
            *owners_scratch(1),
            *owners_scratch(1),
            pltpu.SemaphoreType.DMA((7,)),
            pltpu.SemaphoreType.DMA((2, 7)),
            pltpu.SemaphoreType.DMA((2, count, chunks)),
            pltpu.SemaphoreType.DMA((2, count, chunks)),
            pltpu.SemaphoreType.DMA((2 + len(moves),)),
            *[pltpu.VMEM(a.shape, a.dtype) for a in (*weights, out, x, up, down)],
            pltpu.SemaphoreType.DMA((8,)),
        ],
        compiler_params=pltpu.CompilerParams(
            collective_id=collective_id,
            has_side_effects=True,
            vmem_limit_bytes=60 * 1024 * 1024,
        ),
        name="open_plane",
    )(*weights, gain_one, out, docs, x, up, down, bias, gain_two)


def scatter_stages(
    terms, finish, sent, own, sib, from_x, from_y, diag_a, diag_b, sems, recvs, even=False
):
    _, batch, length, width = own.shape
    half = length // 2
    row, col, other_row, across, sibling = plane_ids()
    across_s = lax.rem(sibling + 2, 4)
    to_x = {"ka": across}
    to_y = {"dpl": other_row}
    to_s = {"ka": sibling}
    mine = ((other_row, across), (row, across), (other_row, col), (row, col))
    theirs = ((other_row, across_s), (row, across_s), (other_row, sibling), (row, sibling))
    lower, upper = pl.ds(0, half), pl.ds(half, half)
    step = 16
    tile = 512

    def hop(src, dst, index, target):
        return pltpu.make_async_remote_copy(
            src_ref=src,
            dst_ref=dst,
            send_sem=sems.at[index],
            recv_sem=recvs.at[index],
            device_id=target,
            device_id_type=MESH,
        )

    swaps = [hop(sent.at[j], sib.at[j], j, to_s) for j in range(1, 4)]
    heads = [
        hop(sent.at[0, :, part, :], sib.at[0, :, part, :], i, to_s)
        for part, i in ((lower, 0), (upper, 10))
    ]
    first_a = hop(own.at[0, :, lower, :], diag_a, 4, to_x)
    first_b = hop(own.at[0, :, upper, :], diag_b, 5, to_y)
    x_lower = hop(own.at[1, :, lower, :], from_x.at[:, lower, :], 6, to_x)
    y_upper = hop(own.at[2, :, upper, :], from_y.at[:, upper, :], 7, to_y)
    x_upper = hop(own.at[1, :, upper, :], from_x.at[:, upper, :], 8, to_x)
    y_lower = hop(own.at[2, :, lower, :], from_y.at[:, lower, :], 9, to_y)

    def make(r, c, out, start=0, size=length):
        def body(n, carry):
            columns = pl.ds(pl.multiple_of(n * tile, tile), tile)
            value = 0.0
            for left, right, flipped in terms:
                block = left[pl.ds(r * batch, batch), pl.ds(c * length + start, size), :]
                block = block.reshape(batch * size, left.shape[2])
                if flipped:
                    value = value + lax.dot_general(
                        block,
                        right[columns, :],
                        (((1,), (1,)), ((), ())),
                        preferred_element_type=F32,
                    )
                else:
                    value = value + jnp.dot(
                        block, right[:, columns], preferred_element_type=F32
                    )
            out[:, pl.ds(start, size), columns] = value.reshape(batch, size, tile).astype(BF16)
            return carry

        lax.fori_loop(0, width // tile, body, 0)

    def give(j):
        make(*theirs[j], sent.at[j])
        swaps[j - 1].start()

    def give_head(i):
        make(*theirs[0], sent.at[0], i * half, half)
        heads[i].start()

    def own_head(i):
        make(*mine[0], own.at[0], i * half, half)

    def merge_head(i):
        heads[i].wait_recv()
        add(own.at[0], i * half, ((own.at[0], i * half), (sib.at[0], i * half)), half)

    def add(out_ref, out_start, parts, size):
        def body(i, carry):
            value = 0.0
            for ref, start in parts:
                value = value + ref[:, pl.ds(start + i * step, step), :].astype(F32)
            out_ref[:, pl.ds(out_start + i * step, step), :] = value.astype(out_ref.dtype)
            return carry

        lax.fori_loop(0, size // step, body, 0)

    def merge(j):
        swaps[j - 1].wait_recv()
        add(own.at[j], 0, ((own.at[j], 0), (sib.at[j], 0)), length)

    def open_heads():
        give_head(0)
        own_head(0)
        give_head(1)

    def send_head():
        merge_head(0)
        first_a.start()
        own_head(1)

    def send_diag():
        merge_head(1)
        first_b.start()
        make(*mine[1], own.at[1])

    def send_x():
        merge(1)
        x_lower.start()
        make(*mine[2], own.at[2])

    def send_y():
        merge(2)
        if not even:
            y_upper.start()
        make(*mine[3], own.at[3])

    def stage_rest():
        if even:
            first_a.wait_recv()
            add(own.at[2], 0, ((own.at[2], 0), (diag_a, 0)), half)
            y_lower.start()
            y_upper.start()
        first_b.wait_recv()
        add(own.at[1], half, ((own.at[1], half), (diag_b, 0)), half)
        x_upper.start()
        if not even:
            first_a.wait_recv()
            add(own.at[2], 0, ((own.at[2], 0), (diag_a, 0)), half)
            y_lower.start()
        merge(3)

    def close(start):
        def body(i, carry):
            at = pl.ds(start + i * step, step)
            for b in range(batch):
                value = own[3, b, at, :].astype(F32)
                value = value + from_x[b, at, :].astype(F32) + from_y[b, at, :].astype(F32)
                finish(b, at, value)
            return carry

        lax.fori_loop(0, half // step, body, 0)

    def close_lower():
        x_lower.wait_recv()
        y_lower.wait_recv()
        close(0)

    def close_upper():
        y_upper.wait_recv()
        x_upper.wait_recv()
        close(half)
        for copy in (first_a, first_b, x_lower, x_upper, y_lower, y_upper):
            copy.wait_send()

    def stage_free():
        for copy in heads + swaps:
            copy.wait_send()

    stages = (
        open_heads,
        send_head,
        lambda: give(1),
        send_diag,
        lambda: give(2),
        send_x,
        lambda: give(3),
        send_y,
        stage_rest,
        close_lower,
        close_upper,
        stage_free,
    )
    return (to_x, to_y, to_s), stages


def scatter_scratch(shape):
    batch, length, width = shape
    return [
        pltpu.VMEM((4,) + shape, BF16),
        pltpu.VMEM((4,) + shape, BF16),
        pltpu.VMEM((4,) + shape, BF16),
        pltpu.VMEM(shape, BF16),
        pltpu.VMEM(shape, BF16),
        pltpu.VMEM((batch, length // 2, width), BF16),
        pltpu.VMEM((batch, length // 2, width), BF16),
        pltpu.SemaphoreType.DMA((11,)),
        pltpu.SemaphoreType.DMA((11,)),
    ]


VMEM = pl.BlockSpec(memory_space=pltpu.VMEM)
ANY = pl.BlockSpec(memory_space=pl.ANY)


def mix_kernel(order, places, gated, x, gate_out, *refs):
    middle, normed_all, weight, normed, load_sem = refs[-17:-12]
    loads = [
        pltpu.make_async_copy(
            gate_out.at[pl.ds(source, rows)],
            weight.at[pl.ds(row, rows), pl.ds(column, gate_out.shape[1])],
            load_sem.at[i],
        )
        for i, (source, row, column, rows) in enumerate(places)
    ]
    for load in loads:
        load.start()

    def finish(b, at, value):
        value = value + read_rows(x, b, at, order).astype(F32)
        middle[b, at, :] = value
        normed[b, at, :] = normalize(value)[0].astype(BF16)

    targets, stages = scatter_stages(((gated, weight, False),), finish, *refs[-12:-3], True)
    lower, upper = (gather_stages(normed, normed_all, *refs[-3:], i, 2)[1] for i in (0, 1))
    greet(targets)
    for load in loads:
        load.wait()
    for stage in stages[:10] + lower[:1] + stages[10:11] + upper[:1]:
        stage()
    for pair in zip(lower[1:], upper[1:]):
        for stage in pair:
            stage()
    stages[11]()


def plane_mix(gated, x, gate_out, places, order, collective_id, *before):
    shape = x.shape
    return pl.pallas_call(
        functools.partial(mix_kernel, order, places),
        out_shape=[
            jax.ShapeDtypeStruct(shape, F32),
            gathered_shape(x),
            jax.ShapeDtypeStruct((gated.shape[2], shape[2]), BF16),
        ],
        in_specs=[VMEM] * 2 + [ANY] * (1 + len(before)),
        out_specs=[VMEM, ANY, VMEM],
        scratch_shapes=[
            pltpu.VMEM(shape, BF16),
            pltpu.SemaphoreType.DMA((len(places),)),
            *scatter_scratch(shape),
            *GATHER_SCRATCH,
        ],
        compiler_params=pltpu.CompilerParams(
            collective_id=collective_id,
            has_side_effects=True,
            vmem_limit_bytes=48 * 1024 * 1024,
        ),
        name="plane_mix",
    )(gated, x, gate_out, *before)


def turn_kernel(order, grad, weight, middle, cot, *refs):
    grad_middle, grad_all, low = refs[-15:-12]

    def finish(b, at, value):
        normed, inv = normalize(middle[b, at, :])
        value = normalize_back(normed, inv, value)
        value = value + read_rows(cot, b, at, order).astype(F32)
        grad_middle[b, at, :] = value
        low[b, at, :] = value.astype(BF16)

    targets, stages = scatter_stages(((grad, weight, True),), finish, *refs[-12:-3], True)
    lower, upper = (gather_stages(low, grad_all, *refs[-3:], i, 2)[1] for i in (0, 1))
    greet(targets)
    for stage in stages[:10] + lower[:1] + stages[10:11] + upper[:1]:
        stage()
    for pair in zip(lower[1:], upper[1:]):
        for stage in pair:
            stage()
    stages[11]()


def plane_turn(grad, weight, middle, cot, order, collective_id, *before):
    shape = middle.shape
    return pl.pallas_call(
        functools.partial(turn_kernel, order),
        out_shape=[jax.ShapeDtypeStruct(shape, F32), gathered_shape(cot)],
        in_specs=[VMEM] * 4 + [ANY] * len(before),
        out_specs=[VMEM, ANY],
        scratch_shapes=[
            pltpu.VMEM(shape, BF16),
            *scatter_scratch(shape),
            *GATHER_SCRATCH,
        ],
        compiler_params=pltpu.CompilerParams(
            collective_id=collective_id,
            has_side_effects=True,
            vmem_limit_bytes=48 * 1024 * 1024,
        ),
        name="plane_turn",
    )(grad, weight, middle, cot, *before)


def put_back(landed, weight, gain, target, moves):
    total = 0.0
    for j, column, place, size in moves:
        value = landed[j, :, place : place + size].astype(F32)
        low = weight[:, column : column + size].astype(BF16).astype(F32)
        total = total + jnp.sum(low * value, axis=-1, keepdims=True)
        target[:, column : column + size] = gain[...] * value
    return total


def last_kernel(order, moves, *refs):
    parts, weight_a, grad_b, weight_b, x, grad_middle = refs[:3], *refs[3:8]
    owned, weights, gains = refs[8:10], refs[10:12], refs[12:14]
    grad_down = refs[14]
    scratch = refs[-14:]
    outs = refs[-20:-14]

    def finish(b, at, value):
        normed, inv = normalize(read_rows(x, b, at, order).astype(F32))
        value = grad_middle[b, at, :] + normalize_back(normed, inv, value)
        write_rows(outs[0], b, at, order, value)

    terms, place = [(grad_b, weight_b, True)], 0
    for part in parts:
        columns = pl.ds(place, part.shape[2])
        terms.append((part, weight_a.at[:, columns], True))
        place += part.shape[2]
    _, stages = scatter_stages(terms, finish, *scratch[:9])
    targets, owners = owners_stages(owned, [blocks_of(ref) for ref in scratch[9:11]], *scratch[11:14])
    greet(targets)
    for stage in owners[:1] + stages[:9]:
        stage()
    size = outs[5].shape[1] // max(len(order), 1)
    for j, i in enumerate(order or (0,)):
        block = grad_down[:, j * size : (j + 1) * size]
        outs[5][:, i * size : (i + 1) * size] = block.astype(F32)
    for stage in stages[9:] + owners[1:2]:
        stage()
    for i in (0, 1):
        if moves[i]:
            outs[3 + i][...] = put_back(scratch[9 + i], weights[i], gains[i], outs[1 + i], moves[i])
        else:
            outs[1 + i][...] = scratch[9 + i][...]
            outs[3 + i][...] = jnp.zeros(outs[3 + i].shape, F32)


def plane_last(
    terms, x, grad_middle, owned, weights, gains, grad_down, moves, order, collective_id, *before
):
    shape = x.shape
    column = jax.ShapeDtypeStruct(gains[0].shape, F32)
    plain = jax.ShapeDtypeStruct((grad_down.shape[0], shape[-1]), F32)
    return pl.pallas_call(
        functools.partial(last_kernel, order, moves),
        out_shape=[jax.ShapeDtypeStruct(shape, F32)]
        + [
            jax.ShapeDtypeStruct(w.shape, F32) if m else jax.ShapeDtypeStruct(o.shape, BF16)
            for o, w, m in zip(owned, weights, moves)
        ]
        + [column, column, plain],
        in_specs=[VMEM] * 8 + [ANY] * 2 + [VMEM] * 5 + [ANY] * len(before),
        out_specs=[VMEM] * 6,
        scratch_shapes=scatter_scratch(shape)
        + [pltpu.VMEM(o.shape, BF16) for o in owned]
        + owners_scratch(2),
        compiler_params=pltpu.CompilerParams(
            collective_id=collective_id,
            has_side_effects=True,
            vmem_limit_bytes=58 * 1024 * 1024,
        ),
        name="plane_last",
    )(*terms, x, grad_middle, *owned, *weights, *gains, grad_down, *before)


def scan_kernel(count, forward, cuts, gathers, order, state, coef, *refs):
    if gathers:
        moved = refs[0]
        total, result, message, landed, send_sem, recv_sem = refs[-11:-5]
        shard, shard_sem = refs[-5:-3]
        targets, stages = gather_stages(shard, result, *refs[-3:])
    else:
        left, right, middle = refs[:3]
        query, key, value, grad, scores, carried = refs[3:9]
        decay, decay_in, decay_out, cos_q, sin_q, cos_k, sin_k = refs[9:16]
        total, result, out_q, out_k, out_v = refs[-20:-15]
        sum_k, sum_v, message, landed, send_sem, recv_sem = refs[-15:-9]
        scale = query.shape[2] ** (-0.5)

        def dot(a, b, contract):
            return lax.dot_general(
                a, b, ((contract[:1], contract[1:]), ((), ())), preferred_element_type=F32
            )

        def within(s):
            low = (dot(grad[s], value[s], (1, 1)) * decay[...]).astype(BF16)
            part = dot(low, key[s], (1, 0))
            part = part + decay_in[...] * dot(grad[s], carried[s], (1, 1))
            part = turn_back(part, (cos_q[...], sin_q[...]))
            out_q[s] = (part * scale).astype(BF16)
            sum_k[s] = dot(low, query[s], (0, 0))
            sum_v[s] = dot(scores[s], grad[s], (0, 0))

        def across(s):
            part = sum_k[s] + decay_out[...] * dot(value[s], total[s], (1, 1))
            out_k[s] = turn_back(part, (cos_k[...], sin_k[...])).astype(BF16)
            part = sum_v[s] + decay_out[...] * dot(key[s], total[s], (1, 0))
            out_v[s] = part.astype(BF16)

        def finish(b, at, value):
            write_rows(result, b, at, order, (middle[b, at, :] + value).astype(BF16))

        targets, stages = scatter_stages(((left, right, False),), finish, *refs[-9:])
    here = lax.axis_index("pb")
    place = here if forward else count - 1 - here
    step = 1 if forward else -1
    has_prev = place > 0
    has_next = place < count - 1
    barrier = pltpu.get_barrier_semaphore()

    @pl.when(has_prev)
    def _():
        pl.semaphore_signal(barrier, inc=1, device_id={"pb": here - step}, device_id_type=MESH)

    @pl.when(has_next)
    def _():
        pl.semaphore_signal(barrier, inc=1, device_id={"pb": here + step}, device_id_type=MESH)

    greeted = has_prev.astype(jnp.int32) + has_next.astype(jnp.int32)
    for target in targets:
        pl.semaphore_signal(barrier, inc=1, device_id=target, device_id_type=MESH)
    pl.semaphore_wait(barrier, greeted + len(targets))

    height = state.shape[1] // cuts
    pieces = [(s, c) for s in range(state.shape[0]) for c in range(cuts)]

    def hop(i):
        s, c = pieces[i]
        rows = pl.ds(c * height, height)
        return pltpu.make_async_remote_copy(
            src_ref=message.at[s, rows],
            dst_ref=landed.at[s, rows],
            send_sem=send_sem.at[i],
            recv_sem=recv_sem.at[i],
            device_id={"pb": here + step},
            device_id_type=MESH,
        )

    def emit(i):
        s, c = pieces[i]
        rows = pl.ds(c * height, height)

        @pl.when(jnp.logical_not(has_prev))
        def _():
            message[s, rows] = state[s, rows].astype(BF16)
            hop(i).start()
            total[s, rows] = jnp.zeros((height, state.shape[2]), BF16)

        @pl.when(has_prev)
        def _():
            hop(i).wait_recv()
            total[s, rows] = (coef[0, s] * landed[s, rows].astype(F32)).astype(BF16)

            @pl.when(has_next)
            def _():
                message[s, rows] = (
                    state[s, rows] + coef[1, s] * total[s, rows].astype(F32)
                ).astype(BF16)
                hop(i).start()

    emit(0)
    if gathers:
        size = shard.shape[-1] // max(len(order), 1)
        for move in (0, 1):
            for j, i in enumerate(order or (0,)):
                copy = pltpu.make_async_copy(
                    moved.at[:, :, pl.ds(i * size, size)],
                    shard.at[:, :, pl.ds(j * size, size)],
                    shard_sem.at[j],
                )
                if move:
                    copy.wait()
                else:
                    copy.start()
        stages[0]()
    count = len(pieces)
    if gathers:
        jobs = {count // 2: stages[1:2], 3 * count // 4: stages[2:3]}
        rest = stages[3:]
    else:
        jobs = {i + 1: [stage] for i, stage in enumerate(stages[:8])}
        seqs = range(state.shape[0])
        inner = [functools.partial(within, s) for s in seqs]
        outer = [functools.partial(across, s) for s in seqs]
        late = [*inner[:3], stages[8], *inner[3:]]
        for i, job in enumerate(late):
            jobs.setdefault(min(9 + i, count - 1), []).append(job)
        rest = [*outer[:-1], *stages[9:], *outer[-1:]]
    for i in range(1, count):
        emit(i)
        for job in jobs.get(i, ()):
            job()
    for job in rest:
        job()

    @pl.when(has_next)
    def _():
        for i in range(len(pieces)):
            hop(i).wait_send()


def line_scan(state, coef, count, forward, order, collective_id, *before, gathered=None, summed=(), local=()):
    cuts = 4
    pieces = state.shape[0] * cuts
    scratch = [
        pltpu.VMEM(state.shape, BF16),
        pltpu.VMEM(state.shape, BF16),
        pltpu.SemaphoreType.DMA((pieces,)),
        pltpu.SemaphoreType.DMA((pieces,)),
    ]
    gathers = gathered is not None
    shapes = [jax.ShapeDtypeStruct(state.shape, BF16)]
    if gathers:
        operands, specs = (gathered,), [ANY]
        shapes.append(gathered_shape(gathered))
        outs = [VMEM, ANY]
        scratch += [
            pltpu.VMEM(gathered.shape, gathered.dtype),
            pltpu.SemaphoreType.DMA((max(len(order), 1),)),
            *GATHER_SCRATCH,
        ]
    else:
        operands = (*summed, *local)
        specs = [VMEM] * len(operands)
        shapes.append(jax.ShapeDtypeStruct(summed[2].shape, BF16))
        shapes += [jax.ShapeDtypeStruct(local[i].shape, BF16) for i in range(3)]
        outs = [VMEM] * 5
        scratch = [pltpu.VMEM(local[i].shape, F32) for i in (1, 2)] + scratch
        scratch += scatter_scratch(summed[2].shape)
    return pl.pallas_call(
        functools.partial(scan_kernel, count, forward, cuts, gathers, order),
        out_shape=shapes,
        in_specs=[VMEM, pl.BlockSpec(memory_space=pltpu.SMEM)] + specs + [ANY] * len(before),
        out_specs=outs,
        scratch_shapes=scratch,
        compiler_params=pltpu.CompilerParams(
            collective_id=collective_id,
            has_side_effects=True,
            vmem_limit_bytes=(16 if gathers else 58) * 1024 * 1024,
        ),
        name="line_scan",
    )(state, coef, *operands, *before)


def final_kernel(line, order, heads_pb, moves, grad, grad_out, *refs):
    weights, gain = refs[:3], refs[3]
    outs, out_out, sums, landed, out_landed = refs[-11:-8], refs[-8], refs[-7], refs[-6], refs[-5]
    targets, stages = owners_stages((grad,), (blocks_of(landed),), *refs[-4:-1])
    greet_partner, trade = trade_stages(line, grad_out, out_landed, refs[-1])
    row, col, other_row, across, sibling = plane_ids()
    across_s = lax.rem(sibling + 2, 4)
    barrier = pltpu.get_barrier_semaphore()
    for target in targets:
        pl.semaphore_signal(barrier, inc=1, device_id=target, device_id_type=MESH)
    pl.semaphore_wait(barrier, greet_partner(barrier) + len(targets))
    stages[0]()
    trade[0]()
    kept, arrive, leave = stages[2]

    def place(r, c):
        head = (c // heads_pb) * (2 * heads_pb) + r * heads_pb + lax.rem(c, heads_pb)
        total = 0.0
        for weight, target, blocks in zip(weights, outs, moves):
            _, _, start, size = blocks[0]
            columns = pl.ds(pl.multiple_of(head * size, size), size)
            value = landed[r * 4 + c, :, start : start + size].astype(F32)
            low = weight[:, columns].astype(BF16).astype(F32)
            target[:, columns] = gain[...] * value
            total = total + jnp.sum(low * value, axis=-1, keepdims=True)
        return total

    kept()
    total = place(row, col)
    for r, c, far in (
        (row, sibling, False),
        (row, across, False),
        (other_row, col, True),
        (row, across_s, False),
        (other_row, sibling, True),
        (other_row, across, True),
        (other_row, across_s, True),
    ):
        arrive(r, c, far)
        total = total + place(r, c)
    sums[...] = total
    trade[1]()
    size = out_out.shape[1] // max(len(order), 1)
    for j, i in enumerate(order or (0,)):
        block = out_landed[:, j * size : (j + 1) * size]
        out_out[:, i * size : (i + 1) * size] = block.astype(F32)
    leave()


def plane_final(
    grad, grad_out, weights, gain, line, order, heads_pb, moves, collective_id, *before
):
    return pl.pallas_call(
        functools.partial(final_kernel, line, order, heads_pb, moves),
        out_shape=[jax.ShapeDtypeStruct(w.shape, F32) for w in weights]
        + [
            jax.ShapeDtypeStruct(grad_out.shape, F32),
            jax.ShapeDtypeStruct(gain.shape, F32),
        ],
        in_specs=[ANY] * 2 + [VMEM] * 4 + [ANY] * len(before),
        out_specs=[VMEM] * 5,
        scratch_shapes=[pltpu.VMEM(grad.shape, BF16), pltpu.VMEM(grad_out.shape, BF16)]
        + owners_scratch(1)
        + list(TRADE_SCRATCH),
        compiler_params=pltpu.CompilerParams(
            collective_id=collective_id,
            has_side_effects=True,
            vmem_limit_bytes=20 * 1024 * 1024,
        ),
        name="plane_final",
    )(grad, grad_out, *weights, gain, *before)


def normalize(values):
    mean = jnp.mean(values, axis=-1, keepdims=True)
    centered = values - mean
    inv = lax.rsqrt(jnp.mean(centered * centered, axis=-1, keepdims=True) + EPSILON)
    return centered * inv, inv


def normalize_back(normed, inv, grad):
    mean = jnp.mean(grad, axis=-1, keepdims=True)
    along = jnp.mean(grad * normed, axis=-1, keepdims=True)
    return inv * (grad - mean - normed * along)


def turn_tables(positions, half, direction):
    pair = jnp.arange(half, dtype=F32)
    frequency = jnp.exp(-jnp.log(10000.0) * pair / half)
    zeta = (pair / half + 0.4) / 1.4
    angles = positions[:, None] * frequency[None, :]
    factor = jnp.exp(direction * positions[:, None] / XPOS_BASE * jnp.log(zeta)[None, :])
    return jnp.cos(angles) * factor, jnp.sin(angles) * factor


def turn(values, tables):
    cosine, sine = tables
    half = values.shape[-1] // 2
    first, second = values[..., :half], values[..., half:]
    return jnp.concatenate(
        [first * cosine - second * sine, second * cosine + first * sine], axis=-1
    )


def turn_back(values, tables):
    cosine, sine = tables
    return turn(values, (cosine, -sine))


def mm(left, right):
    return jnp.einsum("sti,io->sto", left, right, preferred_element_type=F32)


def mm_back(left, right):
    return jnp.einsum("sto,io->sti", left, right, preferred_element_type=F32)


def mm_grad(left, right):
    return jnp.einsum("sti,sto->io", left, right, preferred_element_type=F32)


def after(value, *others):
    for other in others:
        value = value + (0.0 * other[(0,) * other.ndim].astype(F32)).astype(value.dtype)
    return value


def on_device(
    inputs,
    out_cotangent,
    doc_lengths,
    ln1_gain,
    w_query,
    w_key,
    w_value,
    w_gate,
    w_out,
    ln2_gain,
    w_up,
    up_bias,
    w_down,
):
    n_dph, n_dpl, n_pb, n_ka = (lax.axis_size(a) for a in ("dph", "dpl", "pb", "ka"))
    at_dpl, at_pb, at_ka = (lax.axis_index(a) for a in ("dpl", "pb", "ka"))
    batch, length, width = inputs.shape
    span = n_ka * length
    rows = w_query.shape[0]
    wide_rows = w_down.shape[0]
    key_width = w_query.shape[1] // H
    value_width = w_value.shape[1] // H
    units = n_dph * n_pb * wide_rows
    group = n_dpl * n_ka
    heads_pb = H // (n_dpl * n_dph)

    chunk = n_ka * rows

    def pick(values, order):
        return jnp.concatenate(
            [values[..., i * chunk : (i + 1) * chunk] for i in order], axis=-1
        )

    inner = [
        (d * n_dpl + r) * n_pb + p
        for d in range(n_dph)
        for p in range(n_pb)
        for r in range(n_dpl)
    ]

    def to_inner(values):
        return pick(values, inner)

    def to_outer(values):
        return pick(values, [inner.index(i) for i in range(len(inner))])

    def by_unit(weight):
        cut = weight.reshape(rows, n_dph, n_dpl, n_pb, n_ka, wide_rows)
        return jnp.transpose(cut, (2, 4, 0, 1, 3, 5)).reshape(group, rows, units)

    def from_unit(values):
        cut = values.reshape(n_dpl, n_ka, rows, n_dph, n_pb, wide_rows)
        return jnp.transpose(cut, (2, 3, 0, 4, 1, 5)).reshape(rows, -1)

    def gather_line(values):
        return lax.all_gather(values, LINE, axis=0, tiled=True)

    def scatter_line(values):
        return lax.psum_scatter(values, LINE, scatter_dimension=0, tiled=True)

    line = "dph" if n_dph > 1 else "pb"

    gain_one = ln1_gain.astype(BF16).astype(F32)[:, None]
    gain_two = ln2_gain.astype(BF16).astype(F32)[:, None]
    firsts = (w_query, w_key, w_value, w_gate)

    def head_of(j):
        r, c = j // n_ka, j % n_ka
        return (c // heads_pb) * (n_dpl * heads_pb) + r * heads_pb + c % heads_pb

    head_moves = [
        [(j, head_of(j) * size, place, size) for j in range(group)]
        for size, place in (
            (key_width, 0),
            (key_width, key_width),
            (value_width, 2 * key_width),
            (value_width, 0),
        )
    ]
    docs = jnp.pad(doc_lengths, ((0, 8 - batch), (0, 128 - doc_lengths.shape[1])))
    order = tuple(inner) if chunk % 128 == 0 else ()
    rows_in, rows_cot = inputs, out_cotangent
    if not order:
        rows_in, rows_cot = to_inner(inputs), to_inner(out_cotangent)
    out_in, down_in, up_in, unit_moves = w_out, w_down, w_up, []
    if order:
        moves = [(i * chunk, j * chunk, chunk) for j, i in enumerate(order)]
        for j in range(group):
            for q in range(n_dph * n_pb):
                block = (q // n_pb * n_dpl + j // n_ka) * n_pb + q % n_pb
                column = (block * n_ka + j % n_ka) * wide_rows
                unit_moves.append((j, column, q * wide_rows, wide_rows))
    else:
        moves = [(i * units, i * units, units) for i in range(width // units)]
        out_in, down_in = to_inner(w_out), to_inner(w_down)
        up_in = by_unit((w_up.astype(BF16).astype(F32) * gain_two).astype(BF16))
    normed_one_all, up_swapped, weight_qkv, gate_out, down_pack, docs_all = open_plane(
        firsts,
        gain_one,
        out_in,
        docs,
        rows_in,
        up_in,
        down_in,
        up_bias[None, :],
        gain_two,
        line,
        order,
        moves,
        unit_moves,
        head_moves,
        units,
        n_pb,
        0,
    )
    head = (
        (at_ka // heads_pb) * (n_dpl * heads_pb) + at_dpl * heads_pb + at_ka % heads_pb
    ).astype(F32)
    log_gamma = jnp.log(1.0 - jnp.exp2(-5.0 - head))
    offsets = jnp.arange(span, dtype=jnp.int32)
    places = (at_pb * span + offsets).astype(F32)
    tables_q = turn_tables(places, key_width // 2, 1.0)
    tables_k = turn_tables(places, key_width // 2, -1.0)
    distance = offsets[:, None] - offsets[None, :]
    decay = jnp.where(
        distance >= 0, jnp.exp(jnp.maximum(distance, 0).astype(F32) * log_gamma), 0.0
    )
    decay_in = jnp.exp(offsets.astype(F32) * log_gamma)[:, None]
    decay_out = jnp.exp((span - offsets).astype(F32) * log_gamma)[:, None]
    decay_span = jnp.exp(span * log_gamma)
    lengths = docs_all[:, :batch, : doc_lengths.shape[1]].reshape(n_dpl * batch, -1)
    ends = jnp.cumsum(lengths, axis=-1)
    edge = at_pb * span

    def goes_on(start):
        return jnp.all(ends != start, axis=-1).astype(F32)

    coef_forward = jnp.stack([goes_on(edge), jnp.full((n_dpl * batch,), decay_span)])
    coef_backward = jnp.stack([goes_on(edge + span), jnp.full((n_dpl * batch,), decay_span)])

    if n_dph > 1:
        weight_qkv = lax.all_gather(weight_qkv, "dph", axis=0, tiled=True)
    blocks = width // units
    gate_out = gather_line(gate_out)
    first = mm(normed_one_all, weight_qkv)
    query_pre = first[..., :key_width]
    key_pre = first[..., key_width : 2 * key_width]
    value = first[..., 2 * key_width :].astype(BF16)
    scale = key_width ** (-0.5)
    query = (turn(query_pre, tables_q) * scale).astype(BF16)
    key = turn(key_pre, tables_k).astype(BF16)
    key_out = (key.astype(F32) * decay_out).astype(BF16)
    state = jnp.einsum("smd,sme->sde", key_out, value, preferred_element_type=F32)
    carried, cot_all = line_scan(
        state, coef_forward, n_pb, True, order, 2, value, query, key, gathered=rows_cot
    )
    raw = jnp.einsum("snd,smd->snm", query, key, preferred_element_type=F32)
    scores = (raw * decay).astype(BF16)
    retained = jnp.einsum("snm,sme->sne", scores, value, preferred_element_type=F32)
    retained = retained + decay_in * jnp.einsum(
        "snd,sde->sne", query, carried, preferred_element_type=F32
    )
    normed_ret, inv_ret = normalize(retained)
    stride = gate_out.shape[0] // (n_dph * n_pb)
    spread = n_pb // heads_pb
    out_places = []
    for q in range(n_dph * n_pb):
        row = (q % spread * (n_dph * n_pb // spread) + q // spread) * wide_rows
        for i in range(blocks):
            source = q * stride + group * rows + i * wide_rows
            out_places.append((source, row, i * units, wide_rows))
    cut_out = gate_out.reshape(n_dph * n_pb, stride, units)
    bias_up = cut_out[:, stride - 16, :wide_rows].reshape(units).astype(F32)
    weight_up = gather_line(after(up_swapped.reshape(group * rows, -1), gate_out, inv_ret))
    weight_gate = after(cut_out[:, : group * rows].reshape(width, units), inv_ret)
    gate = mm(normed_one_all, weight_gate)
    gated = (gate * jax.nn.sigmoid(gate) * normed_ret).astype(BF16)
    weight_down = gather_line(after(down_pack, gated))
    gate_low = gate.astype(BF16)
    middle, normed_two_all, weight_out = plane_mix(
        gated, rows_in, gate_out, out_places, order, 3, scores, decay_in, decay_out
    )
    up_pre = mm(normed_two_all, weight_up) + bias_up
    bell = 0.5 * (1.0 + lax.erf(up_pre * np.float32(math.sqrt(0.5))))
    active = (up_pre * bell).astype(BF16)

    slope = bell + up_pre * (
        jnp.exp(-0.5 * up_pre * up_pre) * np.float32(1.0 / math.sqrt(2.0 * math.pi))
    )
    grad_up_pre = (mm_back(cot_all, weight_down) * slope).astype(BF16)
    ones = jnp.ones((n_dpl * batch, span, 128), BF16)
    grad_down = jnp.concatenate(
        [mm_grad(active, cot_all).astype(BF16), mm_grad(grad_up_pre, ones).astype(BF16)], axis=-1
    )
    grad_up = mm_grad(normed_two_all, grad_up_pre).astype(BF16)
    grad_middle, grad_mid_all = plane_turn(
        grad_up_pre, weight_up, middle, rows_cot, order, 5, grad_down, grad_up
    )
    grad_down = scatter_line(grad_down)
    grad_up = scatter_line(grad_up)
    grad_gated = after(mm_back(grad_mid_all, weight_out), grad_up)
    gate_again = gate_low.astype(F32)
    opened = jax.nn.sigmoid(gate_again)
    silu = gate_again * opened
    grad_gate = (grad_gated * normed_ret * (opened + silu * (1.0 - opened))).astype(BF16)
    grad_ret = normalize_back(normed_ret, inv_ret, grad_gated * silu).astype(BF16)
    query_in = (query.astype(F32) * decay_in).astype(BF16)
    grad_state = jnp.einsum("snd,sne->sde", query_in, grad_ret, preferred_element_type=F32)
    grad_out = after(mm_grad(gated, grad_mid_all), grad_down).astype(BF16)
    grad_out = (
        grad_out.reshape(n_pb // heads_pb, -1, wide_rows, width)
        .swapaxes(0, 1)
        .reshape(value_width, width)
    )
    grad_gate_w = mm_grad(normed_one_all, grad_gate).astype(BF16)
    _, output, *grad_parts = line_scan(
        grad_state,
        coef_backward,
        n_pb,
        False,
        order,
        7,
        grad_gate_w,
        grad_out,
        summed=(active, weight_down, middle),
        local=(
            query,
            key,
            value,
            grad_ret,
            scores,
            carried,
            decay,
            decay_in,
            decay_out,
            *tables_q,
            *tables_k,
        ),
    )
    grad_gate_w = scatter_line(grad_gate_w)
    grad_out = scatter_line(grad_out)
    grad_qkv = jnp.concatenate(grad_parts, axis=-1)
    grad_qkv_w = mm_grad(normed_one_all, after(grad_qkv, grad_gate_w)).astype(BF16)
    grad_qkv_sum = scatter_line(grad_qkv_w)
    cut = (group, rows, -1)
    grad_inputs, shard_gate, shard_up, sums_gate, sums_up, shard_down = plane_last(
        (*grad_parts, weight_qkv, grad_gate, weight_gate),
        rows_in,
        grad_middle,
        (grad_gate_w.reshape(cut), grad_up.reshape(cut)),
        (w_gate, w_up),
        (gain_one, gain_two),
        grad_down,
        (head_moves[3], unit_moves),
        order,
        8,
        grad_qkv_w,
    )
    if not order:
        output, grad_inputs, shard_down = (to_outer(a) for a in (output, grad_inputs, shard_down))
        shard_up = from_unit(shard_up).astype(F32)
        sums_up = jnp.sum(w_up.astype(BF16).astype(F32) * shard_up, axis=-1, keepdims=True)
        shard_up = gain_two * shard_up

    output, grad_inputs, shard_gate, shard_up, shard_down = (
        after(a, sums_gate) for a in (output, grad_inputs, shard_gate, shard_up, shard_down)
    )

    shard_query, shard_key, shard_value, shard_out, sums_qkv = plane_final(
        grad_qkv_sum.reshape(cut),
        grad_out,
        firsts[:3],
        gain_one,
        line,
        order,
        heads_pb,
        head_moves[:3],
        9,
        sums_gate,
    )
    if not order:
        shard_out = to_outer(shard_out)
    shard_bias = grad_down[:, width].astype(F32)
    return (
        output,
        grad_inputs,
        (sums_qkv + sums_gate)[:, 0],
        shard_query,
        shard_key,
        shard_value,
        shard_gate,
        shard_out,
        sums_up[:, 0],
        shard_up,
        shard_bias,
        shard_down,
    )


def solution(mesh):
    dp, pb, ka = (mesh.shape[a] for a in ("dp", "pb", "ka"))
    fine = Mesh(mesh.devices.reshape(dp // 2, 2, pb, ka), ("dph", "dpl", "pb", "ka"))
    dp_axes = ("dph", "dpl")
    every = ("dph", "dpl", "pb", "ka")
    tokens = P(dp_axes, ("pb", "ka"), None)
    matrix = P(every, None)
    vector = P(every)
    return jax.shard_map(
        on_device,
        mesh=fine,
        in_specs=(
            tokens,
            tokens,
            P(dp_axes, None),
            vector,
            matrix,
            matrix,
            matrix,
            matrix,
            matrix,
            vector,
            matrix,
            vector,
            matrix,
        ),
        out_specs=(
            tokens,
            tokens,
            vector,
            matrix,
            matrix,
            matrix,
            matrix,
            matrix,
            vector,
            matrix,
            vector,
            matrix,
        ),
        check_vma=False,
    )
```

```python
import functools
import math

import jax
import jax.numpy as jnp
import numpy as np
from jax import lax
from jax.experimental import pallas as pl
from jax.experimental.pallas import tpu as pltpu
from jax.sharding import Mesh
from jax.sharding import PartitionSpec as P

H = 8
XPOS_BASE = 512.0
EPSILON = 1e-05
MESH = pl.DeviceIdType.MESH
F32 = jnp.float32
BF16 = jnp.bfloat16

PLANE = ("dpl", "ka")
LINE = ("dph", "pb")


def plane_ids():
    row = lax.axis_index("dpl")
    col = lax.axis_index("ka")
    other_row = 1 - row
    across = lax.rem(col + 2, 4)
    sibling = col + 1 - 2 * lax.rem(col, 2)
    return row, col, other_row, across, sibling


def greet(targets):
    barrier = pltpu.get_barrier_semaphore()
    for target in targets:
        pl.semaphore_signal(barrier, inc=1, device_id=target, device_id_type=MESH)
    pl.semaphore_wait(barrier, len(targets))


def gather_stages(shard, full, local_sem, send_sem, recv_sem, part=0, parts=1):
    batch, length, _ = shard.shape
    whole = length // parts
    first = part * whole
    half = whole // 2
    row, col, other_row, across, sibling = plane_ids()
    to_x = {"ka": across}
    to_y = {"dpl": other_row}
    to_s = {"ka": sibling}

    shard = shard.at[:, pl.ds(first, whole), :]

    def slot(r, c, start=0, size=whole):
        return full.at[pl.ds(r * batch, batch), pl.ds(c * length + first + start, size), :]

    def hop(index, target, dst, src=None):
        return pltpu.make_async_remote_copy(
            src_ref=dst if src is None else src,
            dst_ref=dst,
            send_sem=send_sem.at[part * 9 + index],
            recv_sem=recv_sem.at[part * 9 + index],
            device_id=target,
            device_id_type=MESH,
        )

    mine = pltpu.make_async_copy(shard, slot(row, col), local_sem.at[part])
    from_x = hop(0, to_x, slot(row, col), shard)
    from_y = hop(1, to_y, slot(row, col), shard)
    own_s = hop(2, to_s, slot(row, col), shard)
    diag_y = hop(3, to_y, slot(row, across, 0, half))
    relay_x = hop(4, to_s, slot(row, across))
    diag_x = hop(5, to_x, slot(other_row, col, half, half))
    relay_y = hop(6, to_s, slot(other_row, col))
    relay_a = hop(7, to_s, slot(other_row, across, 0, half))
    relay_b = hop(8, to_s, slot(other_row, across, half, half))

    def begin():
        from_x.start()
        from_y.start()
        own_s.start()
        mine.start()

    def relay():
        from_x.wait_recv()
        diag_y.start()
        relay_x.start()
        from_y.wait_recv()
        diag_x.start()
        relay_y.start()

    def diagonal():
        diag_y.wait_recv()
        relay_a.start()
        diag_x.wait_recv()
        relay_b.start()

    def end():
        for copy in (own_s, relay_x, relay_y, relay_a, relay_b):
            copy.wait_recv()
        for copy in (from_x, from_y, own_s, diag_y, relay_x, diag_x, relay_y, relay_a, relay_b):
            copy.wait_send()
        mine.wait()

    return (to_x, to_y, to_s), (begin, relay, diagonal, end)


GATHER_SCRATCH = (
    pltpu.SemaphoreType.DMA((2,)),
    pltpu.SemaphoreType.DMA((18,)),
    pltpu.SemaphoreType.DMA((18,)),
)


def gathered_shape(shard):
    batch, length, width = shard.shape
    return jax.ShapeDtypeStruct((2 * batch, 4 * length, width), shard.dtype)


def gather_kernel(shard, *refs):
    targets, stages = gather_stages(shard, *refs[-4:])
    greet(targets)
    for stage in stages:
        stage()


def read_rows(ref, b, at, order):
    if not order:
        return ref[b, at, :]
    size = ref.shape[-1] // len(order)
    return jnp.concatenate([ref[b, at, i * size : (i + 1) * size] for i in order], axis=-1)


def write_rows(ref, b, at, order, values):
    if not order:
        ref[b, at, :] = values
        return
    size = ref.shape[-1] // len(order)
    for j, i in enumerate(order):
        ref[b, at, i * size : (i + 1) * size] = values[:, j * size : (j + 1) * size]


def normalize_rows(source, target, order):
    batch, length, _ = source.shape
    step = 16

    def body(i, carry):
        at = pl.ds(i * step, step)
        for b in range(batch):
            normed, _ = normalize(read_rows(source, b, at, order).astype(F32))
            target[b, at, :] = normed.astype(BF16)
        return carry

    lax.fori_loop(0, length // step, body, 0)


def owners_stages(sources, targets, keep_sem, send_sem, recv_sem):
    row, col, other_row, _, _ = plane_ids()
    me = row * 4 + col
    peers = [(row, lax.rem(col + away, 4)) for away in (1, 2, 3)]
    peers += [(other_row, lax.rem(col + away, 4)) for away in (0, 1, 2, 3)]
    copies = []
    for a in range(len(sources)):
        copies.append(
            pltpu.make_async_copy(sources[a].at[me], targets[a](me), keep_sem.at[a])
        )
        for i in (6, 5, 4, 3, 2, 1, 0):
            r, c = peers[i]
            copies.append(
                pltpu.make_async_remote_copy(
                    src_ref=sources[a].at[r * 4 + c],
                    dst_ref=targets[a](me),
                    send_sem=send_sem.at[a, i],
                    recv_sem=recv_sem.at[a, i],
                    device_id={"dpl": r, "ka": c},
                    device_id_type=MESH,
                )
            )

    def begin():
        for copy in copies:
            copy.start()

    def end():
        for copy in copies:
            copy.wait()

    def arrive(r, c, across_rows):
        away = lax.rem(col - c + 4, 4)
        pltpu.make_async_remote_copy(
            src_ref=sources[0].at[me],
            dst_ref=targets[0](r * 4 + c),
            send_sem=send_sem.at[0, 0],
            recv_sem=recv_sem.at[0, away + 3 if across_rows else away - 1],
            device_id={"dpl": other_row, "ka": col},
            device_id_type=MESH,
        ).wait_recv()

    def leave():
        for copy in copies[1:]:
            copy.wait_send()

    near = (copies[0].wait, arrive, leave) if len(sources) == 1 else None
    return [{"dpl": r, "ka": c} for r, c in peers], (begin, end, near)


def blocks_of(ref):
    return lambda j: ref.at[j]


def owners_scratch(count):
    return [
        pltpu.SemaphoreType.DMA((count,)),
        pltpu.SemaphoreType.DMA((count, 7)),
        pltpu.SemaphoreType.DMA((count, 7)),
    ]


def trade_stages(line, source, target, sems):
    place, col = lax.axis_index(line), lax.axis_index("ka")
    moves = place != col
    partner = {line: col, "ka": place}

    def trade():
        return pltpu.make_async_remote_copy(
            src_ref=source,
            dst_ref=target,
            send_sem=sems.at[0],
            recv_sem=sems.at[1],
            device_id=partner,
            device_id_type=MESH,
        )

    def keep():
        return pltpu.make_async_copy(source, target, sems.at[2])

    def greet_partner(barrier):
        @pl.when(moves)
        def _():
            pl.semaphore_signal(barrier, inc=1, device_id=partner, device_id_type=MESH)

        return moves.astype(jnp.int32)

    def begin():
        @pl.when(moves)
        def _():
            trade().start()

        @pl.when(jnp.logical_not(moves))
        def _():
            keep().start()

    def end():
        @pl.when(moves)
        def _():
            trade().wait()

        @pl.when(jnp.logical_not(moves))
        def _():
            keep().wait()

    return greet_partner, (begin, end)


TRADE_SCRATCH = (pltpu.SemaphoreType.DMA((3,)),)


def line_gather_stages(count, chunks, full, send_sem, recv_sem):
    here = lax.axis_index("pb")
    rows = full.shape[0] // count
    size = rows // chunks

    def hop(up, distance, c):
        owner = here - distance if up else here + distance
        place = full.at[pl.ds(owner * rows + c * size, size)]
        return pltpu.make_async_remote_copy(
            src_ref=place,
            dst_ref=place,
            send_sem=send_sem.at[int(up), distance, c],
            recv_sem=recv_sem.at[int(up), distance, c],
            device_id={"pb": here + 1 if up else here - 1},
            device_id_type=MESH,
        )

    def sends(up, distance):
        if up:
            return jnp.logical_and(here >= distance, here < count - 1)
        return jnp.logical_and(here + distance <= count - 1, here > 0)

    def arrives(up, distance):
        return here >= distance if up else here + distance <= count - 1

    def step(distance, c):
        for up in (True, False):
            if distance > 0:

                @pl.when(arrives(up, distance))
                def _():
                    hop(up, distance - 1, c).wait_recv()

            if distance < count - 1:

                @pl.when(sends(up, distance))
                def _():
                    hop(up, distance, c).start()

    def finish():
        for distance in range(count - 1):
            for c in range(chunks):
                for up in (True, False):

                    @pl.when(sends(up, distance))
                    def _():
                        hop(up, distance, c).wait_send()

    return step, finish


def open_kernel(count, chunks, line, order, moves, unit_moves, head_moves, *refs):
    gain_one, docs, bias, gain_two = refs[4], refs[6], refs[10], refs[11]
    fetched = [i for i in range(10) if i not in (4, 6)]
    held, fetch_sem = refs[-9:-1], refs[-1]
    fetches = [
        pltpu.make_async_copy(refs[i], ref, fetch_sem.at[n])
        for n, (i, ref) in enumerate(zip(fetched, held))
    ]
    for copy in fetches:
        copy.start()
    refs = refs[:-9]
    weights, out, x, up, down = held[:4], *held[4:]
    normed_all, up_mine, first_all, gate_out, down_pack, docs_all = refs[-28:-22]
    qkv_pack, gate_pack, out_low, out_mine, normed, up_low, down_low, bias_low = refs[-22:-14]
    sems = refs[-14:]
    row, _, other_row, _, _ = plane_ids()
    here = lax.axis_index("pb")
    group, rows, _ = qkv_pack.shape

    def first_block(j):
        return first_all.at[pl.ds(here * (group * rows) + j * rows, rows)]

    def gate_block(j):
        return gate_out.at[pl.ds(j * rows, rows)]

    _, gather = gather_stages(normed, normed_all, *sems[:3])
    targets, first = owners_stages((qkv_pack,), (first_block,), *sems[3:6])
    _, second = owners_stages((gate_pack,), (gate_block,), *sems[6:9])
    _, third = owners_stages(
        (up_low if unit_moves else up,),
        (blocks_of(up_mine),),
        sems[9].at[pl.ds(0, 1)],
        sems[10].at[pl.ds(0, 1)],
        sems[10].at[pl.ds(1, 1)],
    )
    greet_partner, trade = trade_stages(line, out_low, out_mine, sems[9].at[pl.ds(1, 3)])
    step, finish = line_gather_stages(count, chunks, first_all, *sems[11:13])

    def pack(i, target):
        for j, column, place, size in head_moves[i]:
            block = weights[i][:, column : column + size].astype(BF16).astype(F32)
            target[j, :, place : place + size] = (block * gain_one[...]).astype(BF16)

    barrier = pltpu.get_barrier_semaphore()
    for target in targets:
        pl.semaphore_signal(barrier, inc=1, device_id=target, device_id_type=MESH)

    @pl.when(here > 0)
    def _():
        pl.semaphore_signal(barrier, inc=1, device_id={"pb": here - 1}, device_id_type=MESH)

    @pl.when(here < count - 1)
    def _():
        pl.semaphore_signal(barrier, inc=1, device_id={"pb": here + 1}, device_id_type=MESH)

    ends = (here > 0).astype(jnp.int32) + (here < count - 1).astype(jnp.int32)
    greeted = greet_partner(barrier) + len(targets) + ends
    for i in (0, 1, 2):
        fetches[i].wait()
        pack(i, qkv_pack)
    pl.semaphore_wait(barrier, greeted)
    first[0]()
    give = pltpu.make_async_remote_copy(
        src_ref=docs,
        dst_ref=docs_all.at[row],
        send_sem=sems[9].at[4],
        recv_sem=sems[9].at[5],
        device_id={"dpl": other_row},
        device_id_type=MESH,
    )
    keep = pltpu.make_async_copy(docs, docs_all.at[row], sems[9].at[6])
    give.start()
    keep.start()
    for copy in fetches[3:]:
        copy.wait()
    out_low[...] = out[...].astype(BF16)
    trade[0]()
    _, col, _, across, sibling = plane_ids()
    across_s = lax.rem(sibling + 2, 4)
    kept, arrive, leave = first[2]
    kept()
    arrive(row, sibling, False)
    nearest = [row * 2 + col // 2]
    step(0, nearest[0])
    for r, c, d, far in (
        (row, across, across_s, False),
        (other_row, col, sibling, True),
        (other_row, across, across_s, True),
    ):
        arrive(r, c, far)
        arrive(r, d, far)
        nearest.append(r * 2 + c // 2)
        step(0, nearest[-1])
    normalize_rows(x, normed, order)
    gather[0]()
    pack(3, gate_pack)
    second[0]()
    for j, source, target, size in unit_moves:
        block = up[:, source : source + size].astype(BF16).astype(F32) * gain_two[...]
        up_low[j, :, target : target + size] = block.astype(BF16)
    third[0]()
    lanes, wide = gate_out.shape[1], out.shape[0]
    for source, target, size in moves:
        down_low[:, target : target + size] = down[:, source : source + size].astype(BF16)
    bias_low[...] = jnp.zeros(bias_low.shape, BF16)
    bias_low[0:1, 0:wide] = bias[...].astype(BF16)
    trade[1]()
    edge = gate_out.shape[0] - bias_low.shape[0]
    pairs = [(down_low, down_pack), (bias_low, gate_out.at[pl.ds(edge, bias_low.shape[0])])]
    for source, target, size in moves:
        place = pl.ds(group * rows + target // lanes * wide, wide)
        pairs.append(
            (out_mine.at[:, pl.ds(source, size)], gate_out.at[place, pl.ds(target % lanes, size)])
        )
    copies = [pltpu.make_async_copy(a, b, sems[13].at[i]) for i, (a, b) in enumerate(pairs)]
    for copy in copies:
        copy.start()
    for c in nearest:
        step(1, c)
    gather[1]()
    for distance in range(2, count):
        for i, c in enumerate(nearest):
            step(distance, c)
            if distance == 2 and i == chunks // 2:
                gather[2]()
    leave()
    give.wait()
    keep.wait()
    for copy in copies:
        copy.wait()
    second[1]()
    gather[3]()
    third[1]()
    finish()


def open_plane(
    weights, gain_one, out, docs, x, up, down, bias, gain_two, line, order, moves, unit_moves, head_moves, units, count, collective_id
):
    chunks = 4
    group = len(head_moves[0])
    rows = gain_one.shape[0]
    first = sum(w.shape[1] for w in weights[:3]) // group
    edge = 16
    return pl.pallas_call(
        functools.partial(
            open_kernel, count, chunks, line, order, moves, unit_moves, head_moves
        ),
        out_shape=[
            gathered_shape(x),
            jax.ShapeDtypeStruct((group, rows, units), BF16),
            jax.ShapeDtypeStruct((count * group * rows, first), BF16),
            jax.ShapeDtypeStruct((group * rows + out.size // units + edge, units), BF16),
            jax.ShapeDtypeStruct(down.shape, BF16),
            jax.ShapeDtypeStruct((2,) + docs.shape, docs.dtype),
        ],
        in_specs=[ANY] * 4 + [VMEM, ANY, VMEM, ANY, ANY, ANY, VMEM, VMEM],
        out_specs=[ANY] * 6,
        scratch_shapes=[
            pltpu.VMEM((group, rows, first), BF16),
            pltpu.VMEM((group, rows, units), BF16),
            pltpu.VMEM(out.shape, BF16),
            pltpu.VMEM(out.shape, BF16),
            pltpu.VMEM(x.shape, BF16),
            pltpu.VMEM((group, rows, units), BF16),
            pltpu.VMEM(down.shape, BF16),
            pltpu.VMEM((edge, units), BF16),
            *GATHER_SCRATCH,
            *owners_scratch(1),
            *owners_scratch(1),
            pltpu.SemaphoreType.DMA((7,)),
            pltpu.SemaphoreType.DMA((2, 7)),
            pltpu.SemaphoreType.DMA((2, count, chunks)),
            pltpu.SemaphoreType.DMA((2, count, chunks)),
            pltpu.SemaphoreType.DMA((2 + len(moves),)),
            *[pltpu.VMEM(a.shape, a.dtype) for a in (*weights, out, x, up, down)],
            pltpu.SemaphoreType.DMA((8,)),
        ],
        compiler_params=pltpu.CompilerParams(
            collective_id=collective_id,
            has_side_effects=True,
            vmem_limit_bytes=60 * 1024 * 1024,
        ),
        name="open_plane",
    )(*weights, gain_one, out, docs, x, up, down, bias, gain_two)


def scatter_stages(
    terms, finish, sent, own, sib, from_x, from_y, diag_a, diag_b, sems, recvs, even=False
):
    _, batch, length, width = own.shape
    half = length // 2
    row, col, other_row, across, sibling = plane_ids()
    across_s = lax.rem(sibling + 2, 4)
    to_x = {"ka": across}
    to_y = {"dpl": other_row}
    to_s = {"ka": sibling}
    mine = ((other_row, across), (row, across), (other_row, col), (row, col))
    theirs = ((other_row, across_s), (row, across_s), (other_row, sibling), (row, sibling))
    lower, upper = pl.ds(0, half), pl.ds(half, half)
    step = 16
    tile = 512

    def hop(src, dst, index, target):
        return pltpu.make_async_remote_copy(
            src_ref=src,
            dst_ref=dst,
            send_sem=sems.at[index],
            recv_sem=recvs.at[index],
            device_id=target,
            device_id_type=MESH,
        )

    swaps = [hop(sent.at[j], sib.at[j], j, to_s) for j in range(1, 4)]
    heads = [
        hop(sent.at[0, :, part, :], sib.at[0, :, part, :], i, to_s)
        for part, i in ((lower, 0), (upper, 10))
    ]
    first_a = hop(own.at[0, :, lower, :], diag_a, 4, to_x)
    first_b = hop(own.at[0, :, upper, :], diag_b, 5, to_y)
    x_lower = hop(own.at[1, :, lower, :], from_x.at[:, lower, :], 6, to_x)
    y_upper = hop(own.at[2, :, upper, :], from_y.at[:, upper, :], 7, to_y)
    x_upper = hop(own.at[1, :, upper, :], from_x.at[:, upper, :], 8, to_x)
    y_lower = hop(own.at[2, :, lower, :], from_y.at[:, lower, :], 9, to_y)

    def make(r, c, out, start=0, size=length):
        def body(n, carry):
            columns = pl.ds(pl.multiple_of(n * tile, tile), tile)
            value = 0.0
            for left, right, flipped in terms:
                block = left[pl.ds(r * batch, batch), pl.ds(c * length + start, size), :]
                block = block.reshape(batch * size, left.shape[2])
                if flipped:
                    value = value + lax.dot_general(
                        block,
                        right[columns, :],
                        (((1,), (1,)), ((), ())),
                        preferred_element_type=F32,
                    )
                else:
                    value = value + jnp.dot(
                        block, right[:, columns], preferred_element_type=F32
                    )
            out[:, pl.ds(start, size), columns] = value.reshape(batch, size, tile).astype(BF16)
            return carry

        lax.fori_loop(0, width // tile, body, 0)

    def give(j):
        make(*theirs[j], sent.at[j])
        swaps[j - 1].start()

    def give_head(i):
        make(*theirs[0], sent.at[0], i * half, half)
        heads[i].start()

    def own_head(i):
        make(*mine[0], own.at[0], i * half, half)

    def merge_head(i):
        heads[i].wait_recv()
        add(own.at[0], i * half, ((own.at[0], i * half), (sib.at[0], i * half)), half)

    def add(out_ref, out_start, parts, size):
        def body(i, carry):
            value = 0.0
            for ref, start in parts:
                value = value + ref[:, pl.ds(start + i * step, step), :].astype(F32)
            out_ref[:, pl.ds(out_start + i * step, step), :] = value.astype(out_ref.dtype)
            return carry

        lax.fori_loop(0, size // step, body, 0)

    def merge(j):
        swaps[j - 1].wait_recv()
        add(own.at[j], 0, ((own.at[j], 0), (sib.at[j], 0)), length)

    def open_heads():
        give_head(0)
        own_head(0)
        give_head(1)

    def send_head():
        merge_head(0)
        first_a.start()
        own_head(1)

    def send_diag():
        merge_head(1)
        first_b.start()
        make(*mine[1], own.at[1])

    def send_x():
        merge(1)
        x_lower.start()
        make(*mine[2], own.at[2])

    def send_y():
        merge(2)
        if not even:
            y_upper.start()
        make(*mine[3], own.at[3])

    def stage_rest():
        if even:
            first_a.wait_recv()
            add(own.at[2], 0, ((own.at[2], 0), (diag_a, 0)), half)
            y_lower.start()
            y_upper.start()
        first_b.wait_recv()
        add(own.at[1], half, ((own.at[1], half), (diag_b, 0)), half)
        x_upper.start()
        if not even:
            first_a.wait_recv()
            add(own.at[2], 0, ((own.at[2], 0), (diag_a, 0)), half)
            y_lower.start()
        merge(3)

    def close(start):
        def body(i, carry):
            at = pl.ds(start + i * step, step)
            for b in range(batch):
                value = own[3, b, at, :].astype(F32)
                value = value + from_x[b, at, :].astype(F32) + from_y[b, at, :].astype(F32)
                finish(b, at, value)
            return carry

        lax.fori_loop(0, half // step, body, 0)

    def close_lower():
        x_lower.wait_recv()
        y_lower.wait_recv()
        close(0)

    def close_upper():
        y_upper.wait_recv()
        x_upper.wait_recv()
        close(half)
        for copy in (first_a, first_b, x_lower, x_upper, y_lower, y_upper):
            copy.wait_send()

    def stage_free():
        for copy in heads + swaps:
            copy.wait_send()

    stages = (
        open_heads,
        send_head,
        lambda: give(1),
        send_diag,
        lambda: give(2),
        send_x,
        lambda: give(3),
        send_y,
        stage_rest,
        close_lower,
        close_upper,
        stage_free,
    )
    return (to_x, to_y, to_s), stages


def scatter_scratch(shape):
    batch, length, width = shape
    return [
        pltpu.VMEM((4,) + shape, BF16),
        pltpu.VMEM((4,) + shape, BF16),
        pltpu.VMEM((4,) + shape, BF16),
        pltpu.VMEM(shape, BF16),
        pltpu.VMEM(shape, BF16),
        pltpu.VMEM((batch, length // 2, width), BF16),
        pltpu.VMEM((batch, length // 2, width), BF16),
        pltpu.SemaphoreType.DMA((11,)),
        pltpu.SemaphoreType.DMA((11,)),
    ]


VMEM = pl.BlockSpec(memory_space=pltpu.VMEM)
ANY = pl.BlockSpec(memory_space=pl.ANY)


def mix_kernel(order, places, gated, x, gate_out, *refs):
    middle, normed_all, weight, normed, load_sem = refs[-17:-12]
    loads = [
        pltpu.make_async_copy(
            gate_out.at[pl.ds(source, rows)],
            weight.at[pl.ds(row, rows), pl.ds(column, gate_out.shape[1])],
            load_sem.at[i],
        )
        for i, (source, row, column, rows) in enumerate(places)
    ]
    for load in loads:
        load.start()

    def finish(b, at, value):
        value = value + read_rows(x, b, at, order).astype(F32)
        middle[b, at, :] = value
        normed[b, at, :] = normalize(value)[0].astype(BF16)

    targets, stages = scatter_stages(((gated, weight, False),), finish, *refs[-12:-3], True)
    lower, upper = (gather_stages(normed, normed_all, *refs[-3:], i, 2)[1] for i in (0, 1))
    greet(targets)
    for load in loads:
        load.wait()
    for stage in stages[:10] + lower[:1] + stages[10:11] + upper[:1]:
        stage()
    for pair in zip(lower[1:], upper[1:]):
        for stage in pair:
            stage()
    stages[11]()


def plane_mix(gated, x, gate_out, places, order, collective_id, *before):
    shape = x.shape
    return pl.pallas_call(
        functools.partial(mix_kernel, order, places),
        out_shape=[
            jax.ShapeDtypeStruct(shape, F32),
            gathered_shape(x),
            jax.ShapeDtypeStruct((gated.shape[2], shape[2]), BF16),
        ],
        in_specs=[VMEM] * 2 + [ANY] * (1 + len(before)),
        out_specs=[VMEM, ANY, VMEM],
        scratch_shapes=[
            pltpu.VMEM(shape, BF16),
            pltpu.SemaphoreType.DMA((len(places),)),
            *scatter_scratch(shape),
            *GATHER_SCRATCH,
        ],
        compiler_params=pltpu.CompilerParams(
            collective_id=collective_id,
            has_side_effects=True,
            vmem_limit_bytes=48 * 1024 * 1024,
        ),
        name="plane_mix",
    )(gated, x, gate_out, *before)


def turn_kernel(order, grad, weight, middle, cot, *refs):
    grad_middle, grad_all, low = refs[-15:-12]

    def finish(b, at, value):
        normed, inv = normalize(middle[b, at, :])
        value = normalize_back(normed, inv, value)
        value = value + read_rows(cot, b, at, order).astype(F32)
        grad_middle[b, at, :] = value
        low[b, at, :] = value.astype(BF16)

    targets, stages = scatter_stages(((grad, weight, True),), finish, *refs[-12:-3], True)
    lower, upper = (gather_stages(low, grad_all, *refs[-3:], i, 2)[1] for i in (0, 1))
    greet(targets)
    for stage in stages[:10] + lower[:1] + stages[10:11] + upper[:1]:
        stage()
    for pair in zip(lower[1:], upper[1:]):
        for stage in pair:
            stage()
    stages[11]()


def plane_turn(grad, weight, middle, cot, order, collective_id, *before):
    shape = middle.shape
    return pl.pallas_call(
        functools.partial(turn_kernel, order),
        out_shape=[jax.ShapeDtypeStruct(shape, F32), gathered_shape(cot)],
        in_specs=[VMEM] * 4 + [ANY] * len(before),
        out_specs=[VMEM, ANY],
        scratch_shapes=[
            pltpu.VMEM(shape, BF16),
            *scatter_scratch(shape),
            *GATHER_SCRATCH,
        ],
        compiler_params=pltpu.CompilerParams(
            collective_id=collective_id,
            has_side_effects=True,
            vmem_limit_bytes=48 * 1024 * 1024,
        ),
        name="plane_turn",
    )(grad, weight, middle, cot, *before)


def put_back(landed, weight, gain, target, moves):
    total = 0.0
    for j, column, place, size in moves:
        value = landed[j, :, place : place + size].astype(F32)
        low = weight[:, column : column + size].astype(BF16).astype(F32)
        total = total + jnp.sum(low * value, axis=-1, keepdims=True)
        target[:, column : column + size] = gain[...] * value
    return total


def last_kernel(order, moves, *refs):
    parts, weight_a, grad_b, weight_b, x, grad_middle = refs[:3], *refs[3:8]
    owned, weights, gains = refs[8:10], refs[10:12], refs[12:14]
    grad_down = refs[14]
    scratch = refs[-14:]
    outs = refs[-20:-14]

    def finish(b, at, value):
        normed, inv = normalize(read_rows(x, b, at, order).astype(F32))
        value = grad_middle[b, at, :] + normalize_back(normed, inv, value)
        write_rows(outs[0], b, at, order, value)

    terms, place = [(grad_b, weight_b, True)], 0
    for part in parts:
        columns = pl.ds(place, part.shape[2])
        terms.append((part, weight_a.at[:, columns], True))
        place += part.shape[2]
    _, stages = scatter_stages(terms, finish, *scratch[:9])
    targets, owners = owners_stages(owned, [blocks_of(ref) for ref in scratch[9:11]], *scratch[11:14])
    greet(targets)
    for stage in owners[:1] + stages[:9]:
        stage()
    size = outs[5].shape[1] // max(len(order), 1)
    for j, i in enumerate(order or (0,)):
        block = grad_down[:, j * size : (j + 1) * size]
        outs[5][:, i * size : (i + 1) * size] = block.astype(F32)
    for stage in stages[9:] + owners[1:2]:
        stage()
    for i in (0, 1):
        if moves[i]:
            outs[3 + i][...] = put_back(scratch[9 + i], weights[i], gains[i], outs[1 + i], moves[i])
        else:
            outs[1 + i][...] = scratch[9 + i][...]
            outs[3 + i][...] = jnp.zeros(outs[3 + i].shape, F32)


def plane_last(
    terms, x, grad_middle, owned, weights, gains, grad_down, moves, order, collective_id, *before
):
    shape = x.shape
    column = jax.ShapeDtypeStruct(gains[0].shape, F32)
    plain = jax.ShapeDtypeStruct((grad_down.shape[0], shape[-1]), F32)
    return pl.pallas_call(
        functools.partial(last_kernel, order, moves),
        out_shape=[jax.ShapeDtypeStruct(shape, F32)]
        + [
            jax.ShapeDtypeStruct(w.shape, F32) if m else jax.ShapeDtypeStruct(o.shape, BF16)
            for o, w, m in zip(owned, weights, moves)
        ]
        + [column, column, plain],
        in_specs=[VMEM] * 8 + [ANY] * 2 + [VMEM] * 5 + [ANY] * len(before),
        out_specs=[VMEM] * 6,
        scratch_shapes=scatter_scratch(shape)
        + [pltpu.VMEM(o.shape, BF16) for o in owned]
        + owners_scratch(2),
        compiler_params=pltpu.CompilerParams(
            collective_id=collective_id,
            has_side_effects=True,
            vmem_limit_bytes=58 * 1024 * 1024,
        ),
        name="plane_last",
    )(*terms, x, grad_middle, *owned, *weights, *gains, grad_down, *before)


def scan_kernel(count, forward, cuts, gathers, order, state, coef, *refs):
    if gathers:
        moved = refs[0]
        total, result, message, landed, send_sem, recv_sem = refs[-11:-5]
        shard, shard_sem = refs[-5:-3]
        targets, stages = gather_stages(shard, result, *refs[-3:])
    else:
        left, right, middle = refs[:3]
        query, key, value, grad, scores, carried = refs[3:9]
        decay, decay_in, decay_out, cos_q, sin_q, cos_k, sin_k = refs[9:16]
        total, result, out_q, out_k, out_v = refs[-20:-15]
        sum_k, sum_v, message, landed, send_sem, recv_sem = refs[-15:-9]
        scale = query.shape[2] ** (-0.5)

        def dot(a, b, contract):
            return lax.dot_general(
                a, b, ((contract[:1], contract[1:]), ((), ())), preferred_element_type=F32
            )

        def within(s):
            low = (dot(grad[s], value[s], (1, 1)) * decay[...]).astype(BF16)
            part = dot(low, key[s], (1, 0))
            part = part + decay_in[...] * dot(grad[s], carried[s], (1, 1))
            part = turn_back(part, (cos_q[...], sin_q[...]))
            out_q[s] = (part * scale).astype(BF16)
            sum_k[s] = dot(low, query[s], (0, 0))
            sum_v[s] = dot(scores[s], grad[s], (0, 0))

        def across(s):
            part = sum_k[s] + decay_out[...] * dot(value[s], total[s], (1, 1))
            out_k[s] = turn_back(part, (cos_k[...], sin_k[...])).astype(BF16)
            part = sum_v[s] + decay_out[...] * dot(key[s], total[s], (1, 0))
            out_v[s] = part.astype(BF16)

        def finish(b, at, value):
            write_rows(result, b, at, order, (middle[b, at, :] + value).astype(BF16))

        targets, stages = scatter_stages(((left, right, False),), finish, *refs[-9:])
    here = lax.axis_index("pb")
    place = here if forward else count - 1 - here
    step = 1 if forward else -1
    has_prev = place > 0
    has_next = place < count - 1
    barrier = pltpu.get_barrier_semaphore()

    @pl.when(has_prev)
    def _():
        pl.semaphore_signal(barrier, inc=1, device_id={"pb": here - step}, device_id_type=MESH)

    @pl.when(has_next)
    def _():
        pl.semaphore_signal(barrier, inc=1, device_id={"pb": here + step}, device_id_type=MESH)

    greeted = has_prev.astype(jnp.int32) + has_next.astype(jnp.int32)
    for target in targets:
        pl.semaphore_signal(barrier, inc=1, device_id=target, device_id_type=MESH)
    pl.semaphore_wait(barrier, greeted + len(targets))

    height = state.shape[1] // cuts
    pieces = [(s, c) for s in range(state.shape[0]) for c in range(cuts)]

    def hop(i):
        s, c = pieces[i]
        rows = pl.ds(c * height, height)
        return pltpu.make_async_remote_copy(
            src_ref=message.at[s, rows],
            dst_ref=landed.at[s, rows],
            send_sem=send_sem.at[i],
            recv_sem=recv_sem.at[i],
            device_id={"pb": here + step},
            device_id_type=MESH,
        )

    def emit(i):
        s, c = pieces[i]
        rows = pl.ds(c * height, height)

        @pl.when(jnp.logical_not(has_prev))
        def _():
            message[s, rows] = state[s, rows].astype(BF16)
            hop(i).start()
            total[s, rows] = jnp.zeros((height, state.shape[2]), BF16)

        @pl.when(has_prev)
        def _():
            hop(i).wait_recv()
            total[s, rows] = (coef[0, s] * landed[s, rows].astype(F32)).astype(BF16)

            @pl.when(has_next)
            def _():
                message[s, rows] = (
                    state[s, rows] + coef[1, s] * total[s, rows].astype(F32)
                ).astype(BF16)
                hop(i).start()

    emit(0)
    if gathers:
        size = shard.shape[-1] // max(len(order), 1)
        for move in (0, 1):
            for j, i in enumerate(order or (0,)):
                copy = pltpu.make_async_copy(
                    moved.at[:, :, pl.ds(i * size, size)],
                    shard.at[:, :, pl.ds(j * size, size)],
                    shard_sem.at[j],
                )
                if move:
                    copy.wait()
                else:
                    copy.start()
        stages[0]()
    count = len(pieces)
    if gathers:
        jobs = {count // 2: stages[1:2], 3 * count // 4: stages[2:3]}
        rest = stages[3:]
    else:
        jobs = {i + 1: [stage] for i, stage in enumerate(stages[:8])}
        seqs = range(state.shape[0])
        inner = [functools.partial(within, s) for s in seqs]
        outer = [functools.partial(across, s) for s in seqs]
        late = [*inner[:3], stages[8], *inner[3:]]
        for i, job in enumerate(late):
            jobs.setdefault(min(7 + 2 * i, count - 1), []).append(job)
        rest = [*outer[:-1], *stages[9:], *outer[-1:]]
    for i in range(1, count):
        emit(i)
        for job in jobs.get(i, ()):
            job()
    for job in rest:
        job()

    @pl.when(has_next)
    def _():
        for i in range(len(pieces)):
            hop(i).wait_send()


def line_scan(state, coef, count, forward, order, collective_id, *before, gathered=None, summed=(), local=()):
    cuts = 4
    pieces = state.shape[0] * cuts
    scratch = [
        pltpu.VMEM(state.shape, BF16),
        pltpu.VMEM(state.shape, BF16),
        pltpu.SemaphoreType.DMA((pieces,)),
        pltpu.SemaphoreType.DMA((pieces,)),
    ]
    gathers = gathered is not None
    shapes = [jax.ShapeDtypeStruct(state.shape, BF16)]
    if gathers:
        operands, specs = (gathered,), [ANY]
        shapes.append(gathered_shape(gathered))
        outs = [VMEM, ANY]
        scratch += [
            pltpu.VMEM(gathered.shape, gathered.dtype),
            pltpu.SemaphoreType.DMA((max(len(order), 1),)),
            *GATHER_SCRATCH,
        ]
    else:
        operands = (*summed, *local)
        specs = [VMEM] * len(operands)
        shapes.append(jax.ShapeDtypeStruct(summed[2].shape, BF16))
        shapes += [jax.ShapeDtypeStruct(local[i].shape, BF16) for i in range(3)]
        outs = [VMEM] * 5
        scratch = [pltpu.VMEM(local[i].shape, F32) for i in (1, 2)] + scratch
        scratch += scatter_scratch(summed[2].shape)
    return pl.pallas_call(
        functools.partial(scan_kernel, count, forward, cuts, gathers, order),
        out_shape=shapes,
        in_specs=[VMEM, pl.BlockSpec(memory_space=pltpu.SMEM)] + specs + [ANY] * len(before),
        out_specs=outs,
        scratch_shapes=scratch,
        compiler_params=pltpu.CompilerParams(
            collective_id=collective_id,
            has_side_effects=True,
            vmem_limit_bytes=(16 if gathers else 58) * 1024 * 1024,
        ),
        name="line_scan",
    )(state, coef, *operands, *before)


def final_kernel(line, order, heads_pb, moves, grad, grad_out, *refs):
    weights, gain = refs[:3], refs[3]
    outs, out_out, sums, landed, out_landed = refs[-11:-8], refs[-8], refs[-7], refs[-6], refs[-5]
    targets, stages = owners_stages((grad,), (blocks_of(landed),), *refs[-4:-1])
    greet_partner, trade = trade_stages(line, grad_out, out_landed, refs[-1])
    row, col, other_row, across, sibling = plane_ids()
    across_s = lax.rem(sibling + 2, 4)
    barrier = pltpu.get_barrier_semaphore()
    for target in targets:
        pl.semaphore_signal(barrier, inc=1, device_id=target, device_id_type=MESH)
    pl.semaphore_wait(barrier, greet_partner(barrier) + len(targets))
    stages[0]()
    trade[0]()
    kept, arrive, leave = stages[2]

    def place(r, c):
        head = (c // heads_pb) * (2 * heads_pb) + r * heads_pb + lax.rem(c, heads_pb)
        total = 0.0
        for weight, target, blocks in zip(weights, outs, moves):
            _, _, start, size = blocks[0]
            columns = pl.ds(pl.multiple_of(head * size, size), size)
            value = landed[r * 4 + c, :, start : start + size].astype(F32)
            low = weight[:, columns].astype(BF16).astype(F32)
            target[:, columns] = gain[...] * value
            total = total + jnp.sum(low * value, axis=-1, keepdims=True)
        return total

    kept()
    total = place(row, col)
    for r, c, far in (
        (row, sibling, False),
        (row, across, False),
        (other_row, col, True),
        (row, across_s, False),
        (other_row, sibling, True),
        (other_row, across, True),
        (other_row, across_s, True),
    ):
        arrive(r, c, far)
        total = total + place(r, c)
    sums[...] = total
    trade[1]()
    size = out_out.shape[1] // max(len(order), 1)
    for j, i in enumerate(order or (0,)):
        block = out_landed[:, j * size : (j + 1) * size]
        out_out[:, i * size : (i + 1) * size] = block.astype(F32)
    leave()


def plane_final(
    grad, grad_out, weights, gain, line, order, heads_pb, moves, collective_id, *before
):
    return pl.pallas_call(
        functools.partial(final_kernel, line, order, heads_pb, moves),
        out_shape=[jax.ShapeDtypeStruct(w.shape, F32) for w in weights]
        + [
            jax.ShapeDtypeStruct(grad_out.shape, F32),
            jax.ShapeDtypeStruct(gain.shape, F32),
        ],
        in_specs=[ANY] * 2 + [VMEM] * 4 + [ANY] * len(before),
        out_specs=[VMEM] * 5,
        scratch_shapes=[pltpu.VMEM(grad.shape, BF16), pltpu.VMEM(grad_out.shape, BF16)]
        + owners_scratch(1)
        + list(TRADE_SCRATCH),
        compiler_params=pltpu.CompilerParams(
            collective_id=collective_id,
            has_side_effects=True,
            vmem_limit_bytes=20 * 1024 * 1024,
        ),
        name="plane_final",
    )(grad, grad_out, *weights, gain, *before)


def normalize(values):
    mean = jnp.mean(values, axis=-1, keepdims=True)
    centered = values - mean
    inv = lax.rsqrt(jnp.mean(centered * centered, axis=-1, keepdims=True) + EPSILON)
    return centered * inv, inv


def normalize_back(normed, inv, grad):
    mean = jnp.mean(grad, axis=-1, keepdims=True)
    along = jnp.mean(grad * normed, axis=-1, keepdims=True)
    return inv * (grad - mean - normed * along)


def turn_tables(positions, half, direction):
    pair = jnp.arange(half, dtype=F32)
    frequency = jnp.exp(-jnp.log(10000.0) * pair / half)
    zeta = (pair / half + 0.4) / 1.4
    angles = positions[:, None] * frequency[None, :]
    factor = jnp.exp(direction * positions[:, None] / XPOS_BASE * jnp.log(zeta)[None, :])
    return jnp.cos(angles) * factor, jnp.sin(angles) * factor


def turn(values, tables):
    cosine, sine = tables
    half = values.shape[-1] // 2
    first, second = values[..., :half], values[..., half:]
    return jnp.concatenate(
        [first * cosine - second * sine, second * cosine + first * sine], axis=-1
    )


def turn_back(values, tables):
    cosine, sine = tables
    return turn(values, (cosine, -sine))


def mm(left, right):
    return jnp.einsum("sti,io->sto", left, right, preferred_element_type=F32)


def mm_back(left, right):
    return jnp.einsum("sto,io->sti", left, right, preferred_element_type=F32)


def mm_grad(left, right):
    return jnp.einsum("sti,sto->io", left, right, preferred_element_type=F32)


def after(value, *others):
    for other in others:
        value = value + (0.0 * other[(0,) * other.ndim].astype(F32)).astype(value.dtype)
    return value


def on_device(
    inputs,
    out_cotangent,
    doc_lengths,
    ln1_gain,
    w_query,
    w_key,
    w_value,
    w_gate,
    w_out,
    ln2_gain,
    w_up,
    up_bias,
    w_down,
):
    n_dph, n_dpl, n_pb, n_ka = (lax.axis_size(a) for a in ("dph", "dpl", "pb", "ka"))
    at_dpl, at_pb, at_ka = (lax.axis_index(a) for a in ("dpl", "pb", "ka"))
    batch, length, width = inputs.shape
    span = n_ka * length
    rows = w_query.shape[0]
    wide_rows = w_down.shape[0]
    key_width = w_query.shape[1] // H
    value_width = w_value.shape[1] // H
    units = n_dph * n_pb * wide_rows
    group = n_dpl * n_ka
    heads_pb = H // (n_dpl * n_dph)

    chunk = n_ka * rows

    def pick(values, order):
        return jnp.concatenate(
            [values[..., i * chunk : (i + 1) * chunk] for i in order], axis=-1
        )

    inner = [
        (d * n_dpl + r) * n_pb + p
        for d in range(n_dph)
        for p in range(n_pb)
        for r in range(n_dpl)
    ]

    def to_inner(values):
        return pick(values, inner)

    def to_outer(values):
        return pick(values, [inner.index(i) for i in range(len(inner))])

    def by_unit(weight):
        cut = weight.reshape(rows, n_dph, n_dpl, n_pb, n_ka, wide_rows)
        return jnp.transpose(cut, (2, 4, 0, 1, 3, 5)).reshape(group, rows, units)

    def from_unit(values):
        cut = values.reshape(n_dpl, n_ka, rows, n_dph, n_pb, wide_rows)
        return jnp.transpose(cut, (2, 3, 0, 4, 1, 5)).reshape(rows, -1)

    def gather_line(values):
        return lax.all_gather(values, LINE, axis=0, tiled=True)

    def scatter_line(values):
        return lax.psum_scatter(values, LINE, scatter_dimension=0, tiled=True)

    line = "dph" if n_dph > 1 else "pb"

    gain_one = ln1_gain.astype(BF16).astype(F32)[:, None]
    gain_two = ln2_gain.astype(BF16).astype(F32)[:, None]
    firsts = (w_query, w_key, w_value, w_gate)

    def head_of(j):
        r, c = j // n_ka, j % n_ka
        return (c // heads_pb) * (n_dpl * heads_pb) + r * heads_pb + c % heads_pb

    head_moves = [
        [(j, head_of(j) * size, place, size) for j in range(group)]
        for size, place in (
            (key_width, 0),
            (key_width, key_width),
            (value_width, 2 * key_width),
            (value_width, 0),
        )
    ]
    docs = jnp.pad(doc_lengths, ((0, 8 - batch), (0, 128 - doc_lengths.shape[1])))
    order = tuple(inner) if chunk % 128 == 0 else ()
    rows_in, rows_cot = inputs, out_cotangent
    if not order:
        rows_in, rows_cot = to_inner(inputs), to_inner(out_cotangent)
    out_in, down_in, up_in, unit_moves = w_out, w_down, w_up, []
    if order:
        moves = [(i * chunk, j * chunk, chunk) for j, i in enumerate(order)]
        for j in range(group):
            for q in range(n_dph * n_pb):
                block = (q // n_pb * n_dpl + j // n_ka) * n_pb + q % n_pb
                column = (block * n_ka + j % n_ka) * wide_rows
                unit_moves.append((j, column, q * wide_rows, wide_rows))
    else:
        moves = [(i * units, i * units, units) for i in range(width // units)]
        out_in, down_in = to_inner(w_out), to_inner(w_down)
        up_in = by_unit((w_up.astype(BF16).astype(F32) * gain_two).astype(BF16))
    normed_one_all, up_swapped, weight_qkv, gate_out, down_pack, docs_all = open_plane(
        firsts,
        gain_one,
        out_in,
        docs,
        rows_in,
        up_in,
        down_in,
        up_bias[None, :],
        gain_two,
        line,
        order,
        moves,
        unit_moves,
        head_moves,
        units,
        n_pb,
        0,
    )
    head = (
        (at_ka // heads_pb) * (n_dpl * heads_pb) + at_dpl * heads_pb + at_ka % heads_pb
    ).astype(F32)
    log_gamma = jnp.log(1.0 - jnp.exp2(-5.0 - head))
    offsets = jnp.arange(span, dtype=jnp.int32)
    places = (at_pb * span + offsets).astype(F32)
    tables_q = turn_tables(places, key_width // 2, 1.0)
    tables_k = turn_tables(places, key_width // 2, -1.0)
    distance = offsets[:, None] - offsets[None, :]
    decay = jnp.where(
        distance >= 0, jnp.exp(jnp.maximum(distance, 0).astype(F32) * log_gamma), 0.0
    )
    decay_in = jnp.exp(offsets.astype(F32) * log_gamma)[:, None]
    decay_out = jnp.exp((span - offsets).astype(F32) * log_gamma)[:, None]
    decay_span = jnp.exp(span * log_gamma)
    lengths = docs_all[:, :batch, : doc_lengths.shape[1]].reshape(n_dpl * batch, -1)
    ends = jnp.cumsum(lengths, axis=-1)
    edge = at_pb * span

    def goes_on(start):
        return jnp.all(ends != start, axis=-1).astype(F32)

    coef_forward = jnp.stack([goes_on(edge), jnp.full((n_dpl * batch,), decay_span)])
    coef_backward = jnp.stack([goes_on(edge + span), jnp.full((n_dpl * batch,), decay_span)])

    if n_dph > 1:
        weight_qkv = lax.all_gather(weight_qkv, "dph", axis=0, tiled=True)
    blocks = width // units
    gate_out = gather_line(gate_out)
    first = mm(normed_one_all, weight_qkv)
    query_pre = first[..., :key_width]
    key_pre = first[..., key_width : 2 * key_width]
    value = first[..., 2 * key_width :].astype(BF16)
    scale = key_width ** (-0.5)
    query = (turn(query_pre, tables_q) * scale).astype(BF16)
    key = turn(key_pre, tables_k).astype(BF16)
    key_out = (key.astype(F32) * decay_out).astype(BF16)
    state = jnp.einsum("smd,sme->sde", key_out, value, preferred_element_type=F32)
    carried, cot_all = line_scan(
        state, coef_forward, n_pb, True, order, 2, value, query, key, gathered=rows_cot
    )
    raw = jnp.einsum("snd,smd->snm", query, key, preferred_element_type=F32)
    scores = (raw * decay).astype(BF16)
    retained = jnp.einsum("snm,sme->sne", scores, value, preferred_element_type=F32)
    retained = retained + decay_in * jnp.einsum(
        "snd,sde->sne", query, carried, preferred_element_type=F32
    )
    normed_ret, inv_ret = normalize(retained)
    stride = gate_out.shape[0] // (n_dph * n_pb)
    spread = n_pb // heads_pb
    out_places = []
    for q in range(n_dph * n_pb):
        row = (q % spread * (n_dph * n_pb // spread) + q // spread) * wide_rows
        for i in range(blocks):
            source = q * stride + group * rows + i * wide_rows
            out_places.append((source, row, i * units, wide_rows))
    cut_out = gate_out.reshape(n_dph * n_pb, stride, units)
    bias_up = cut_out[:, stride - 16, :wide_rows].reshape(units).astype(F32)
    weight_up = gather_line(after(up_swapped.reshape(group * rows, -1), gate_out, inv_ret))
    weight_gate = after(cut_out[:, : group * rows].reshape(width, units), inv_ret)
    gate = mm(normed_one_all, weight_gate)
    gated = (gate * jax.nn.sigmoid(gate) * normed_ret).astype(BF16)
    weight_down = gather_line(after(down_pack, gated))
    gate_low = gate.astype(BF16)
    middle, normed_two_all, weight_out = plane_mix(
        gated, rows_in, gate_out, out_places, order, 3, scores, decay_in, decay_out
    )
    up_pre = mm(normed_two_all, weight_up) + bias_up
    bell = 0.5 * (1.0 + lax.erf(up_pre * np.float32(math.sqrt(0.5))))
    active = (up_pre * bell).astype(BF16)

    slope = bell + up_pre * (
        jnp.exp(-0.5 * up_pre * up_pre) * np.float32(1.0 / math.sqrt(2.0 * math.pi))
    )
    grad_up_pre = (mm_back(cot_all, weight_down) * slope).astype(BF16)
    ones = jnp.ones((n_dpl * batch, span, 128), BF16)
    grad_down = jnp.concatenate(
        [mm_grad(active, cot_all).astype(BF16), mm_grad(grad_up_pre, ones).astype(BF16)], axis=-1
    )
    grad_up = mm_grad(normed_two_all, grad_up_pre).astype(BF16)
    grad_middle, grad_mid_all = plane_turn(
        grad_up_pre, weight_up, middle, rows_cot, order, 5, grad_down, grad_up
    )
    grad_down = scatter_line(grad_down)
    grad_up = scatter_line(grad_up)
    grad_gated = after(mm_back(grad_mid_all, weight_out), grad_up)
    gate_again = gate_low.astype(F32)
    opened = jax.nn.sigmoid(gate_again)
    silu = gate_again * opened
    grad_gate = (grad_gated * normed_ret * (opened + silu * (1.0 - opened))).astype(BF16)
    grad_ret = normalize_back(normed_ret, inv_ret, grad_gated * silu).astype(BF16)
    query_in = (query.astype(F32) * decay_in).astype(BF16)
    grad_state = jnp.einsum("snd,sne->sde", query_in, grad_ret, preferred_element_type=F32)
    grad_out = after(mm_grad(gated, grad_mid_all), grad_down).astype(BF16)
    grad_out = (
        grad_out.reshape(n_pb // heads_pb, -1, wide_rows, width)
        .swapaxes(0, 1)
        .reshape(value_width, width)
    )
    grad_gate_w = mm_grad(normed_one_all, grad_gate).astype(BF16)
    _, output, *grad_parts = line_scan(
        grad_state,
        coef_backward,
        n_pb,
        False,
        order,
        7,
        grad_gate_w,
        grad_out,
        summed=(active, weight_down, middle),
        local=(
            query,
            key,
            value,
            grad_ret,
            scores,
            carried,
            decay,
            decay_in,
            decay_out,
            *tables_q,
            *tables_k,
        ),
    )
    grad_gate_w = scatter_line(grad_gate_w)
    grad_out = scatter_line(grad_out)
    grad_qkv = jnp.concatenate(grad_parts, axis=-1)
    grad_qkv_w = mm_grad(normed_one_all, after(grad_qkv, grad_gate_w)).astype(BF16)
    grad_qkv_sum = scatter_line(grad_qkv_w)
    cut = (group, rows, -1)
    grad_inputs, shard_gate, shard_up, sums_gate, sums_up, shard_down = plane_last(
        (*grad_parts, weight_qkv, grad_gate, weight_gate),
        rows_in,
        grad_middle,
        (grad_gate_w.reshape(cut), grad_up.reshape(cut)),
        (w_gate, w_up),
        (gain_one, gain_two),
        grad_down,
        (head_moves[3], unit_moves),
        order,
        8,
        grad_qkv_w,
    )
    if not order:
        output, grad_inputs, shard_down = (to_outer(a) for a in (output, grad_inputs, shard_down))
        shard_up = from_unit(shard_up).astype(F32)
        sums_up = jnp.sum(w_up.astype(BF16).astype(F32) * shard_up, axis=-1, keepdims=True)
        shard_up = gain_two * shard_up

    output, grad_inputs, shard_gate, shard_up, shard_down = (
        after(a, sums_gate) for a in (output, grad_inputs, shard_gate, shard_up, shard_down)
    )

    shard_query, shard_key, shard_value, shard_out, sums_qkv = plane_final(
        grad_qkv_sum.reshape(cut),
        grad_out,
        firsts[:3],
        gain_one,
        line,
        order,
        heads_pb,
        head_moves[:3],
        9,
        sums_gate,
    )
    if not order:
        shard_out = to_outer(shard_out)
    shard_bias = grad_down[:, width].astype(F32)
    return (
        output,
        grad_inputs,
        (sums_qkv + sums_gate)[:, 0],
        shard_query,
        shard_key,
        shard_value,
        shard_gate,
        shard_out,
        sums_up[:, 0],
        shard_up,
        shard_bias,
        shard_down,
    )


def solution(mesh):
    dp, pb, ka = (mesh.shape[a] for a in ("dp", "pb", "ka"))
    fine = Mesh(mesh.devices.reshape(dp // 2, 2, pb, ka), ("dph", "dpl", "pb", "ka"))
    dp_axes = ("dph", "dpl")
    every = ("dph", "dpl", "pb", "ka")
    tokens = P(dp_axes, ("pb", "ka"), None)
    matrix = P(every, None)
    vector = P(every)
    return jax.shard_map(
        on_device,
        mesh=fine,
        in_specs=(
            tokens,
            tokens,
            P(dp_axes, None),
            vector,
            matrix,
            matrix,
            matrix,
            matrix,
            matrix,
            vector,
            matrix,
            vector,
            matrix,
        ),
        out_specs=(
            tokens,
            tokens,
            vector,
            matrix,
            matrix,
            matrix,
            matrix,
            matrix,
            vector,
            matrix,
            vector,
            matrix,
        ),
        check_vma=False,
    )
```
